32 devices in a mesh: func: 4 (over z), box: 8 (over y, x, core).
Axes of the slice: x: 2, y: 2, z: 4, core: 2. Of those that a mesh axis runs over, the one named last changes fastest.
Arguments:
- coeffs: bfloat16 [768, 32, 1024], P(('func', 'box')), may hold values from -8 to 8
- centers: int32 [768], replicated, may hold values from 0 to 383, as said below
- kinetic: bfloat16 [1024, 1024], replicated, may hold values from -0.1875 to 0.1875
- potential: float32 [384, 1024], P(('func', 'box')), may hold values from -1 to 1
Outputs:
- filtered: bfloat16 [768, 32, 1024], P(('func', 'box'))
- gram_band: float32 [768, 256], P(('func', 'box'))
The draws below stay inside these ranges and needn't reach their ends.
Inputs may be any that keep to these rules, and one draw needn't show every extreme that they name: `centers`: centers never fall. The boxes form aligned groups of 32, and the groups aligned blocks of four; every box of a group is the center of the same number of functions, 1, 2 or 4, and each block of four groups holds the numbers 1, 1, 2 and 4 in an order whose running total of (number - 2) stays between -1 and 1. So between 32 and 128 functions touch each box, and some box is touched by exactly 128.
All inputs are finite; a program needn't handle non-finite values.
Results may differ from the reference program's by a relative error of at most 0.0057.
Values may be sent and summed in bfloat16 or wider, within the bound.
No kernel may reach another device: no remote copies, remote signals or barrier semaphores. Data moves between devices by JAX's collectives and lax.ppermute only.
A program may use at most 64 MiB of HBM per device.

```python
import jax
import jax.numpy as jnp
from jax import lax

SUP = 32
P_SIZE = 1024
NF = 768
NB = 384


def draw_coeffs(key, part):
    key_values, key_scales = jax.random.split(key)
    base_values = jnp.clip(jax.random.normal(key_values, (NF, SUP, P_SIZE), jnp.float32), -3.9, 3.9)
    scales = jnp.exp(jax.random.uniform(key_scales, (NF, SUP, 1), jnp.float32, -0.7, 0.7))
    return (base_values * scales).astype(jnp.bfloat16)


def draw_centers(key, part):
    groups = NB // SUP
    blocks = groups // 4
    orders = jnp.array([[1, 2, 4, 1], [1, 4, 1, 2], [1, 4, 2, 1], [2, 1, 4, 1]], dtype=jnp.int32)
    chosen = jax.random.randint(key, (blocks,), 0, 4).astype(jnp.int32)
    density = orders[chosen].reshape(groups)
    counts = jnp.repeat(density, SUP, total_repeat_length=NB)
    box_ends = jnp.cumsum(counts).astype(jnp.int32)
    return jnp.searchsorted(box_ends, jnp.arange(NF, dtype=jnp.int32), side='right').astype(jnp.int32)


def steps_of(own_key, dims, cuts, low, top_value):
    level = 1.0
    for position, blocks in cuts:
        heights = jax.random.uniform(jax.random.fold_in(jax.random.fold_in(own_key, 6), position), (blocks,), jnp.float32, low / len(cuts), top_value / len(cuts))
        level = level * jnp.repeat(jnp.exp(heights), dims[position] // blocks).reshape((-1,) + (1,) * (len(dims) - 1 - position))
    return level


def centred(key, shape, scale, bound, kind=jnp.bfloat16):
    entries = jax.random.normal(key, shape, jnp.float32) * scale
    return jnp.minimum(jnp.maximum(entries, -bound), bound).astype(kind)


def setup_inputs(seed: int = 0) -> dict:
    key_list = jax.random.split(jax.random.key(seed), 5)
    return {
        "coeffs": draw_coeffs(jax.random.fold_in(key_list[4], 71), 0),
        "centers": draw_centers(jax.random.fold_in(key_list[4], 71), 0),
        "kinetic": centred(key_list[2], (P_SIZE, P_SIZE), P_SIZE ** -0.5, 0.1875),
        "potential": jnp.clip(jax.random.uniform(key_list[3], (NB, P_SIZE), jnp.float32, -1.0, 1.0) * steps_of(key_list[3], (NB, P_SIZE), ((0, 32),), -0.4, 0.0), -1.0, 1.0),
    }


group_boxes = 16


def to_band(matrix):
    leading = matrix.shape[:-2]
    matrix_order = matrix.shape[-1]
    spaces = [(0, 0)] * len(leading)
    padded = jnp.pad(matrix, spaces + [(0, 0), (matrix_order - 1, 1)])
    flattened = padded.reshape(leading + (2 * matrix_order * matrix_order,))
    flattened = jnp.pad(flattened, spaces + [(0, matrix_order)])
    return flattened.reshape(leading + (matrix_order, 2 * matrix_order + 1))[..., : 2 * matrix_order]


def from_band(band_rows):
    leading = band_rows.shape[:-2]
    matrix_order = band_rows.shape[-2]
    flattened = band_rows.reshape(leading + (2 * matrix_order * matrix_order,))
    flattened = flattened[..., : matrix_order * (2 * matrix_order - 1)]
    return flattened.reshape(leading + (matrix_order, 2 * matrix_order - 1))[..., matrix_order - 1:]


def reference(coeffs, centers, kinetic, potential):
    capacity = 4 * SUP
    volume = 1.0 / (SUP * P_SIZE)
    every_box = jnp.arange(NB, dtype=jnp.int32)
    window_start = (every_box - SUP + 1) % NB
    first_row = jnp.searchsorted(centers, window_start, side="left").astype(jnp.int32)
    end_row = jnp.searchsorted(centers, every_box + 1, side="left").astype(jnp.int32)
    filled = (end_row - first_row) % NF
    flat_coeffs = coeffs.reshape(NF * SUP, P_SIZE)
    potential_all = potential.reshape(NB, P_SIZE)
    slot_ids = jnp.arange(capacity, dtype=jnp.int32)

    def gather_box(first_box):
        box_ids = first_box + jnp.arange(group_boxes, dtype=jnp.int32)
        row_ids = (first_row[box_ids][:, None] + slot_ids[None, :]) % NF
        live_slot = slot_ids[None, :] < filled[box_ids][:, None]
        support_step = jnp.minimum((box_ids[:, None] - centers[row_ids]) % NB, SUP - 1)
        target = (row_ids * SUP + support_step).astype(jnp.int32)
        pieces = jnp.where(live_slot[..., None], flat_coeffs[target], jnp.zeros((), coeffs.dtype))
        return box_ids, row_ids, live_slot, target, pieces

    def first_pass(running, first_box):
        box_ids, row_ids, live_slot, target, pieces = gather_box(first_box)
        widened = pieces.astype(jnp.float32)
        gram_box = volume * jnp.einsum("kmp,knp->kmn", widened, widened)
        band_rows = to_band(gram_box)
        running = running.at[row_ids.reshape(-1)].add(band_rows.reshape(-1, 2 * capacity))
        return running, None

    starts = jnp.arange(NB // group_boxes, dtype=jnp.int32) * group_boxes
    gram_band, unused = lax.scan(first_pass, jnp.zeros((NF, 2 * capacity), jnp.float32), starts)
    diag_mask = (jnp.arange(2 * capacity) == capacity - 1).astype(jnp.float32)
    correction = (1.5 * diag_mask - 0.5 * gram_band).astype(jnp.bfloat16)

    def second_pass(running, first_box):
        box_ids, row_ids, live_slot, target, pieces = gather_box(first_box)
        mixing = from_band(correction[row_ids])
        corrected = jnp.einsum("kml,klp->kmp", mixing.astype(jnp.float32), pieces.astype(jnp.float32)).astype(jnp.bfloat16)
        widened = corrected.astype(jnp.float32)
        applied = jnp.einsum("kmp,pq->kmq", widened, kinetic.astype(jnp.float32))
        applied = (applied + potential_all[box_ids][:, None, :] * widened).astype(jnp.bfloat16)
        placing = jnp.where(live_slot, target, NF * SUP).astype(jnp.int32)
        running = running.at[placing.reshape(-1)].set(applied.reshape(-1, P_SIZE), mode="drop")
        return running, None

    filtered, unused = lax.scan(second_pass, jnp.zeros((NF * SUP, P_SIZE), jnp.bfloat16), starts)
    return filtered.reshape(NF, SUP, P_SIZE), gram_band
```

```python
import jax
import jax.numpy as jnp
from jax import lax
from jax.sharding import PartitionSpec as P

AXES = ("func", "box")


def passed_along(value, steps):
    count = lax.axis_size(AXES)
    pairs = [(source, (source + steps) % count) for source in range(count)]
    return lax.ppermute(value, AXES, pairs)


def on_device(coeffs, centers, kinetic, potential):
    fun_dev, support, points = coeffs.shape
    devices = lax.axis_size(AXES)
    me = lax.axis_index(AXES)
    box_dev = fun_dev // 2
    box_all = box_dev * devices
    volume = 1.0 / (support * points)
    shift = 1
    reach = 3
    offsets = list(range(-reach, reach + 1))
    order = sorted(offsets, key=lambda k: (abs(k), k))
    span = len(offsets)
    window = span * fun_dev
    reading = 4 * support

    my_potential = passed_along(potential, -shift)
    my_centers = lax.dynamic_slice_in_dim(centers, me * fun_dev, fun_dev)
    local_box = jnp.arange(box_dev, dtype=jnp.int32)
    steps = jnp.arange(support, dtype=jnp.int32)
    target = (me + shift + jnp.array(offsets, jnp.int32)) % devices
    target_box = target[:, None] * box_dev + local_box[None, :]
    step_out = (target_box[:, None, :] - my_centers[None, :, None]) % box_all
    select = (step_out[..., None] == steps).astype(jnp.bfloat16)
    outgoing = jnp.einsum(
        "jfks,fsp->jfkp", select, coeffs, preferred_element_type=jnp.float32
    ).astype(jnp.bfloat16)
    arrived = [None] * span
    for k in order:
        piece = outgoing[k + reach]
        arrived[reach - k] = piece if k == 0 else passed_along(piece, k)
    pieces = jnp.concatenate([a.reshape(fun_dev, box_dev * points) for a in arrived], axis=0)
    partial = volume * lax.dot_general(
        pieces, pieces, (((1,), (1,)), ((), ())), preferred_element_type=jnp.float32
    )
    total = partial
    wide = (2 * span - 1) * fun_dev
    rows = jnp.pad(partial[reach * fun_dev : (reach + 1) * fun_dev], ((0, 0), (reach * fun_dev, reach * fun_dev)))
    for k in order:
        if k == 0:
            continue
        other = passed_along(partial, k)
        at = -k * fun_dev
        total = total + lax.pad(other, 0.0, ((at, -at, 0), (at, -at, 0)))
        row_at = (reach + k) * fun_dev
        rows = rows + jnp.pad(other[row_at : row_at + fun_dev], ((0, 0), ((reach - k) * fun_dev, (reach + k) * fun_dev)))
    first = (2 * reach) * fun_dev - (reading - 1)
    gram_band = jnp.stack([rows[r, first + r : first + r + 2 * reading] for r in range(fun_dev)])
    last = (jnp.arange(2 * reading) < 2 * reading - 1)
    gram_band = jnp.where(last, gram_band, 0.0)
    diag = jnp.eye(window, dtype=jnp.float32)
    correction = (1.5 * diag - 0.5 * total).astype(jnp.bfloat16)
    corrected = lax.dot_general(
        correction, pieces, (((1,), (0,)), ((), ())), preferred_element_type=jnp.float32
    ).astype(jnp.bfloat16).reshape(window, box_dev, points)
    applied = jnp.einsum("fbp,pq->fbq", corrected, kinetic, preferred_element_type=jnp.float32)
    applied = (applied + my_potential[None] * corrected.astype(jnp.float32)).astype(jnp.bfloat16)
    coming = [None] * span
    for k in order:
        piece = applied[(reach - k) * fun_dev : (reach - k + 1) * fun_dev]
        coming[k + reach] = piece if k == 0 else passed_along(piece, -k)
    returned = jnp.stack(coming)
    filtered = jnp.einsum(
        "jfks,jfkp->fsp", select, returned, preferred_element_type=jnp.float32
    ).astype(jnp.bfloat16)
    return (filtered, gram_band)


def solution(mesh):
    placed = (P(AXES, None, None), P(), P(), P(AXES, None))
    return jax.shard_map(
        on_device,
        mesh=mesh,
        in_specs=placed,
        out_specs=(P(AXES, None, None), P(AXES, None)),
        check_vma=False,
    )
```

```python
import functools
import itertools

import jax
import jax.numpy as jnp
import numpy as np
from jax import lax
from jax.experimental import pallas as pl
from jax.experimental.pallas import tpu as pltpu
from jax.sharding import PartitionSpec as P

AXES = ("func", "box")
REACH = 3
SLOT = 32
STEP = 8


def passed_along(value, steps):
    count = lax.axis_size(AXES)
    pairs = [(source, (source + steps) % count) for source in range(count)]
    return lax.ppermute(value, AXES, pairs)


def rounded_up(value, multiple):
    return -(-int(value) // multiple) * multiple


@functools.lru_cache(maxsize=None)
def bounds(fun_dev, support):
    box_dev = fun_dev // 2
    orders = [
        order
        for order in sorted(set(itertools.permutations((1, 1, 2, 4))))
        if np.abs(np.cumsum(np.array(order) - 2)).max() <= 1
    ]
    box_all, fun_all = 12 * support, 24 * support
    assert fun_all % fun_dev == 0
    devices = fun_all // fun_dev
    rows = np.zeros(2 * REACH + 1, np.int64)
    low, high, boxes, end = 10**6, -(10**6), 0, 0
    for picks in itertools.product(orders, repeat=3):
        density = np.repeat(np.concatenate(picks), support)
        centers = np.repeat(np.arange(box_all), density)
        load = sum(np.roll(density, t) for t in range(support))
        below = np.concatenate([[0], np.cumsum(np.tile(load, 3))])
        over = np.clip(np.arange(box_all)[:, None] + support - box_all, 0, None)
        carried = int((over[:, 0] * density).sum())
        below = below - carried
        twice = below[:-1] + below[1:]
        cut = np.array([
            np.searchsorted(twice, 2 * support * fun_dev * (devices + d), side="right")
            for d in range(-REACH - 1, devices + REACH + 2)
        ]) - box_all
        first = REACH + 1
        width = np.diff(cut)
        place = cut - box_dev * (np.arange(len(cut)) - first)
        low, high = min(low, place.min()), max(high, place.max())
        boxes = max(boxes, width.max())
        end = max(end, (place[:-1] + width).max())
        box = centers[:, None] + np.arange(support)
        owner = np.searchsorted(cut, box, side="right") - 1 - first
        device = np.arange(fun_all)[:, None] // fun_dev
        offset = owner - device
        assert np.abs(offset).max() <= REACH
        count = np.bincount((device * (2 * REACH + 1) + offset + REACH).ravel(), minlength=devices * (2 * REACH + 1))
        rows = np.maximum(rows, count.reshape(devices, -1).max(0))
    return (
        tuple(rounded_up(r, 16) for r in rows),
        int(low),
        int(high),
        rounded_up(boxes, STEP),
        -(-int(end) // box_dev),
    )


def before(counts):
    return jnp.cumsum(counts, axis=-1) - counts


def unpack_kernel(slots, width_ref, column_ref, keep_ref, *refs):
    sources = refs[:slots]
    window_ref, gram_ref, total = refs[slots:]
    step = pl.program_id(0)
    first = step * STEP

    @pl.when(step == 0)
    def _():
        total[...] = jnp.zeros_like(total)

    @pl.when(first < width_ref[0])
    def _():
        for e in range(slots):
            start = column_ref[e * SLOT : (e + 1) * SLOT, 0:1]
            low = column_ref[e * SLOT : (e + 1) * SLOT, 1:2]
            high = column_ref[e * SLOT : (e + 1) * SLOT, 2:3]
            rows = sources[e].shape[0]
            lane = lax.broadcasted_iota(jnp.int32, (SLOT, rows), 1)
            picks = []
            for b in range(STEP):
                box = first + b
                row = jnp.where((box >= low) & (box < high), start + box, -1)
                picks.append((lane == row).astype(jnp.float32).astype(jnp.bfloat16))
            pick = jnp.concatenate(picks, axis=0)
            found = jnp.dot(pick, sources[e][...], preferred_element_type=jnp.float32)
            window_ref[:, e * SLOT : (e + 1) * SLOT, :] = found.astype(jnp.bfloat16).reshape(
                STEP, SLOT, found.shape[-1]
            )
        for b in range(STEP):
            here = window_ref[b]
            total[...] += lax.dot_general(
                here, here, (((1,), (1,)), ((), ())), preferred_element_type=jnp.float32
            )

    @pl.when(step == pl.num_programs(0) - 1)
    def _():
        keep = keep_ref[...]
        half = jnp.dot(total[...], keep, precision=lax.Precision.HIGHEST, preferred_element_type=jnp.float32)
        gram_ref[...] = lax.dot_general(
            keep, half, (((0,), (0,)), ((), ())), precision=lax.Precision.HIGHEST,
            preferred_element_type=jnp.float32,
        )


def mix_kernel(slots, width_ref, mixing_ref, place_ref, window_ref, *refs):
    outs = refs[:slots]
    mixed = refs[slots]
    step = pl.program_id(0)

    @pl.when(step == 0)
    def _():
        for out in outs:
            out[...] = jnp.zeros_like(out)

    @pl.when(step * STEP < width_ref[0])
    def _():
        for b in range(STEP):
            mixed[b] = jnp.dot(
                mixing_ref[...], window_ref[b], preferred_element_type=jnp.float32
            ).astype(jnp.bfloat16)
        for e in range(slots):
            rows = outs[e].shape[0]
            wanted = lax.broadcasted_iota(jnp.int32, (rows, STEP * SLOT), 0)
            pick = (wanted == place_ref[0, e : e + 1, :]).astype(jnp.float32).astype(jnp.bfloat16)
            part = mixed[:, e * SLOT : (e + 1) * SLOT, :].reshape(STEP * SLOT, mixed.shape[-1])
            outs[e][...] += jnp.dot(pick, part, preferred_element_type=jnp.float32).astype(jnp.bfloat16)


def home_kernel(slots, bases, column_ref, *refs):
    sources = refs[:slots]
    out_ref = refs[slots]
    row = column_ref[:, 0:1]
    value = None
    for e in range(slots):
        rows = sources[e].shape[0]
        lane = lax.broadcasted_iota(jnp.int32, (column_ref.shape[0], rows), 1)
        pick = (lane == row - bases[e]).astype(jnp.float32).astype(jnp.bfloat16)
        term = jnp.dot(pick, sources[e][...], preferred_element_type=jnp.float32)
        value = term if value is None else value + term
    out_ref[...] = value.astype(jnp.bfloat16)


def whole(shape):
    return pl.BlockSpec(shape, lambda g: (0,) * len(shape))


def on_device(coeffs, centers, kinetic, potential):
    fun_dev, support, points = coeffs.shape
    devices = lax.axis_size(AXES)
    me = lax.axis_index(AXES)
    fun_all = fun_dev * devices
    box_dev = fun_dev // 2
    box_all = box_dev * devices
    volume = 1.0 / (support * points)
    reading = 4 * support
    slots = 2 * REACH + 1
    offsets = list(range(-REACH, REACH + 1))
    order = sorted(offsets, key=lambda k: (abs(abs(k) - 1.9), k))
    window = slots * fun_dev
    rows, low_cut, high_cut, boxes, blocks = bounds(fun_dev, support)
    rows_of = {k: rows[k + REACH] for k in offsets}
    flat = coeffs.reshape(fun_dev * support, points)

    halo = REACH + -(-(reading + 8) // fun_dev)
    ahead = halo + 2
    around = jnp.concatenate(
        [centers[fun_all - halo * fun_dev :], centers, centers[: ahead * fun_dev]]
    )
    near = lax.dynamic_slice_in_dim(around, me * fun_dev, (halo + ahead) * fun_dev)
    near = (near - me * box_dev + box_all // 2) % box_all - box_all // 2
    sides = jnp.arange(-REACH, REACH + 2, dtype=jnp.int32)
    tries = low_cut + jnp.arange(high_cut - low_cut + 1, dtype=jnp.int32)
    tried = sides[:, None] * box_dev + tries[None, :]
    gap = tried[..., None] - near
    twice = jnp.sum(jnp.clip(gap, 0, support) + jnp.clip(gap + 1, 0, support), axis=-1)
    goal = 2 * support * fun_dev * (halo + sides)
    cut = low_cut + sides * box_dev + jnp.sum((twice <= goal[:, None]).astype(jnp.int32), axis=-1)

    mine = near[halo * fun_dev : (halo + 1) * fun_dev]
    edge = jnp.clip(cut[:, None] - mine[None, :], 0, support)
    leave = edge[1:] - edge[:-1]
    leave_at = before(leave)
    steps = jnp.arange(support, dtype=jnp.int32)
    goes = (steps >= edge[:-1, :, None]) & (steps < edge[1:, :, None])
    row_out = jnp.where(goes, leave_at[..., None] + steps - edge[:-1, :, None], -1)
    row_out = row_out.reshape(slots, fun_dev * support)

    arrived = {}
    for k in order:
        if k == 0:
            continue
        pick = (jnp.arange(rows_of[k], dtype=jnp.int32)[:, None] == row_out[k + REACH]).astype(jnp.bfloat16)
        packed = jnp.dot(pick, flat, preferred_element_type=jnp.float32).astype(jnp.bfloat16)
        arrived[k] = passed_along(packed, k)

    bases, total_rows = {}, 0
    for k in offsets:
        bases[k] = total_rows
        total_rows += rows_of[k]
    base_of = jnp.array([bases[k] for k in offsets], jnp.int32)
    home_row = jnp.sum(
        jnp.where(row_out >= 0, row_out + base_of[:, None], 0), axis=0
    )
    home_column = jnp.broadcast_to(home_row[:, None], (fun_dev * support, 8))

    others = near[(halo - REACH) * fun_dev : (halo + REACH + 1) * fun_dev].reshape(slots, fun_dev)
    start_cut, end_cut = cut[REACH], cut[REACH + 1]
    width = end_cut - start_cut
    edge_low = jnp.clip(start_cut - others, 0, support)
    edge_high = jnp.clip(end_cut - others, 0, support)
    come_at = before(edge_high - edge_low)
    box_low = edge_low + others - start_cut
    box_high = edge_high + others - start_cut
    packed_start = come_at - box_low
    own = jnp.arange(slots)[:, None] == REACH
    local_start = jnp.arange(fun_dev, dtype=jnp.int32)[None, :] * support + start_cut - others
    unpack_start = jnp.where(own, local_start, packed_start)
    columns = jnp.stack([unpack_start, box_low, box_high], axis=-1)
    columns = jnp.pad(columns, ((0, 0), (0, SLOT - fun_dev), (0, 5))).reshape(slots * SLOT, 8)
    box_range = jnp.arange(boxes, dtype=jnp.int32)[None, :, None]
    lies = (box_range >= box_low[:, None, :]) & (box_range < box_high[:, None, :])
    place = jnp.where(lies, packed_start[:, None, :] + box_range, -1)
    place = jnp.pad(place, ((0, 0), (0, 0), (0, SLOT - fun_dev)), constant_values=-1)
    place_rows = place.reshape(slots, boxes // STEP, STEP * SLOT).transpose(1, 0, 2)

    keep = np.zeros((slots * SLOT, window), np.float32)
    for e in range(slots):
        for f in range(fun_dev):
            keep[e * SLOT + f, e * fun_dev + f] = 1.0
    wide = slots * SLOT
    sources = [flat if e == REACH else arrived[REACH - e] for e in range(slots)]
    width_of = width.reshape(1)
    smem = pl.BlockSpec(memory_space=pltpu.SMEM)
    block = pl.BlockSpec((STEP, wide, points), lambda g: (g, 0, 0))
    pieces, partial = pl.pallas_call(
        functools.partial(unpack_kernel, slots),
        grid=(boxes // STEP,),
        out_shape=(
            jax.ShapeDtypeStruct((boxes, wide, points), jnp.bfloat16),
            jax.ShapeDtypeStruct((window, window), jnp.float32),
        ),
        in_specs=[smem, whole(columns.shape), whole(keep.shape)] + [whole(s.shape) for s in sources],
        out_specs=(block, whole((window, window))),
        scratch_shapes=[pltpu.VMEM((wide, wide), jnp.float32)],
        compiler_params=pltpu.CompilerParams(vmem_limit_bytes=48 * 2**20),
        name="unpack",
    )(width_of, columns, jnp.asarray(keep), *sources)
    partial = volume * partial

    waited, _ = lax.optimization_barrier((potential, tuple(arrived.values())))
    nearby = [waited if t == 0 else passed_along(waited, -t) for t in range(blocks)]
    nearby = jnp.pad(jnp.concatenate(nearby), ((0, max(0, high_cut + boxes - blocks * box_dev)), (0, 0)))
    region = lax.dynamic_slice_in_dim(nearby, start_cut, boxes)

    gram_rows = 0.0
    for k in order:
        at = (REACH - k) * fun_dev
        if k == 0:
            other = partial[at : at + fun_dev]
        else:
            sent_at = (REACH + k) * fun_dev
            other = passed_along(partial[sent_at : sent_at + fun_dev], k)
        gram_rows = gram_rows + jnp.pad(other, ((0, 0), (at, 2 * REACH * fun_dev - at)))
    first = 2 * REACH * fun_dev - (reading - 1)
    gram_band = jnp.stack([gram_rows[r, first + r : first + r + 2 * reading] for r in range(fun_dev)])
    gram_band = jnp.where(jnp.arange(2 * reading) < 2 * reading - 1, gram_band, 0.0)
    eye = jnp.eye(fun_dev, gram_rows.shape[1], 2 * REACH * fun_dev, dtype=jnp.float32)
    correction_rows = (1.5 * eye - 0.5 * gram_rows).astype(jnp.bfloat16)
    mixing_rows = [None] * slots
    for k in order:
        at = (REACH + k) * fun_dev
        sent = correction_rows[:, at : at + window]
        mixing_rows[REACH - k] = sent if k == 0 else passed_along(sent, k)
    correction = jnp.stack(mixing_rows)
    spaced = jnp.pad(
        correction.reshape(slots, fun_dev, slots, fun_dev),
        ((0, 0), (0, SLOT - fun_dev), (0, 0), (0, SLOT - fun_dev)),
    ).reshape(wide, wide)

    out_rows = [rows_of[REACH - e] for e in range(slots)]
    packed = pl.pallas_call(
        functools.partial(mix_kernel, slots),
        grid=(boxes // STEP,),
        out_shape=tuple(jax.ShapeDtypeStruct((r, points), jnp.bfloat16) for r in out_rows),
        in_specs=[
            smem,
            whole((wide, wide)),
            pl.BlockSpec((1, slots, STEP * SLOT), lambda g: (g, 0, 0)),
            block,
        ],
        out_specs=tuple(whole((r, points)) for r in out_rows),
        scratch_shapes=[pltpu.VMEM((STEP, wide, points), jnp.bfloat16)],
        compiler_params=pltpu.CompilerParams(vmem_limit_bytes=48 * 2**20),
        name="mix",
    )(width_of, spaced, place_rows, pieces)

    returned = {}
    for k in order:
        e = REACH - k
        here = packed[e]
        at_box = jnp.any(
            place[e][None] == jnp.arange(rows_of[k], dtype=jnp.int32)[:, None, None], axis=-1
        ).astype(jnp.float32)
        local = jnp.dot(at_box, region, precision=lax.Precision.HIGHEST)
        applied = jnp.dot(here, kinetic, preferred_element_type=jnp.float32)
        applied = (applied + local * here.astype(jnp.float32)).astype(jnp.bfloat16)
        returned[k] = applied if k == 0 else passed_along(applied, -k)

    parts = fun_dev * support // 256
    filtered = pl.pallas_call(
        functools.partial(home_kernel, slots, [bases[k] for k in offsets]),
        grid=(parts,),
        out_shape=jax.ShapeDtypeStruct((fun_dev * support, points), jnp.bfloat16),
        in_specs=[pl.BlockSpec((256, 8), lambda g: (g, 0))] + [whole((rows_of[k], points)) for k in offsets],
        out_specs=pl.BlockSpec((256, points), lambda g: (g, 0)),
        compiler_params=pltpu.CompilerParams(vmem_limit_bytes=32 * 2**20),
        name="home",
    )(home_column, *[returned[k] for k in offsets])
    return (filtered.reshape(coeffs.shape), gram_band)


def solution(mesh):
    placed = (P(AXES, None, None), P(), P(), P(AXES, None))
    return jax.shard_map(
        on_device,
        mesh=mesh,
        in_specs=placed,
        out_specs=(P(AXES, None, None), P(AXES, None)),
        check_vma=False,
    )
```

```python
import functools
import itertools

import jax
import jax.numpy as jnp
import numpy as np
from jax import lax
from jax.experimental import pallas as pl
from jax.experimental.pallas import tpu as pltpu
from jax.sharding import PartitionSpec as P

AXES = ("func", "box")
REACH = 3
SLOT = 32
STEP = 8


def passed_along(value, steps):
    count = lax.axis_size(AXES)
    pairs = [(source, (source + steps) % count) for source in range(count)]
    return lax.ppermute(value, AXES, pairs)


def rounded_up(value, multiple):
    return -(-int(value) // multiple) * multiple


@functools.lru_cache(maxsize=None)
def bounds(fun_dev, support):
    box_dev = fun_dev // 2
    orders = [
        order
        for order in sorted(set(itertools.permutations((1, 1, 2, 4))))
        if np.abs(np.cumsum(np.array(order) - 2)).max() <= 1
    ]
    box_all, fun_all = 12 * support, 24 * support
    assert fun_all % fun_dev == 0
    devices = fun_all // fun_dev
    rows = np.zeros(2 * REACH + 1, np.int64)
    low, high, boxes, end = 10**6, -(10**6), 0, 0
    for picks in itertools.product(orders, repeat=3):
        density = np.repeat(np.concatenate(picks), support)
        centers = np.repeat(np.arange(box_all), density)
        load = sum(np.roll(density, t) for t in range(support))
        below = np.concatenate([[0], np.cumsum(np.tile(load, 3))])
        over = np.clip(np.arange(box_all)[:, None] + support - box_all, 0, None)
        carried = int((over[:, 0] * density).sum())
        below = below - carried
        twice = below[:-1] + below[1:]
        cut = np.array([
            np.searchsorted(twice, 2 * support * fun_dev * (devices + d), side="right")
            for d in range(-REACH - 1, devices + REACH + 2)
        ]) - box_all
        first = REACH + 1
        width = np.diff(cut)
        place = cut - box_dev * (np.arange(len(cut)) - first)
        low, high = min(low, place.min()), max(high, place.max())
        boxes = max(boxes, width.max())
        end = max(end, (place[:-1] + width).max())
        box = centers[:, None] + np.arange(support)
        owner = np.searchsorted(cut, box, side="right") - 1 - first
        device = np.arange(fun_all)[:, None] // fun_dev
        offset = owner - device
        assert np.abs(offset).max() <= REACH
        count = np.bincount((device * (2 * REACH + 1) + offset + REACH).ravel(), minlength=devices * (2 * REACH + 1))
        rows = np.maximum(rows, count.reshape(devices, -1).max(0))
    return (
        tuple(rounded_up(r, 32 if k < REACH else 16) for k, r in enumerate(rows)),
        int(low),
        int(high),
        rounded_up(boxes, STEP),
        -(-int(end) // box_dev),
    )


def iota(shape, dim):
    return lax.broadcasted_iota(jnp.int32, shape, dim).astype(jnp.float32)


def one_hot(mask):
    return jnp.where(mask, 1.0, 0.0).astype(jnp.bfloat16)


def spread_over(column, to):
    return jnp.sum(jnp.where(iota((column.shape[0], to.shape[1]), 0) == to, column, 0.0), axis=0, keepdims=True)


def times(a, b, dims=((1,), (0,)), precision=None):
    return lax.dot_general(
        a, b, (dims, ((), ())), precision=precision, preferred_element_type=jnp.float32
    )


def pack_kernel(plan, me_ref, centers_ref, flat_ref, potential_ref, *refs):
    fun_dev, support, devices, halo, rows, low_cut, high_cut = plan
    slots = 2 * REACH + 1
    outs = dict(zip([k for k in range(-REACH, REACH + 1) if k], refs[: slots - 1]))
    near_ref, cut_ref, home_ref, own_ref = refs[slots - 1 :]
    me = me_ref[0]
    box_dev = fun_dev // 2
    fun_all, box_all = fun_dev * devices, box_dev * devices
    count = near_ref.shape[0]

    start = me * fun_dev - halo * fun_dev
    start = jnp.where(start < 0, start + fun_all, start).astype(jnp.float32)
    at = start + iota((count, 1), 0)
    at = jnp.where(at >= fun_all, at - fun_all, at)
    near = jnp.sum(
        jnp.where(iota((count, fun_all), 1) == at, centers_ref[...].astype(jnp.float32), 0.0), axis=1, keepdims=True
    )
    near = near - (me * box_dev).astype(jnp.float32)
    near = jnp.where(near < -(box_all // 2), near + box_all, near)
    near = jnp.where(near >= box_all // 2, near - box_all, near)
    near_row = spread_over(near, iota((1, count), 1))
    near_ref[...] = jnp.broadcast_to(near, near_ref.shape)

    tries = high_cut - low_cut + 1
    trial = iota((rounded_up(tries, 8), 1), 0)
    cuts = []
    for k in range(-REACH, REACH + 2):
        gap = trial + float(low_cut + k * box_dev) - near_row
        twice = jnp.sum(
            jnp.clip(gap, 0.0, support) + jnp.clip(gap + 1.0, 0.0, support), axis=1, keepdims=True
        )
        goal = float(2 * support * fun_dev * (halo + k))
        passed = jnp.where((twice <= goal) & (trial < tries), 1.0, 0.0)
        cut = jnp.sum(passed) + float(low_cut + k * box_dev)
        cuts.append(cut)
        cut_ref[k + REACH] = cut.astype(jnp.int32)

    mine = near[halo * fun_dev : (halo + 1) * fun_dev]
    pieces = fun_dev * support
    piece = lax.broadcasted_iota(jnp.int32, (1, pieces), 1)
    of_fun = lax.shift_right_logical(piece, support.bit_length() - 1).astype(jnp.float32)
    step = piece.astype(jnp.float32) - of_fun * support
    mine_row = spread_over(mine, of_fun)
    earlier = iota((fun_dev, pieces), 0) < of_fun
    potential = potential_ref[...]
    high = potential.astype(jnp.bfloat16)
    low = (potential - high.astype(jnp.float32)).astype(jnp.bfloat16)
    half = potential.shape[0]
    own_ref[:half] = high
    own_ref[half:] = low
    home, base = jnp.zeros((1, pieces), jnp.float32), 0
    for k in range(-REACH, REACH + 1):
        first, end = cuts[k + REACH], cuts[k + REACH + 1]
        leave = jnp.clip(end - mine, 0.0, support) - jnp.clip(first - mine, 0.0, support)
        leave_at = jnp.sum(jnp.where(earlier, leave, 0.0), axis=0, keepdims=True)
        low_edge = jnp.clip(first - mine_row, 0.0, support)
        goes = (step >= low_edge) & (step < jnp.clip(end - mine_row, 0.0, support))
        row = leave_at + step - low_edge
        home = home + jnp.where(goes, row + float(base), 0.0)
        base += rows[k + REACH]
        if k:
            row = jnp.where(goes, row, -1.0)
            pick = one_hot(iota((rows[k + REACH], pieces), 0) == row)
            outs[k][: rows[k + REACH]] = times(pick, flat_ref[...]).astype(jnp.bfloat16)
            if k < 0:
                outs[k][rows[k + REACH] : rows[k + REACH] + half] = high
                outs[k][rows[k + REACH] + half :] = low
    home_ref[...] = home


def table_kernel(plan, cut_ref, near_ref, column_ref, place_ref):
    fun_dev, support, halo, boxes = plan
    slots = 2 * REACH + 1
    first = cut_ref[REACH].astype(jnp.float32)
    end = cut_ref[REACH + 1].astype(jnp.float32)
    lane = iota((SLOT, 128), 1)
    along = lax.broadcasted_iota(jnp.int32, (1, boxes * SLOT), 1)
    box = lax.shift_right_logical(along, SLOT.bit_length() - 1).astype(jnp.float32)
    of_fun = along.astype(jnp.float32) - box * SLOT
    for e in range(slots):
        at = (halo - REACH + e) * fun_dev
        others = near_ref[at : at + fun_dev, 0:1]
        edge_low = jnp.clip(first - others, 0.0, support)
        edge_high = jnp.clip(end - others, 0.0, support)
        come = edge_high - edge_low
        come_row = spread_over(come, lane[:1])
        come_at = jnp.sum(
            jnp.where(lane[:fun_dev] < iota((fun_dev, 128), 0), come_row, 0.0), axis=1, keepdims=True
        )
        box_low = edge_low + others - first
        box_high = edge_high + others - first
        packed = come_at - box_low
        unpacked = iota((fun_dev, 1), 0) * support + first - others if e == REACH else packed
        spare = jnp.zeros((SLOT - fun_dev, 1), jnp.float32)
        packed, unpacked, box_low, box_high = (
            jnp.concatenate([column, spare], axis=0) for column in (packed, unpacked, box_low, box_high)
        )
        column_ref[e * SLOT : (e + 1) * SLOT, :] = jnp.where(
            lane == 0.0, unpacked, jnp.where(lane == 1.0, box_low, box_high)
        )
        lies = (box >= spread_over(box_low, of_fun)) & (box < spread_over(box_high, of_fun))
        place_ref[e : e + 1, :] = jnp.where(lies, spread_over(packed, of_fun) + box, -1.0)
    place_ref[slots:, :] = jnp.full((place_ref.shape[0] - slots, boxes * SLOT), -1.0, jnp.float32)


def function_of(shape, dim, fun_dev):
    row = lax.broadcasted_iota(jnp.int32, shape, dim)
    slot = lax.shift_right_logical(row, SLOT.bit_length() - 1)
    in_slot = row - slot * SLOT
    return jnp.where(in_slot < fun_dev, slot * fun_dev + in_slot, -1)


def moved(value, shift):
    return pltpu.roll(value, shift % value.shape[1], 1)


def skewed(value, sign):
    row = lax.broadcasted_iota(jnp.int32, value.shape, 0)
    bit = 1
    while bit < value.shape[0]:
        value = jnp.where((row & bit) != 0, moved(value, sign * bit), value)
        bit *= 2
    return value


def unpack_kernel(plan, cut_ref, me_ref, column_ref, *refs):
    fun_dev, devices, reading, volume, rows = plan
    slots = 2 * REACH + 1
    sources = refs[:slots]
    window_ref, gram_ref, total = refs[slots:]
    step = pl.program_id(0)
    first = step * STEP
    width = cut_ref[REACH + 1] - cut_ref[REACH]

    @pl.when(step == 0)
    def _():
        total[...] = jnp.zeros_like(total)

    @pl.when(first < width)
    def _():
        for e in range(slots):
            start = column_ref[e * SLOT : (e + 1) * SLOT, 0:1]
            low = column_ref[e * SLOT : (e + 1) * SLOT, 1:2]
            high = column_ref[e * SLOT : (e + 1) * SLOT, 2:3]
            lane = iota((SLOT, rows[e]), 1)
            picks = []
            for b in range(STEP):
                box = (first + b).astype(jnp.float32)
                row = jnp.where((box >= low) & (box < high), start + box, -1.0)
                picks.append(one_hot(lane == row))
            found = times(jnp.concatenate(picks, axis=0), sources[e][: rows[e]])
            window_ref[:, e * SLOT : (e + 1) * SLOT, :] = found.astype(jnp.bfloat16).reshape(
                STEP, SLOT, found.shape[-1]
            )
        for b in range(STEP):
            here = window_ref[b]
            total[...] += times(here, here, ((1,), (1,)))

    @pl.when(step == pl.num_programs(0) - 1)
    def _():
        wide, window = total.shape[0], slots * fun_dev
        lanes = rounded_up(window + 2 * reading, 128)
        keep_rows = jnp.where(
            function_of((window, wide), 1, fun_dev) == lax.broadcasted_iota(jnp.int32, (window, wide), 0), 1.0, 0.0
        )
        keep_lanes = jnp.where(
            function_of((wide, lanes), 0, fun_dev) == lax.broadcasted_iota(jnp.int32, (wide, lanes), 1), volume, 0.0
        )
        exact = lax.Precision.HIGHEST
        dense = times(times(keep_rows, total[...], precision=exact), keep_lanes, precision=exact)
        gram_ref[...] = jnp.zeros_like(gram_ref)
        for e in range(slots):
            band = moved(dense[e * fun_dev : (e + 1) * fun_dev], reading - 1 - e * fun_dev)
            device = me_ref[0] + (e - REACH)
            device = jnp.where(device < 0, device + devices, device)
            device = jnp.where(device >= devices, device - devices, device)
            gram_ref[device] = skewed(band, -1)[:, : 2 * reading]


def mix_kernel(plan, cut_ref, me_ref, place_ref, window_ref, gram_ref, kinetic_ref, *refs):
    fun_dev, box_dev, devices, reading, blocks = plan
    slots = 2 * REACH + 1
    regions = refs[:blocks]
    outs = refs[blocks : blocks + slots]
    own_box_ref, region_ref = refs[blocks + slots : blocks + slots + 2]
    mixing, mixed = refs[blocks + slots + 2 : blocks + slots + 4]
    at_boxes = refs[blocks + slots + 4 :]
    at_boxes = at_boxes[:REACH] + (own_box_ref,) + at_boxes[REACH:]
    step = pl.program_id(0)
    width = cut_ref[REACH + 1] - cut_ref[REACH]
    wide = slots * SLOT

    @pl.when(step == 0)
    def _():
        for out, at_box in zip(outs, at_boxes):
            out[...] = jnp.zeros_like(out)
            at_box[...] = jnp.zeros_like(at_box)
        lanes = rounded_up(slots * fun_dev + 2 * reading, 128)
        lane = lax.broadcasted_iota(jnp.int32, (fun_dev, lanes), 1)
        parts = []
        for e in range(slots):
            device = me_ref[0] + (e - REACH)
            device = jnp.where(device < 0, device + devices, device)
            device = jnp.where(device >= devices, device - devices, device)
            band = gram_ref[device]
            band = jnp.concatenate([band, jnp.zeros((fun_dev, lanes - 2 * reading), jnp.float32)], axis=1)
            band = jnp.where(lane == reading - 1, 1.5, 0.0) - 0.5 * band
            parts.append(moved(skewed(band, 1), e * fun_dev - (reading - 1)))
            parts.append(jnp.zeros((SLOT - fun_dev, lanes), jnp.float32))
        dense = jnp.concatenate(parts, axis=0).astype(jnp.bfloat16)
        keep = one_hot(
            function_of((lanes, wide), 1, fun_dev) == lax.broadcasted_iota(jnp.int32, (lanes, wide), 0)
        )
        mixing[...] = times(dense, keep).astype(jnp.bfloat16)
        half = regions[0].shape[0] // 2
        value = None
        for t in range(blocks):
            shape = (region_ref.shape[0], 2 * half)
            row, col = iota(shape, 0), iota(shape, 1)
            box = row - jnp.where(row >= SLOT, float(SLOT), 0.0) + cut_ref[REACH].astype(jnp.float32) - t * box_dev
            wanted = box + jnp.where(row >= SLOT, float(half), 0.0)
            good = (box >= 0) & (box < box_dev) & (row < 2 * SLOT)
            term = times(one_hot(good & (col == wanted)), regions[t][...])
            value = term if value is None else value + term
        region_ref[...] = value.astype(jnp.bfloat16)

    @pl.when(step * STEP < width)
    def _():
        for b in range(STEP):
            mixed[b] = times(mixing[...], window_ref[b]).astype(jnp.bfloat16)
        shape = (STEP * SLOT, region_ref.shape[0])
        along = lax.broadcasted_iota(jnp.int32, shape, 0)
        box = lax.shift_right_logical(along, SLOT.bit_length() - 1) + step * STEP
        col = lax.broadcasted_iota(jnp.int32, shape, 1)
        boxes_of = one_hot((col == box) | (col == box + SLOT))
        for e in range(slots):
            pick = one_hot(iota((outs[e].shape[0], STEP * SLOT), 0) == place_ref[e : e + 1, :])
            part = mixed[:, e * SLOT : (e + 1) * SLOT, :].reshape(STEP * SLOT, mixed.shape[-1])
            outs[e][...] += times(pick, part).astype(jnp.bfloat16)
            at_boxes[e][...] += times(pick, boxes_of).astype(jnp.bfloat16)

    @pl.when(step == pl.num_programs(0) - 1)
    def _():
        for e in range(slots):
            if e != REACH:
                filtered_rows(outs[e], outs[e], at_boxes[e], region_ref, kinetic_ref)


def filtered_rows(out_ref, here_ref, at_box_ref, region_ref, kinetic_ref):
    here = here_ref[...]
    local = times(at_box_ref[...], region_ref[...])
    applied = times(here, kinetic_ref[...])
    out_ref[...] = (applied + local * here.astype(jnp.float32)).astype(jnp.bfloat16)


def local_kernel(here_ref, at_box_ref, region_ref, kinetic_ref, out_ref):
    filtered_rows(out_ref, here_ref, at_box_ref, region_ref, kinetic_ref)


def home_kernel(groups, home_ref, *refs):
    sources, out_ref = refs[:-1], refs[-1]
    count = out_ref.shape[0]
    shape = (count, home_ref.shape[1])
    at = iota(shape, 0) + (pl.program_id(0) * count).astype(jnp.float32)
    row = jnp.sum(jnp.where(iota(shape, 1) == at, home_ref[...], 0.0), axis=1, keepdims=True)
    value, base = None, 0
    for group in groups:
        parts = [sources[e][...] for e in group]
        held = parts[0] if len(parts) == 1 else jnp.concatenate(parts, axis=0)
        pick = one_hot(iota((count, held.shape[0]), 1) == row - float(base))
        base += held.shape[0]
        term = times(pick, held)
        value = term if value is None else value + term
    out_ref[...] = value.astype(jnp.bfloat16)


def whole(shape):
    return pl.BlockSpec(shape, lambda g: (0,) * len(shape))


def on_device(coeffs, centers, kinetic, potential):
    fun_dev, support, points = coeffs.shape
    devices = lax.axis_size(AXES)
    me = lax.axis_index(AXES).astype(jnp.int32).reshape(1)
    box_dev = fun_dev // 2
    volume = 1.0 / (support * points)
    reading = 4 * support
    slots = 2 * REACH + 1
    offsets = list(range(-REACH, REACH + 1))
    order = sorted([k for k in offsets if k], key=lambda k: (abs(abs(k) - 1.9), k))
    rows, low_cut, high_cut, boxes, blocks = bounds(fun_dev, support)
    assert blocks <= REACH + 1 and support & (support - 1) == 0
    rows_of = {k: rows[k + REACH] for k in offsets}
    flat = coeffs.reshape(fun_dev * support, points)
    halo = REACH + -(-(reading + 8) // fun_dev)
    count = rounded_up((2 * halo + 2) * fun_dev, 128)
    half = rounded_up(box_dev, 16)
    bf16, f32 = jnp.bfloat16, jnp.float32
    smem = pl.BlockSpec(memory_space=pltpu.SMEM)
    limit = pltpu.CompilerParams(vmem_limit_bytes=52 * 2**20)

    sent_rows = [rows_of[k] + (2 * half if k < 0 else 0) for k in offsets if k]
    *packed, near, cut, home_row, own_region = pl.pallas_call(
        functools.partial(pack_kernel, (fun_dev, support, devices, halo, rows, low_cut, high_cut)),
        out_shape=tuple(jax.ShapeDtypeStruct((r, points), bf16) for r in sent_rows)
        + (
            jax.ShapeDtypeStruct((count, 128), f32),
            jax.ShapeDtypeStruct((slots + 1,), jnp.int32),
            jax.ShapeDtypeStruct((1, fun_dev * support), f32),
            jax.ShapeDtypeStruct((2 * half, points), bf16),
        ),
        in_specs=[smem] + [pl.BlockSpec(memory_space=pltpu.VMEM)] * 3,
        out_specs=tuple(pl.BlockSpec(memory_space=pltpu.VMEM) for _ in range(slots)) + (smem,)
        + tuple(pl.BlockSpec(memory_space=pltpu.VMEM) for _ in range(2)),
        compiler_params=limit,
        name="pack",
    )(me, centers.reshape(1, -1), flat, jnp.pad(potential, ((0, half - box_dev), (0, 0))))
    packed = dict(zip([k for k in offsets if k], packed))
    arrived = {k: passed_along(packed[k], k) for k in order}

    columns, places = pl.pallas_call(
        functools.partial(table_kernel, (fun_dev, support, halo, boxes)),
        out_shape=(
            jax.ShapeDtypeStruct((slots * SLOT, 128), f32),
            jax.ShapeDtypeStruct((8, boxes * SLOT), f32),
        ),
        in_specs=[smem, pl.BlockSpec(memory_space=pltpu.VMEM)],
        compiler_params=limit,
        name="tables",
    )(cut, near)

    wide = slots * SLOT
    sources = [flat if e == REACH else arrived[REACH - e] for e in range(slots)]
    read_rows = [flat.shape[0] if e == REACH else rows_of[REACH - e] for e in range(slots)]
    block = pl.BlockSpec((STEP, wide, points), lambda g: (g, 0, 0))
    band = (devices, fun_dev, 2 * reading)
    pieces, partial = pl.pallas_call(
        functools.partial(unpack_kernel, (fun_dev, devices, reading, volume, read_rows)),
        grid=(boxes // STEP,),
        out_shape=(jax.ShapeDtypeStruct((boxes, wide, points), bf16), jax.ShapeDtypeStruct(band, f32)),
        in_specs=[smem, smem, whole(columns.shape)] + [whole(s.shape) for s in sources],
        out_specs=(block, whole(band)),
        scratch_shapes=[pltpu.VMEM((wide, wide), f32)],
        compiler_params=limit,
        name="unpack",
    )(cut, me, columns, *sources)

    gram = lax.psum(partial, AXES)
    gram_band = lax.dynamic_index_in_dim(gram, me[0], 0, keepdims=False)

    out_rows = [rows_of[REACH - e] for e in range(slots)]
    regions = [own_region] + [arrived[-t] for t in range(1, blocks)]
    region_specs = [whole((2 * half, points))] + [
        pl.BlockSpec((2 * half, points), lambda g, at=rows_of[-t] // (2 * half): (at, 0)) for t in range(1, blocks)
    ]
    *mixed, own_boxes, region = pl.pallas_call(
        functools.partial(mix_kernel, (fun_dev, box_dev, devices, reading, blocks)),
        grid=(boxes // STEP,),
        out_shape=tuple(jax.ShapeDtypeStruct((r, points), bf16) for r in out_rows)
        + (jax.ShapeDtypeStruct((rows_of[0], 128), bf16), jax.ShapeDtypeStruct((128, points), bf16)),
        in_specs=[
            smem,
            smem,
            pl.BlockSpec((8, STEP * SLOT), lambda g: (0, g)),
            block,
            whole(band),
            whole(kinetic.shape),
        ]
        + region_specs,
        out_specs=tuple(whole((r, points)) for r in out_rows) + (whole((rows_of[0], 128)), whole((128, points))),
        scratch_shapes=[pltpu.VMEM((wide, wide), bf16), pltpu.VMEM((STEP, wide, points), bf16)]
        + [pltpu.VMEM((r, 128), bf16) for e, r in enumerate(out_rows) if e != REACH],
        compiler_params=limit,
        name="mix",
    )(cut, me, places, pieces, gram, kinetic, *regions)

    returned = {k: passed_along(mixed[REACH - k], -k) for k in order}
    returned[0] = pl.pallas_call(
        local_kernel,
        grid=(rows_of[0] // 256,),
        out_shape=jax.ShapeDtypeStruct((rows_of[0], points), bf16),
        in_specs=[
            pl.BlockSpec((256, points), lambda g: (g, 0)),
            pl.BlockSpec((256, 128), lambda g: (g, 0)),
            whole(region.shape),
            whole(kinetic.shape),
        ],
        out_specs=pl.BlockSpec((256, points), lambda g: (g, 0)),
        compiler_params=limit,
        name="local",
    )(mixed[REACH], own_boxes, region, kinetic)

    groups, held = [], 257
    for e, k in enumerate(offsets):
        if held + rows_of[k] <= 256:
            groups[-1].append(e)
            held += rows_of[k]
        else:
            groups.append([e])
            held = rows_of[k]
    filtered = pl.pallas_call(
        functools.partial(home_kernel, groups),
        grid=(fun_dev * support // 256,),
        out_shape=jax.ShapeDtypeStruct((fun_dev * support, points), bf16),
        in_specs=[whole(home_row.shape)] + [whole((rows_of[k], points)) for k in offsets],
        out_specs=pl.BlockSpec((256, points), lambda g: (g, 0)),
        compiler_params=limit,
        name="home",
    )(home_row, *[returned[k] for k in offsets])
    return (filtered.reshape(coeffs.shape), gram_band)


def solution(mesh):
    placed = (P(AXES, None, None), P(), P(), P(AXES, None))
    return jax.shard_map(
        on_device,
        mesh=mesh,
        in_specs=placed,
        out_specs=(P(AXES, None, None), P(AXES, None)),
        check_vma=False,
    )
```

```python
import functools
import itertools

import jax
import jax.numpy as jnp
import numpy as np
from jax import lax
from jax.experimental import pallas as pl
from jax.experimental.pallas import tpu as pltpu
from jax.sharding import PartitionSpec as P

AXES = ("func", "box")
REACH = 3
SLOT = 32
STEP = 8


def passed_along(value, steps):
    count = lax.axis_size(AXES)
    pairs = [(source, (source + steps) % count) for source in range(count)]
    return lax.ppermute(value, AXES, pairs)


def sent_in_order(values, order, sign):
    there = {}
    for k in order:
        value = values[k]
        if k == order[-1]:
            value, there[order[0]] = lax.optimization_barrier((value, there[order[0]]))
        there[k] = passed_along(value, sign * k)
    return there


def rounded_up(value, multiple):
    return -(-int(value) // multiple) * multiple


@functools.lru_cache(maxsize=None)
def bounds(fun_dev, support):
    box_dev = fun_dev // 2
    orders = [
        order
        for order in sorted(set(itertools.permutations((1, 1, 2, 4))))
        if np.abs(np.cumsum(np.array(order) - 2)).max() <= 1
    ]
    box_all, fun_all = 12 * support, 24 * support
    assert fun_all % fun_dev == 0
    devices = fun_all // fun_dev
    rows = np.zeros(2 * REACH + 1, np.int64)
    low, high, boxes, end = 10**6, -(10**6), 0, 0
    for picks in itertools.product(orders, repeat=3):
        density = np.repeat(np.concatenate(picks), support)
        centers = np.repeat(np.arange(box_all), density)
        load = sum(np.roll(density, t) for t in range(support))
        below = np.concatenate([[0], np.cumsum(np.tile(load, 3))])
        over = np.clip(np.arange(box_all)[:, None] + support - box_all, 0, None)
        carried = int((over[:, 0] * density).sum())
        below = below - carried
        twice = below[:-1] + below[1:]
        cut = np.array([
            np.searchsorted(twice, 2 * support * fun_dev * (devices + d), side="right")
            for d in range(-REACH - 1, devices + REACH + 2)
        ]) - box_all
        first = REACH + 1
        width = np.diff(cut)
        place = cut - box_dev * (np.arange(len(cut)) - first)
        low, high = min(low, place.min()), max(high, place.max())
        boxes = max(boxes, width.max())
        end = max(end, (place[:-1] + width).max())
        box = centers[:, None] + np.arange(support)
        owner = np.searchsorted(cut, box, side="right") - 1 - first
        device = np.arange(fun_all)[:, None] // fun_dev
        offset = owner - device
        assert np.abs(offset).max() <= REACH
        count = np.bincount((device * (2 * REACH + 1) + offset + REACH).ravel(), minlength=devices * (2 * REACH + 1))
        rows = np.maximum(rows, count.reshape(devices, -1).max(0))
    return (
        tuple(int(r) for r in rows),
        int(low),
        int(high),
        rounded_up(boxes, STEP),
        -(-int(end) // box_dev),
    )


def iota(shape, dim):
    return lax.broadcasted_iota(jnp.int32, shape, dim).astype(jnp.float32)


def one_hot(mask):
    return jnp.where(mask, 1.0, 0.0).astype(jnp.bfloat16)


def spread_over(column, to):
    return jnp.sum(jnp.where(iota((column.shape[0], to.shape[1]), 0) == to, column, 0.0), axis=0, keepdims=True)


def times(a, b, dims=((1,), (0,)), precision=None):
    return lax.dot_general(
        a, b, (dims, ((), ())), precision=precision, preferred_element_type=jnp.float32
    )


def pack_kernel(plan, me_ref, centers_ref, flat_ref, potential_ref, *refs):
    fun_dev, support, devices, halo, rows, back, low_cut, high_cut = plan
    slots = 2 * REACH + 1
    outs = dict(zip([k for k in range(-REACH, REACH + 1) if k], refs[: slots - 1]))
    near_ref, cut_ref, home_ref, own_ref = refs[slots - 1 :]
    me = me_ref[0]
    box_dev = fun_dev // 2
    fun_all, box_all = fun_dev * devices, box_dev * devices
    count = near_ref.shape[0]

    start = me * fun_dev - halo * fun_dev
    start = jnp.where(start < 0, start + fun_all, start).astype(jnp.float32)
    at = start + iota((count, 1), 0)
    at = jnp.where(at >= fun_all, at - fun_all, at)
    near = jnp.sum(
        jnp.where(iota((count, fun_all), 1) == at, centers_ref[...].astype(jnp.float32), 0.0), axis=1, keepdims=True
    )
    near = near - (me * box_dev).astype(jnp.float32)
    near = jnp.where(near < -(box_all // 2), near + box_all, near)
    near = jnp.where(near >= box_all // 2, near - box_all, near)
    near_row = spread_over(near, iota((1, count), 1))
    near_ref[...] = jnp.broadcast_to(near, near_ref.shape)

    tries = high_cut - low_cut + 1
    trial = iota((rounded_up(tries, 8), 1), 0)
    cuts = []
    for k in range(-REACH, REACH + 2):
        gap = trial + float(low_cut + k * box_dev) - near_row
        twice = jnp.sum(
            jnp.clip(gap, 0.0, support) + jnp.clip(gap + 1.0, 0.0, support), axis=1, keepdims=True
        )
        goal = float(2 * support * fun_dev * (halo + k))
        passed = jnp.where((twice <= goal) & (trial < tries), 1.0, 0.0)
        cut = jnp.sum(passed) + float(low_cut + k * box_dev)
        cuts.append(cut)
        cut_ref[k + REACH] = cut.astype(jnp.int32)

    mine = near[halo * fun_dev : (halo + 1) * fun_dev]
    pieces = fun_dev * support
    piece = lax.broadcasted_iota(jnp.int32, (1, pieces), 1)
    of_fun = lax.shift_right_logical(piece, support.bit_length() - 1).astype(jnp.float32)
    step = piece.astype(jnp.float32) - of_fun * support
    mine_row = spread_over(mine, of_fun)
    earlier = iota((fun_dev, pieces), 0) < of_fun
    potential = potential_ref[...]
    high = potential.astype(jnp.bfloat16)
    own_ref[: potential.shape[0]] = high
    own_ref[potential.shape[0] :] = (potential - high.astype(jnp.float32)).astype(jnp.bfloat16)
    home, base = jnp.zeros((1, pieces), jnp.float32), 0
    for k in range(-REACH, REACH + 1):
        first, end = cuts[k + REACH], cuts[k + REACH + 1]
        leave = jnp.clip(end - mine, 0.0, support) - jnp.clip(first - mine, 0.0, support)
        leave_at = jnp.sum(jnp.where(earlier, leave, 0.0), axis=0, keepdims=True)
        low_edge = jnp.clip(first - mine_row, 0.0, support)
        goes = (step >= low_edge) & (step < jnp.clip(end - mine_row, 0.0, support))
        row = leave_at + step - low_edge
        home = home + jnp.where(goes, row + float(base), 0.0)
        base += back[k + REACH]
        if k:
            row = jnp.where(goes, row, -1.0)
            sent = outs[k].shape[0]
            value = times(one_hot(iota((sent, pieces), 0) == row), flat_ref[...])
            if k < 0:
                shape = (sent, own_ref.shape[0])
                part = iota(shape, 0) - float(rows[k + REACH])
                col = iota(shape, 1)
                half = float(own_ref.shape[0] // 2)
                from_col = jnp.where(part < box_dev, part, part - box_dev + half)
                inside = (part >= 0) & (part < 2 * box_dev)
                value = value + times(one_hot(inside & (col == from_col)), own_ref[...])
            outs[k][...] = value.astype(jnp.bfloat16)
    home_ref[...] = home


def table_kernel(plan, cut_ref, near_ref, column_ref, place_ref, active_ref):
    fun_dev, support, halo, boxes = plan
    slots = 2 * REACH + 1
    first = cut_ref[REACH].astype(jnp.float32)
    end = cut_ref[REACH + 1].astype(jnp.float32)
    lane = iota((SLOT, 128), 1)
    along = lax.broadcasted_iota(jnp.int32, (1, boxes * SLOT), 1)
    box = lax.shift_right_logical(along, SLOT.bit_length() - 1).astype(jnp.float32)
    of_fun = along.astype(jnp.float32) - box * SLOT
    for e in range(slots):
        at = (halo - REACH + e) * fun_dev
        others = near_ref[at : at + fun_dev, 0:1]
        edge_low = jnp.clip(first - others, 0.0, support)
        edge_high = jnp.clip(end - others, 0.0, support)
        come = edge_high - edge_low
        come_row = spread_over(come, lane[:1])
        come_at = jnp.sum(
            jnp.where(lane[:fun_dev] < iota((fun_dev, 128), 0), come_row, 0.0), axis=1, keepdims=True
        )
        box_low = edge_low + others - first
        box_high = edge_high + others - first
        packed = come_at - box_low
        unpacked = iota((fun_dev, 1), 0) * support + first - others if e == REACH else packed
        spare = jnp.zeros((SLOT - fun_dev, 1), jnp.float32)
        packed, unpacked, box_low, box_high = (
            jnp.concatenate([column, spare], axis=0) for column in (packed, unpacked, box_low, box_high)
        )
        column_ref[e * SLOT : (e + 1) * SLOT, :] = jnp.where(
            lane == 0.0, unpacked, jnp.where(lane == 1.0, box_low, box_high)
        )
        lies = (box >= spread_over(box_low, of_fun)) & (box < spread_over(box_high, of_fun))
        place_ref[e : e + 1, :] = jnp.where(lies, spread_over(packed, of_fun) + box, -1.0)
        for g in range(boxes // STEP):
            here = (box >= g * STEP) & (box < (g + 1) * STEP) & lies
            active_ref[e * (boxes // STEP) + g] = jnp.sum(jnp.where(here, 1.0, 0.0)).astype(jnp.int32)
    place_ref[slots:, :] = jnp.full((place_ref.shape[0] - slots, boxes * SLOT), -1.0, jnp.float32)


def function_of(shape, dim, fun_dev):
    row = lax.broadcasted_iota(jnp.int32, shape, dim)
    slot = lax.shift_right_logical(row, SLOT.bit_length() - 1)
    in_slot = row - slot * SLOT
    return jnp.where(in_slot < fun_dev, slot * fun_dev + in_slot, -1)


def moved(value, shift):
    return pltpu.roll(value, shift % value.shape[1], 1)


def skewed(value, sign):
    row = lax.broadcasted_iota(jnp.int32, value.shape, 0)
    bit = 1
    while bit < value.shape[0]:
        value = jnp.where((row & bit) != 0, moved(value, sign * bit), value)
        bit *= 2
    return value


def band_lanes(fun_dev, reading):
    window = (2 * REACH + 1) * fun_dev
    return rounded_up(window + reading + fun_dev + max(0, window - reading), 128)


def unpack_kernel(plan, cut_ref, active_ref, column_ref, own_ref, *refs):
    fun_dev, box_dev, reading, volume, rows, back, blocks = plan
    slots = 2 * REACH + 1
    sources = refs[:slots]
    window_ref, region_ref = refs[slots : slots + 2]
    gram_refs = refs[slots + 2 : -1]
    total = refs[-1]
    step, steps = pl.program_id(0), pl.num_programs(0)
    first = step * STEP
    width = cut_ref[REACH + 1] - cut_ref[REACH]

    @pl.when(step == 0)
    def _():
        total[...] = jnp.zeros_like(total)
        value = None
        for t in range(blocks):
            held = own_ref if t == 0 else sources[REACH + t]
            at = 0 if t == 0 else rows[REACH + t]
            from_row = at // 16 * 16
            held = held[from_row:]
            second = own_ref.shape[0] // 2 if t == 0 else box_dev
            shape = (region_ref.shape[0], held.shape[0])
            row, col = iota(shape, 0), iota(shape, 1)
            box = row - jnp.where(row >= SLOT, float(SLOT), 0.0) + cut_ref[REACH].astype(jnp.float32) - t * box_dev
            wanted = box + jnp.where(row >= SLOT, float(second), 0.0) + float(at - from_row)
            good = (box >= 0) & (box < box_dev) & (row < 2 * SLOT)
            term = times(one_hot(good & (col == wanted)), held)
            value = term if value is None else value + term
        region_ref[...] = value.astype(jnp.bfloat16)

    @pl.when(first < width)
    def _():
        for e in range(slots):
            used = active_ref[e * steps + step] > 0

            @pl.when(used)
            def _():
                start = column_ref[e * SLOT : (e + 1) * SLOT, 0:1]
                low = column_ref[e * SLOT : (e + 1) * SLOT, 1:2]
                high = column_ref[e * SLOT : (e + 1) * SLOT, 2:3]
                lane = iota((SLOT, back[e]), 1)
                picks = []
                for b in range(STEP):
                    box = (first + b).astype(jnp.float32)
                    row = jnp.where((box >= low) & (box < high), start + box, -1.0)
                    picks.append(one_hot(lane == row))
                found = times(jnp.concatenate(picks, axis=0), sources[e][: back[e]])
                window_ref[:, e * SLOT : (e + 1) * SLOT, :] = found.astype(jnp.bfloat16).reshape(
                    STEP, SLOT, found.shape[-1]
                )

            @pl.when(jnp.logical_not(used))
            def _():
                window_ref[:, e * SLOT : (e + 1) * SLOT, :] = jnp.zeros(
                    (STEP, SLOT, window_ref.shape[-1]), jnp.bfloat16
                )
        value = total[...]
        for b in range(STEP):
            here = window_ref[b]
            value = value + times(here, here, ((1,), (1,)))
        total[...] = value

    @pl.when(step == steps - 1)
    def _():
        wide, lanes = total.shape[0], band_lanes(fun_dev, reading)
        keep = jnp.where(
            function_of((wide, lanes), 0, fun_dev) == lax.broadcasted_iota(jnp.int32, (wide, lanes), 1), volume, 0.0
        )
        dense = times(total[...], keep, precision=lax.Precision.HIGHEST)
        for e in range(slots):
            rows_here = dense[e * SLOT : e * SLOT + fun_dev]
            gram_refs[e][...] = skewed(moved(rows_here, reading - 1 - e * fun_dev), -1)[:, : 2 * reading]


def sum_kernel(reading, *refs):
    gram_ref, mixing_ref = refs[-2:]
    value = refs[0][...]
    for ref in refs[1:-2]:
        value = value + ref[...]
    gram_ref[...] = value
    diagonal = jnp.where(lax.broadcasted_iota(jnp.int32, value.shape, 1) == reading - 1, 1.5, 0.0)
    row = diagonal - 0.5 * value
    spare = jnp.zeros((mixing_ref.shape[0] - row.shape[0], row.shape[1]), jnp.float32)
    mixing_ref[...] = jnp.concatenate([row, spare], axis=0).astype(jnp.bfloat16)


def mix_kernel(plan, cut_ref, active_ref, place_ref, window_ref, *refs):
    fun_dev, reading = plan
    slots = 2 * REACH + 1
    bands = refs[:slots]
    outs = refs[slots : 2 * slots]
    at_boxes = refs[2 * slots : 3 * slots]
    mixing, mixed = refs[3 * slots :]
    step, steps = pl.program_id(0), pl.num_programs(0)
    width = cut_ref[REACH + 1] - cut_ref[REACH]
    wide = slots * SLOT

    @pl.when(step == 0)
    def _():
        for out, at_box in zip(outs, at_boxes):
            out[...] = jnp.zeros_like(out)
            at_box[...] = jnp.zeros_like(at_box)
        lanes = band_lanes(fun_dev, reading)
        parts = []
        for e in range(slots):
            band = bands[e][...].astype(jnp.float32)
            band = jnp.concatenate([band, jnp.zeros((SLOT, lanes - 2 * reading), jnp.float32)], axis=1)
            parts.append(moved(skewed(band, 1), e * fun_dev - (reading - 1)))
        dense = jnp.concatenate(parts, axis=0).astype(jnp.bfloat16)
        keep = one_hot(
            function_of((lanes, wide), 1, fun_dev) == lax.broadcasted_iota(jnp.int32, (lanes, wide), 0)
        )
        mixing[...] = times(dense, keep).astype(jnp.bfloat16)

    @pl.when(step * STEP < width)
    def _():
        for b in range(STEP):
            mixed[b] = times(mixing[...], window_ref[b]).astype(jnp.bfloat16)
        shape = (STEP * SLOT, at_boxes[0].shape[1])
        along = lax.broadcasted_iota(jnp.int32, shape, 0)
        box = lax.shift_right_logical(along, SLOT.bit_length() - 1) + step * STEP
        col = lax.broadcasted_iota(jnp.int32, shape, 1)
        boxes_of = one_hot((col == box) | (col == box + SLOT))
        for e in range(slots):
            @pl.when(active_ref[e * steps + step] > 0)
            def _():
                pick = one_hot(iota((outs[e].shape[0], STEP * SLOT), 0) == place_ref[e : e + 1, :])
                part = mixed[:, e * SLOT : (e + 1) * SLOT, :].reshape(STEP * SLOT, mixed.shape[-1])
                outs[e][...] += times(pick, part).astype(jnp.bfloat16)
                at_boxes[e][...] += times(pick, boxes_of).astype(jnp.bfloat16)


def filter_kernel(region_ref, kinetic_ref, *refs):
    count = len(refs) // 3
    for here_ref, at_box_ref, out_ref in zip(refs[:count], refs[count : 2 * count], refs[2 * count :]):
        here = here_ref[...]
        local = times(at_box_ref[...], region_ref[...])
        applied = times(here, kinetic_ref[...])
        out_ref[...] = (applied + local * here.astype(jnp.float32)).astype(jnp.bfloat16)


def home_kernel(groups, home_ref, *refs):
    sources, out_ref = refs[:-1], refs[-1]
    count = out_ref.shape[0]
    shape = (count, home_ref.shape[1])
    at = iota(shape, 0) + (pl.program_id(0) * count).astype(jnp.float32)
    row = jnp.sum(jnp.where(iota(shape, 1) == at, home_ref[...], 0.0), axis=1, keepdims=True)
    value, base = None, 0
    for group in groups:
        parts = [sources[e][...] for e in group]
        held = parts[0] if len(parts) == 1 else jnp.concatenate(parts, axis=0)
        pick = one_hot(iota((count, held.shape[0]), 1) == row - float(base))
        base += held.shape[0]
        term = times(pick, held)
        value = term if value is None else value + term
    out_ref[...] = value.astype(jnp.bfloat16)


def whole(shape):
    return pl.BlockSpec(shape, lambda g: (0,) * len(shape))


def on_device(coeffs, centers, kinetic, potential):
    fun_dev, support, points = coeffs.shape
    devices = lax.axis_size(AXES)
    me = lax.axis_index(AXES).astype(jnp.int32).reshape(1)
    box_dev = fun_dev // 2
    volume = 1.0 / (support * points)
    reading = 4 * support
    slots = 2 * REACH + 1
    offsets = list(range(-REACH, REACH + 1))
    order = [REACH, -REACH] + [sign * k for k in range(REACH - 1, 0, -1) for sign in (1, -1)]
    rows, low_cut, high_cut, boxes, blocks = bounds(fun_dev, support)
    assert blocks <= REACH + 1 and support & (support - 1) == 0
    back = tuple(rounded_up(r, 16) for r in rows)
    rows_of = {k: back[k + REACH] for k in offsets}
    flat = coeffs.reshape(fun_dev * support, points)
    halo = REACH + -(-(reading + 8) // fun_dev)
    count = rounded_up((2 * halo + 2) * fun_dev, 128)
    half = rounded_up(box_dev, 16)
    bf16, f32 = jnp.bfloat16, jnp.float32
    smem = pl.BlockSpec(memory_space=pltpu.SMEM)
    vmem = pl.BlockSpec(memory_space=pltpu.VMEM)
    limit = pltpu.CompilerParams(vmem_limit_bytes=52 * 2**20)

    sent_rows = [rounded_up(rows[k + REACH] + (2 * box_dev if k < 0 else 0), 16) for k in offsets if k]
    *packed, near, cut, home_row, own_region = pl.pallas_call(
        functools.partial(pack_kernel, (fun_dev, support, devices, halo, rows, back, low_cut, high_cut)),
        out_shape=tuple(jax.ShapeDtypeStruct((r, points), bf16) for r in sent_rows)
        + (
            jax.ShapeDtypeStruct((count, 128), f32),
            jax.ShapeDtypeStruct((slots + 1,), jnp.int32),
            jax.ShapeDtypeStruct((1, fun_dev * support), f32),
            jax.ShapeDtypeStruct((2 * half, points), bf16),
        ),
        in_specs=[smem] + [vmem] * 3,
        out_specs=tuple(vmem for _ in range(slots)) + (smem,)
        + tuple(vmem for _ in range(2)),
        compiler_params=limit,
        name="pack",
    )(me, centers.reshape(1, -1), flat, jnp.pad(potential, ((0, half - box_dev), (0, 0))))
    packed = dict(zip([k for k in offsets if k], packed))
    arrived = sent_in_order(packed, order, 1)

    columns, places, active = pl.pallas_call(
        functools.partial(table_kernel, (fun_dev, support, halo, boxes)),
        out_shape=(
            jax.ShapeDtypeStruct((slots * SLOT, 128), f32),
            jax.ShapeDtypeStruct((8, boxes * SLOT), f32),
            jax.ShapeDtypeStruct((slots * (boxes // STEP),), jnp.int32),
        ),
        in_specs=[smem, vmem],
        out_specs=(vmem, vmem, smem),
        compiler_params=limit,
        name="tables",
    )(cut, near)

    wide = slots * SLOT
    sources = [flat if e == REACH else arrived[REACH - e] for e in range(slots)]
    read_rows = [flat.shape[0] if e == REACH else rows_of[REACH - e] for e in range(slots)]
    exact_rows = [rows[2 * REACH - e] for e in range(slots)]
    block = pl.BlockSpec((STEP, wide, points), lambda g: (g, 0, 0))
    band = (fun_dev, 2 * reading)
    pieces, region, *grams = pl.pallas_call(
        functools.partial(unpack_kernel, (fun_dev, box_dev, reading, volume, exact_rows, read_rows, blocks)),
        grid=(boxes // STEP,),
        out_shape=(
            jax.ShapeDtypeStruct((boxes, wide, points), bf16),
            jax.ShapeDtypeStruct((128, points), bf16),
        )
        + tuple(jax.ShapeDtypeStruct(band, f32) for _ in range(slots)),
        in_specs=[smem, smem, whole(columns.shape), whole(own_region.shape)] + [whole(s.shape) for s in sources],
        out_specs=(block, whole((128, points))) + tuple(whole(band) for _ in range(slots)),
        scratch_shapes=[pltpu.VMEM((wide, wide), f32)],
        compiler_params=limit,
        name="unpack",
    )(cut, active, columns, own_region, *sources)

    summed = sent_in_order({k: grams[REACH + k] for k in order}, order, 1)
    gram_band, mixing_rows = pl.pallas_call(
        functools.partial(sum_kernel, reading),
        out_shape=(jax.ShapeDtypeStruct(band, f32), jax.ShapeDtypeStruct((SLOT, 2 * reading), bf16)),
        in_specs=[vmem] * slots,
        out_specs=(vmem, vmem),
        compiler_params=limit,
        name="sum",
    )(grams[REACH], *[summed[k] for k in order])
    mixing_of = sent_in_order({k: mixing_rows for k in order}, order, 1)
    mixing_of[0] = mixing_rows

    out_rows = [rows_of[REACH - e] for e in range(slots)]
    shapes = [(r, points) for r in out_rows] + [(r, 128) for r in out_rows]
    mixed = pl.pallas_call(
        functools.partial(mix_kernel, (fun_dev, reading)),
        grid=(boxes // STEP,),
        out_shape=tuple(jax.ShapeDtypeStruct(shape, bf16) for shape in shapes),
        in_specs=[smem, smem, pl.BlockSpec((8, STEP * SLOT), lambda g: (0, g)), block]
        + [whole((SLOT, 2 * reading))] * slots,
        out_specs=tuple(whole(shape) for shape in shapes),
        scratch_shapes=[pltpu.VMEM((wide, wide), bf16), pltpu.VMEM((STEP, wide, points), bf16)],
        compiler_params=limit,
        name="mix",
    )(cut, active, places, pieces, *[mixing_of[REACH - e] for e in range(slots)])

    filtered_rows = {}
    for group in [order[:3]] + [order[3:5], order[5:], [0]]:
        at = [REACH - k for k in group]
        got = pl.pallas_call(
            filter_kernel,
            out_shape=tuple(jax.ShapeDtypeStruct((out_rows[e], points), bf16) for e in at),
            in_specs=[vmem] * (2 + 2 * len(at)),
            out_specs=tuple(vmem for _ in at),
            compiler_params=limit,
            name="filter",
        )(region, kinetic, *[mixed[e] for e in at], *[mixed[slots + e] for e in at])
        filtered_rows.update(zip(group, got))
    returned = sent_in_order({k: filtered_rows[k] for k in order}, order, -1)
    returned[0] = filtered_rows[0]

    groups, held = [], 257
    for e, k in enumerate(offsets):
        if held + rows_of[k] <= 256:
            groups[-1].append(e)
            held += rows_of[k]
        else:
            groups.append([e])
            held = rows_of[k]
    filtered = pl.pallas_call(
        functools.partial(home_kernel, groups),
        grid=(fun_dev * support // 256,),
        out_shape=jax.ShapeDtypeStruct((fun_dev * support, points), bf16),
        in_specs=[whole(home_row.shape)] + [whole((rows_of[k], points)) for k in offsets],
        out_specs=pl.BlockSpec((256, points), lambda g: (g, 0)),
        compiler_params=limit,
        name="home",
    )(home_row, *[returned[k] for k in offsets])
    return (filtered.reshape(coeffs.shape), gram_band)


def solution(mesh):
    placed = (P(AXES, None, None), P(), P(), P(AXES, None))
    return jax.shard_map(
        on_device,
        mesh=mesh,
        in_specs=placed,
        out_specs=(P(AXES, None, None), P(AXES, None)),
        check_vma=False,
    )
```

```python
import functools
import itertools

import jax
import jax.numpy as jnp
import numpy as np
from jax import lax
from jax.experimental import pallas as pl
from jax.experimental.pallas import tpu as pltpu
from jax.sharding import PartitionSpec as P

AXES = ("func", "box")
REACH = 3
SLOT = 32
STEP = 8


def passed_along(value, steps):
    count = lax.axis_size(AXES)
    pairs = [(source, (source + steps) % count) for source in range(count)]
    return lax.ppermute(value, AXES, pairs)


def sent(values, keys, sign):
    return {k: passed_along(values[k], sign * k) for k in keys}


def after(values, keys, there):
    held, there = lax.optimization_barrier(({k: values[k] for k in keys}, there))
    return held, there


def rounded_up(value, multiple):
    return -(-int(value) // multiple) * multiple


@functools.lru_cache(maxsize=None)
def bounds(fun_dev, support):
    box_dev = fun_dev // 2
    orders = [
        order
        for order in sorted(set(itertools.permutations((1, 1, 2, 4))))
        if np.abs(np.cumsum(np.array(order) - 2)).max() <= 1
    ]
    box_all, fun_all = 12 * support, 24 * support
    assert fun_all % fun_dev == 0
    devices = fun_all // fun_dev
    rows = np.zeros(2 * REACH + 1, np.int64)
    low, high, boxes, end = 10**6, -(10**6), 0, 0
    for picks in itertools.product(orders, repeat=3):
        density = np.repeat(np.concatenate(picks), support)
        centers = np.repeat(np.arange(box_all), density)
        load = sum(np.roll(density, t) for t in range(support))
        below = np.concatenate([[0], np.cumsum(np.tile(load, 3))])
        over = np.clip(np.arange(box_all)[:, None] + support - box_all, 0, None)
        carried = int((over[:, 0] * density).sum())
        below = below - carried
        twice = below[:-1] + below[1:]
        cut = np.array([
            np.searchsorted(twice, 2 * support * fun_dev * (devices + d), side="right")
            for d in range(-REACH - 1, devices + REACH + 2)
        ]) - box_all
        first = REACH + 1
        width = np.diff(cut)
        place = cut - box_dev * (np.arange(len(cut)) - first)
        low, high = min(low, place.min()), max(high, place.max())
        boxes = max(boxes, width.max())
        end = max(end, (place[:-1] + width).max())
        box = centers[:, None] + np.arange(support)
        owner = np.searchsorted(cut, box, side="right") - 1 - first
        device = np.arange(fun_all)[:, None] // fun_dev
        offset = owner - device
        assert np.abs(offset).max() <= REACH
        count = np.bincount((device * (2 * REACH + 1) + offset + REACH).ravel(), minlength=devices * (2 * REACH + 1))
        rows = np.maximum(rows, count.reshape(devices, -1).max(0))
    return (
        tuple(int(r) for r in rows),
        int(low),
        int(high),
        rounded_up(boxes, STEP),
        -(-int(end) // box_dev),
    )


def iota(shape, dim):
    return lax.broadcasted_iota(jnp.int32, shape, dim).astype(jnp.float32)


def one_hot(mask):
    return jnp.where(mask, 1.0, 0.0).astype(jnp.bfloat16)


def spread_over(column, to):
    return jnp.sum(jnp.where(iota((column.shape[0], to.shape[1]), 0) == to, column, 0.0), axis=0, keepdims=True)


def times(a, b, dims=((1,), (0,)), precision=None):
    return lax.dot_general(
        a, b, (dims, ((), ())), precision=precision, preferred_element_type=jnp.float32
    )


def pack_kernel(plan, me_ref, centers_ref, flat_ref, potential_ref, *refs):
    fun_dev, support, devices, halo, rows, back, low_cut, high_cut, now = plan
    outs = dict(zip(now, refs[: len(now)]))
    near_ref, cut_ref, row_ref, home_ref, own_ref = refs[len(now) :]
    me = me_ref[0]
    box_dev = fun_dev // 2
    fun_all, box_all = fun_dev * devices, box_dev * devices
    count = near_ref.shape[0]

    start = me * fun_dev - halo * fun_dev
    start = jnp.where(start < 0, start + fun_all, start).astype(jnp.float32)
    at = start + iota((count, 1), 0)
    at = jnp.where(at >= fun_all, at - fun_all, at)
    near = jnp.sum(
        jnp.where(iota((count, fun_all), 1) == at, centers_ref[...].astype(jnp.float32), 0.0), axis=1, keepdims=True
    )
    near = near - (me * box_dev).astype(jnp.float32)
    near = jnp.where(near < -(box_all // 2), near + box_all, near)
    near = jnp.where(near >= box_all // 2, near - box_all, near)
    near_row = spread_over(near, iota((1, count), 1))
    near_ref[...] = jnp.broadcast_to(near, near_ref.shape)

    tries = high_cut - low_cut + 1
    trial = iota((rounded_up(tries, 8), 1), 0)
    cuts = []
    for k in range(-REACH, REACH + 2):
        gap = trial + float(low_cut + k * box_dev) - near_row
        twice = jnp.sum(
            jnp.clip(gap, 0.0, support) + jnp.clip(gap + 1.0, 0.0, support), axis=1, keepdims=True
        )
        goal = float(2 * support * fun_dev * (halo + k))
        passed = jnp.where((twice <= goal) & (trial < tries), 1.0, 0.0)
        cut = jnp.sum(passed) + float(low_cut + k * box_dev)
        cuts.append(cut)
        cut_ref[k + REACH] = cut.astype(jnp.int32)

    potential = potential_ref[...]
    high = potential.astype(jnp.bfloat16)
    low = (potential - high.astype(jnp.float32)).astype(jnp.bfloat16)
    shape = (own_ref.shape[0], box_dev)
    at_high = iota(shape, 0) == iota(shape, 1)
    at_low = iota(shape, 0) - float(shape[0] // 2) == iota(shape, 1)
    own_ref[...] = (times(one_hot(at_high), high) + times(one_hot(at_low), low)).astype(jnp.bfloat16)

    mine = near[halo * fun_dev : (halo + 1) * fun_dev]
    pieces = fun_dev * support
    piece = lax.broadcasted_iota(jnp.int32, (1, pieces), 1)
    of_fun = lax.shift_right_logical(piece, support.bit_length() - 1).astype(jnp.float32)
    step = piece.astype(jnp.float32) - of_fun * support
    mine_row = spread_over(mine, of_fun)
    earlier = iota((fun_dev, pieces), 0) < of_fun
    home, base = jnp.zeros((1, pieces), jnp.float32), 0
    for k in range(-REACH, REACH + 1):
        first, end = cuts[k + REACH], cuts[k + REACH + 1]
        leave = jnp.clip(end - mine, 0.0, support) - jnp.clip(first - mine, 0.0, support)
        leave_at = jnp.sum(jnp.where(earlier, leave, 0.0), axis=0, keepdims=True)
        low_edge = jnp.clip(first - mine_row, 0.0, support)
        goes = (step >= low_edge) & (step < jnp.clip(end - mine_row, 0.0, support))
        row = leave_at + step - low_edge
        home = home + jnp.where(goes, row + float(base), 0.0)
        base += back[k + REACH]
        row_ref[k + REACH : k + REACH + 1] = jnp.where(goes, row, -1.0)
    row_ref[2 * REACH + 1 :] = jnp.full((row_ref.shape[0] - 2 * REACH - 1, pieces), -1.0, jnp.float32)
    home_ref[...] = home
    packed_rows(rows, box_dev, row_ref, flat_ref, own_ref, outs)


def packed_rows(rows, box_dev, row_ref, flat_ref, own_ref, outs):
    for k, out_ref in outs.items():
        sent = out_ref.shape[0]
        row = row_ref[k + REACH : k + REACH + 1]
        value = times(one_hot(iota((sent, row.shape[1]), 0) == row), flat_ref[...])
        if k < 0:
            shape = (sent, own_ref.shape[0])
            part = iota(shape, 0) - float(rows[k + REACH])
            from_col = jnp.where(part < box_dev, part, part - box_dev + float(shape[1] // 2))
            inside = (part >= 0) & (part < 2 * box_dev)
            value = value + times(one_hot(inside & (iota(shape, 1) == from_col)), own_ref[...])
        out_ref[...] = value.astype(jnp.bfloat16)


def pack_rest_kernel(plan, row_ref, flat_ref, own_ref, *refs):
    rows, box_dev, now = plan
    packed_rows(rows, box_dev, row_ref, flat_ref, own_ref, dict(zip(now, refs)))


def picked(start, low, high, first, rows):
    lane = iota((SLOT, rows), 1)
    picks = []
    for b in range(STEP):
        box = first + float(b)
        row = jnp.where((box >= low) & (box < high), start + box, -1.0)
        picks.append(one_hot(lane == row))
    return jnp.concatenate(picks, axis=0)


def table_kernel(plan, cut_ref, near_ref, flat_ref, column_ref, place_ref, active_ref, local_ref):
    fun_dev, support, halo, boxes = plan
    slots = 2 * REACH + 1
    first = cut_ref[REACH].astype(jnp.float32)
    end = cut_ref[REACH + 1].astype(jnp.float32)
    lane = iota((SLOT, 128), 1)
    along = lax.broadcasted_iota(jnp.int32, (1, boxes * SLOT), 1)
    box = lax.shift_right_logical(along, SLOT.bit_length() - 1).astype(jnp.float32)
    of_fun = along.astype(jnp.float32) - box * SLOT
    levels = [1] * (boxes // STEP)
    for e in range(slots):
        at = (halo - REACH + e) * fun_dev
        others = near_ref[at : at + fun_dev, 0:1]
        edge_low = jnp.clip(first - others, 0.0, support)
        edge_high = jnp.clip(end - others, 0.0, support)
        come = edge_high - edge_low
        come_row = spread_over(come, lane[:1])
        come_at = jnp.sum(
            jnp.where(lane[:fun_dev] < iota((fun_dev, 128), 0), come_row, 0.0), axis=1, keepdims=True
        )
        box_low = edge_low + others - first
        box_high = edge_high + others - first
        packed = come_at - box_low
        spare = jnp.zeros((SLOT - fun_dev, 1), jnp.float32)
        if e == REACH:
            own_start = iota((fun_dev, 1), 0) * support + first - others
            own_start = jnp.concatenate([own_start, spare], axis=0)
        packed, box_low, box_high = (
            jnp.concatenate([column, spare], axis=0) for column in (packed, box_low, box_high)
        )
        if e == REACH:
            for g in range(boxes // STEP):
                pick = picked(own_start, box_low, box_high, float(g * STEP), flat_ref.shape[0])
                local_ref[g * STEP : (g + 1) * STEP] = times(pick, flat_ref[...]).astype(jnp.bfloat16).reshape(
                    STEP, SLOT, flat_ref.shape[1]
                )
        column_ref[e * SLOT : (e + 1) * SLOT, :] = jnp.where(
            lane == 0.0, packed, jnp.where(lane == 1.0, box_low, box_high)
        )
        lies = (box >= spread_over(box_low, of_fun)) & (box < spread_over(box_high, of_fun))
        place_ref[e : e + 1, :] = jnp.where(lies, spread_over(packed, of_fun) + box, -1.0)
        for g in range(boxes // STEP):
            here = (box >= g * STEP) & (box < (g + 1) * STEP) & lies
            used = jnp.sum(jnp.where(here, 1.0, 0.0)).astype(jnp.int32)
            active_ref[e * (boxes // STEP) + g] = used
            level = jnp.where(used > 0, max(1, abs(e - REACH)), 1)
            levels[g] = jnp.maximum(levels[g], level)
    for g in range(boxes // STEP):
        active_ref[slots * (boxes // STEP) + g] = levels[g]
    place_ref[slots:, :] = jnp.full((place_ref.shape[0] - slots, boxes * SLOT), -1.0, jnp.float32)


def function_of(shape, dim, fun_dev):
    row = lax.broadcasted_iota(jnp.int32, shape, dim)
    slot = lax.shift_right_logical(row, SLOT.bit_length() - 1)
    in_slot = row - slot * SLOT
    return jnp.where(in_slot < fun_dev, slot * fun_dev + in_slot, -1)


def moved(value, shift):
    return pltpu.roll(value, shift % value.shape[1], 1)


def skewed(value, sign):
    row = lax.broadcasted_iota(jnp.int32, value.shape, 0)
    bit = 1
    while bit < value.shape[0]:
        value = jnp.where((row & bit) != 0, moved(value, sign * bit), value)
        bit *= 2
    return value


def band_lanes(fun_dev, reading):
    window = (2 * REACH + 1) * fun_dev
    return rounded_up(window + reading + fun_dev + max(0, window - reading), 128)


def level_rows(level):
    return (REACH - level) * SLOT, (REACH + level + 1) * SLOT


def unpack_kernel(plan, cut_ref, active_ref, column_ref, own_ref, local_ref, *refs):
    fun_dev, box_dev, reading, volume, rows, back, blocks = plan
    slots = 2 * REACH + 1
    sources = refs[:REACH] + (None,) + refs[REACH : slots - 1]
    window_ref, region_ref = refs[slots - 1 : slots + 1]
    gram_refs = refs[slots + 1 : 2 * slots + 1]
    dense = refs[2 * slots + 1]
    totals = refs[2 * slots + 2 :]
    step, steps = pl.program_id(0), pl.num_programs(0)
    first = step * STEP
    width = cut_ref[REACH + 1] - cut_ref[REACH]

    @pl.when(step == 0)
    def _():
        for total in totals:
            total[...] = jnp.zeros_like(total)
        value = None
        for t in range(blocks):
            held = own_ref if t == 0 else sources[REACH + t]
            at = 0 if t == 0 else rows[REACH + t]
            from_row = at // 16 * 16
            held = held[from_row:]
            second = own_ref.shape[0] // 2 if t == 0 else box_dev
            shape = (region_ref.shape[0], held.shape[0])
            row, col = iota(shape, 0), iota(shape, 1)
            box = row - jnp.where(row >= SLOT, float(SLOT), 0.0) + cut_ref[REACH].astype(jnp.float32) - t * box_dev
            wanted = box + jnp.where(row >= SLOT, float(second), 0.0) + float(at - from_row)
            good = (box >= 0) & (box < box_dev) & (row < 2 * SLOT)
            term = times(one_hot(good & (col == wanted)), held)
            value = term if value is None else value + term
        region_ref[...] = value.astype(jnp.bfloat16)

    @pl.when(first < width)
    def _():
        level = active_ref[slots * steps + step]
        window_ref[:, REACH * SLOT : (REACH + 1) * SLOT, :] = local_ref[...]
        for e in range(slots):
            if e == REACH:
                continue
            used = active_ref[e * steps + step] > 0

            @pl.when(used)
            def _():
                start = column_ref[e * SLOT : (e + 1) * SLOT, 0:1]
                low = column_ref[e * SLOT : (e + 1) * SLOT, 1:2]
                high = column_ref[e * SLOT : (e + 1) * SLOT, 2:3]
                pick = picked(start, low, high, first.astype(jnp.float32), back[e])
                found = times(pick, sources[e][: back[e]])
                window_ref[:, e * SLOT : (e + 1) * SLOT, :] = found.astype(jnp.bfloat16).reshape(
                    STEP, SLOT, found.shape[-1]
                )

            @pl.when(jnp.logical_not(used) & (level >= abs(e - REACH)))
            def _():
                window_ref[:, e * SLOT : (e + 1) * SLOT, :] = jnp.zeros(
                    (STEP, SLOT, window_ref.shape[-1]), jnp.bfloat16
                )
        for part, total in enumerate(totals):
            @pl.when(level == part + 1)
            def _():
                low, high = level_rows(part + 1)
                value = total[...]
                for b in range(STEP):
                    here = window_ref[b, low:high]
                    value = value + times(here, here, ((1,), (1,)))
                total[...] = value

    @pl.when(step == steps - 1)
    def _():
        wide, lanes = dense.shape
        keep = jnp.where(
            function_of((wide, lanes), 0, fun_dev) == lax.broadcasted_iota(jnp.int32, (wide, lanes), 1), volume, 0.0
        )
        dense[...] = times(totals[-1][...], keep, precision=lax.Precision.HIGHEST)
        for part, total in enumerate(totals[:-1]):
            low, high = level_rows(part + 1)
            dense[low:high] += times(total[...], keep[low:high], precision=lax.Precision.HIGHEST)
        for e in range(slots):
            rows_here = dense[e * SLOT : e * SLOT + fun_dev]
            gram_refs[e][...] = skewed(moved(rows_here, reading - 1 - e * fun_dev), -1)[:, : 2 * reading]


def sum_kernel(reading, *refs):
    gram_ref, mixing_ref = refs[-2:]
    value = refs[0][...]
    for ref in refs[1:-2]:
        value = value + ref[...]
    gram_ref[...] = value
    diagonal = jnp.where(lax.broadcasted_iota(jnp.int32, value.shape, 1) == reading - 1, 1.5, 0.0)
    row = diagonal - 0.5 * value
    spare = jnp.zeros((mixing_ref.shape[0] - row.shape[0], row.shape[1]), jnp.float32)
    mixing_ref[...] = jnp.concatenate([row, spare], axis=0).astype(jnp.bfloat16)


def mix_kernel(plan, cut_ref, active_ref, place_ref, window_ref, *refs):
    fun_dev, reading, band_order = plan
    slots = 2 * REACH + 1
    bands = dict(zip(band_order, refs[:slots]))
    outs = refs[slots : 2 * slots]
    at_boxes = refs[2 * slots : 3 * slots]
    mixed = refs[3 * slots]
    mixings = refs[3 * slots + 1 :]
    step, steps = pl.program_id(0), pl.num_programs(0)
    width = cut_ref[REACH + 1] - cut_ref[REACH]
    @pl.when(step == 0)
    def _():
        for out, at_box in zip(outs, at_boxes):
            out[...] = jnp.zeros_like(out)
            at_box[...] = jnp.zeros_like(at_box)
        lanes = band_lanes(fun_dev, reading)
        parts = []
        for e in range(slots):
            band = bands[REACH - e][...].astype(jnp.float32)
            band = jnp.concatenate([band, jnp.zeros((SLOT, lanes - 2 * reading), jnp.float32)], axis=1)
            parts.append(moved(skewed(band, 1), e * fun_dev - (reading - 1)))
        dense = jnp.concatenate(parts, axis=0).astype(jnp.bfloat16)
        for part, mixing in enumerate(mixings):
            low, high = level_rows(part + 1)
            shape = (lanes, mixing.shape[1])
            column = function_of(shape, 1, fun_dev)
            column = jnp.where(column >= 0, column + low // SLOT * fun_dev, -1)
            keep = one_hot(column == lax.broadcasted_iota(jnp.int32, shape, 0))
            mixing[...] = times(dense[low:high], keep).astype(jnp.bfloat16)

    @pl.when(step * STEP < width)
    def _():
        level = active_ref[slots * steps + step]
        for part, mixing in enumerate(mixings):
            @pl.when(level == part + 1)
            def _():
                low, high = level_rows(part + 1)
                for b in range(STEP):
                    mixed[b, low:high] = times(mixing[...], window_ref[b, low:high]).astype(jnp.bfloat16)
        shape = (STEP * SLOT, at_boxes[0].shape[1])
        along = lax.broadcasted_iota(jnp.int32, shape, 0)
        box = lax.shift_right_logical(along, SLOT.bit_length() - 1) + step * STEP
        col = lax.broadcasted_iota(jnp.int32, shape, 1)
        boxes_of = one_hot((col == box) | (col == box + SLOT))
        for e in range(slots):
            @pl.when(active_ref[e * steps + step] > 0)
            def _():
                pick = one_hot(iota((outs[e].shape[0], STEP * SLOT), 0) == place_ref[e : e + 1, :])
                part = mixed[:, e * SLOT : (e + 1) * SLOT, :].reshape(STEP * SLOT, mixed.shape[-1])
                outs[e][...] += times(pick, part).astype(jnp.bfloat16)
                at_boxes[e][...] += times(pick, boxes_of).astype(jnp.bfloat16)


def home_kernel(groups, home_ref, *refs):
    sources, out_ref = refs[:-1], refs[-1]
    count = out_ref.shape[0]
    shape = (count, home_ref.shape[1])
    at = iota(shape, 0) + (pl.program_id(0) * count).astype(jnp.float32)
    row = jnp.sum(jnp.where(iota(shape, 1) == at, home_ref[...], 0.0), axis=1, keepdims=True)
    value, base = None, 0
    for group in groups:
        parts = [sources[e][...] for e in group]
        held = parts[0] if len(parts) == 1 else jnp.concatenate(parts, axis=0)
        pick = one_hot(iota((count, held.shape[0]), 1) == row - float(base))
        base += held.shape[0]
        term = times(pick, held)
        value = term if value is None else value + term
    out_ref[...] = value.astype(jnp.bfloat16)


def whole(shape):
    return pl.BlockSpec(shape, lambda g: (0,) * len(shape))


def on_device(coeffs, centers, kinetic, potential):
    fun_dev, support, points = coeffs.shape
    devices = lax.axis_size(AXES)
    me = lax.axis_index(AXES).astype(jnp.int32).reshape(1)
    box_dev = fun_dev // 2
    volume = 1.0 / (support * points)
    reading = 4 * support
    slots = 2 * REACH + 1
    offsets = list(range(-REACH, REACH + 1))
    far = [REACH, -REACH]
    rest = [sign * k for k in range(1, REACH) for sign in (1, -1)]
    one_way = list(range(REACH, 0, -1)) + list(range(-REACH, 0))
    rows, low_cut, high_cut, boxes, blocks = bounds(fun_dev, support)
    assert blocks <= REACH + 1 and support & (support - 1) == 0
    back = tuple(rounded_up(r, 16) for r in rows)
    rows_of = {k: back[k + REACH] for k in offsets}
    flat = coeffs.reshape(fun_dev * support, points)
    halo = REACH + -(-(reading + 8) // fun_dev)
    count = rounded_up((2 * halo + 2) * fun_dev, 128)
    half = rounded_up(box_dev, 16)
    bf16, f32 = jnp.bfloat16, jnp.float32
    smem = pl.BlockSpec(memory_space=pltpu.SMEM)
    vmem = pl.BlockSpec(memory_space=pltpu.VMEM)
    limit = pltpu.CompilerParams(vmem_limit_bytes=52 * 2**20)

    sent_rows = {k: rounded_up(rows[k + REACH] + (2 * box_dev if k < 0 else 0), 16) for k in offsets if k}
    *packed_far, near, cut, row_out, home_row, own_region = pl.pallas_call(
        functools.partial(pack_kernel, (fun_dev, support, devices, halo, rows, back, low_cut, high_cut, far)),
        out_shape=tuple(jax.ShapeDtypeStruct((sent_rows[k], points), bf16) for k in far)
        + (
            jax.ShapeDtypeStruct((count, 128), f32),
            jax.ShapeDtypeStruct((slots + 1,), jnp.int32),
            jax.ShapeDtypeStruct((8, fun_dev * support), f32),
            jax.ShapeDtypeStruct((1, fun_dev * support), f32),
            jax.ShapeDtypeStruct((2 * half, points), bf16),
        ),
        in_specs=[smem] + [vmem] * 3,
        out_specs=(vmem,) * 3 + (smem,) + (vmem,) * 3,
        compiler_params=limit,
        name="pack_far",
    )(me, centers.reshape(1, -1), flat, potential)
    arrived = sent(dict(zip(far, packed_far)), far, 1)
    packed = dict(zip(rest, pl.pallas_call(
        functools.partial(pack_rest_kernel, (rows, box_dev, rest)),
        out_shape=tuple(jax.ShapeDtypeStruct((sent_rows[k], points), bf16) for k in rest),
        in_specs=[vmem] * 3,
        out_specs=(vmem,) * len(rest),
        compiler_params=limit,
        name="pack_rest",
    )(row_out, flat, own_region)))
    late, arrived = after(packed, rest[2:], arrived)
    arrived.update(sent(packed, rest[:2], 1))
    arrived.update(sent(late, rest[2:], 1))

    columns, places, active, local = pl.pallas_call(
        functools.partial(table_kernel, (fun_dev, support, halo, boxes)),
        out_shape=(
            jax.ShapeDtypeStruct((slots * SLOT, 128), f32),
            jax.ShapeDtypeStruct((8, boxes * SLOT), f32),
            jax.ShapeDtypeStruct(((slots + 1) * (boxes // STEP),), jnp.int32),
            jax.ShapeDtypeStruct((boxes, SLOT, points), bf16),
        ),
        in_specs=[smem, vmem, vmem],
        out_specs=(vmem, vmem, smem, vmem),
        compiler_params=limit,
        name="tables",
    )(cut, near, flat)

    wide = slots * SLOT
    sources = [arrived[REACH - e] for e in range(slots) if e != REACH]
    read_rows = [rows_of[REACH - e] for e in range(slots)]
    level_sizes = [level_rows(part + 1)[1] - level_rows(part + 1)[0] for part in range(REACH)]
    exact_rows = [rows[2 * REACH - e] for e in range(slots)]
    block = pl.BlockSpec((STEP, wide, points), lambda g: (g, 0, 0))
    band = (fun_dev, 2 * reading)
    pieces, region, *grams = pl.pallas_call(
        functools.partial(unpack_kernel, (fun_dev, box_dev, reading, volume, exact_rows, read_rows, blocks)),
        grid=(boxes // STEP,),
        out_shape=(
            jax.ShapeDtypeStruct((boxes, wide, points), bf16),
            jax.ShapeDtypeStruct((128, points), bf16),
        )
        + tuple(jax.ShapeDtypeStruct(band, f32) for _ in range(slots)),
        in_specs=[smem, smem, whole(columns.shape), whole(own_region.shape), pl.BlockSpec((STEP, SLOT, points), lambda g: (g, 0, 0))]
        + [whole(s.shape) for s in sources],
        out_specs=(block, whole((128, points))) + tuple(whole(band) for _ in range(slots)),
        scratch_shapes=[pltpu.VMEM((wide, band_lanes(fun_dev, reading)), f32)]
        + [pltpu.VMEM((size, size), f32) for size in level_sizes],
        compiler_params=limit,
        name="unpack",
    )(cut, active, columns, own_region, local, *sources)

    summed = sent({k: grams[REACH + k] for k in one_way}, one_way, 1)
    gram_band, mixing_rows = pl.pallas_call(
        functools.partial(sum_kernel, reading),
        out_shape=(jax.ShapeDtypeStruct(band, f32), jax.ShapeDtypeStruct((SLOT, 2 * reading), bf16)),
        in_specs=[vmem] * slots,
        out_specs=(vmem, vmem),
        compiler_params=limit,
        name="sum",
    )(grams[REACH], *[summed[k] for k in one_way])
    mixing_of = sent({k: mixing_rows for k in one_way}, one_way, 1)
    mixing_of[0] = mixing_rows
    band_order = one_way + [0]

    out_rows = [rows_of[REACH - e] for e in range(slots)]
    shapes = [(r, points) for r in out_rows] + [(r, 128) for r in out_rows]
    mixed = pl.pallas_call(
        functools.partial(mix_kernel, (fun_dev, reading, band_order)),
        grid=(boxes // STEP,),
        out_shape=tuple(jax.ShapeDtypeStruct(shape, bf16) for shape in shapes),
        in_specs=[smem, smem, pl.BlockSpec((8, STEP * SLOT), lambda g: (0, g)), block]
        + [whole((SLOT, 2 * reading))] * slots,
        out_specs=tuple(whole(shape) for shape in shapes),
        scratch_shapes=[pltpu.VMEM((STEP, wide, points), bf16)]
        + [pltpu.VMEM((size, size), bf16) for size in level_sizes],
        compiler_params=limit,
        name="mix",
    )(cut, active, places, pieces, *[mixing_of[k] for k in band_order])

    ready = {}
    for k in far + rest + [0]:
        here, at_box = mixed[REACH - k], mixed[slots + REACH - k]
        near_by = jnp.dot(at_box, region, preferred_element_type=f32)
        applied = jnp.dot(here, kinetic, preferred_element_type=f32)
        ready[k] = (applied + near_by * here.astype(f32)).astype(bf16)
    returned = sent(ready, far, -1)
    late, returned = after(ready, rest[2:], returned)
    returned.update(sent(ready, rest[:2], -1))
    returned.update(sent(late, rest[2:], -1))
    returned[0] = ready[0]

    groups, held = [], 257
    for e, k in enumerate(offsets):
        if held + rows_of[k] <= 256:
            groups[-1].append(e)
            held += rows_of[k]
        else:
            groups.append([e])
            held = rows_of[k]
    filtered = pl.pallas_call(
        functools.partial(home_kernel, groups),
        grid=(fun_dev * support // 256,),
        out_shape=jax.ShapeDtypeStruct((fun_dev * support, points), bf16),
        in_specs=[whole(home_row.shape)] + [whole((rows_of[k], points)) for k in offsets],
        out_specs=pl.BlockSpec((256, points), lambda g: (g, 0)),
        compiler_params=limit,
        name="home",
    )(home_row, *[returned[k] for k in offsets])
    return (filtered.reshape(coeffs.shape), gram_band)


def solution(mesh):
    placed = (P(AXES, None, None), P(), P(), P(AXES, None))
    return jax.shard_map(
        on_device,
        mesh=mesh,
        in_specs=placed,
        out_specs=(P(AXES, None, None), P(AXES, None)),
        check_vma=False,
    )
```

```python
import functools
import itertools

import jax
import jax.numpy as jnp
import numpy as np
from jax import lax
from jax.experimental import pallas as pl
from jax.experimental.pallas import tpu as pltpu
from jax.sharding import PartitionSpec as P

AXES = ("func", "box")
REACH = 3
SLOT = 32
STEP = 8


def passed_along(value, steps):
    count = lax.axis_size(AXES)
    pairs = [(source, (source + steps) % count) for source in range(count)]
    return lax.ppermute(value, AXES, pairs)


def sent(values, keys, sign):
    return {k: passed_along(values[k], sign * k) for k in keys}


def all_sent(values, now, last, sign):
    there = sent(values, now, sign)
    value, there[now[0]] = lax.optimization_barrier((values[last], there[now[0]]))
    there[last] = passed_along(value, sign * last)
    return there


def rounded_up(value, multiple):
    return -(-int(value) // multiple) * multiple


@functools.lru_cache(maxsize=None)
def bounds(fun_dev, support):
    box_dev = fun_dev // 2
    orders = [
        order
        for order in sorted(set(itertools.permutations((1, 1, 2, 4))))
        if np.abs(np.cumsum(np.array(order) - 2)).max() <= 1
    ]
    box_all, fun_all = 12 * support, 24 * support
    assert fun_all % fun_dev == 0
    devices = fun_all // fun_dev
    rows = np.zeros(2 * REACH + 1, np.int64)
    low, high, boxes, end = 10**6, -(10**6), 0, 0
    for picks in itertools.product(orders, repeat=3):
        density = np.repeat(np.concatenate(picks), support)
        centers = np.repeat(np.arange(box_all), density)
        load = sum(np.roll(density, t) for t in range(support))
        below = np.concatenate([[0], np.cumsum(np.tile(load, 3))])
        over = np.clip(np.arange(box_all)[:, None] + support - box_all, 0, None)
        carried = int((over[:, 0] * density).sum())
        below = below - carried
        twice = below[:-1] + below[1:]
        cut = np.array([
            np.searchsorted(twice, 2 * support * fun_dev * (devices + d), side="right")
            for d in range(-REACH - 1, devices + REACH + 2)
        ]) - box_all
        first = REACH + 1
        width = np.diff(cut)
        place = cut - box_dev * (np.arange(len(cut)) - first)
        low, high = min(low, place.min()), max(high, place.max())
        boxes = max(boxes, width.max())
        end = max(end, (place[:-1] + width).max())
        box = centers[:, None] + np.arange(support)
        owner = np.searchsorted(cut, box, side="right") - 1 - first
        device = np.arange(fun_all)[:, None] // fun_dev
        offset = owner - device
        assert np.abs(offset).max() <= REACH
        count = np.bincount((device * (2 * REACH + 1) + offset + REACH).ravel(), minlength=devices * (2 * REACH + 1))
        rows = np.maximum(rows, count.reshape(devices, -1).max(0))
    return (
        tuple(int(r) for r in rows),
        int(low),
        int(high),
        rounded_up(boxes, STEP),
        -(-int(end) // box_dev),
    )


def iota(shape, dim):
    return lax.broadcasted_iota(jnp.int32, shape, dim).astype(jnp.float32)


def one_hot(mask):
    return jnp.where(mask, 1.0, 0.0).astype(jnp.bfloat16)


def spread_over(column, to):
    return jnp.sum(jnp.where(iota((column.shape[0], to.shape[1]), 0) == to, column, 0.0), axis=0, keepdims=True)


def times(a, b, dims=((1,), (0,)), precision=None):
    return lax.dot_general(
        a, b, (dims, ((), ())), precision=precision, preferred_element_type=jnp.float32
    )


def pack_kernel(plan, me_ref, centers_ref, flat_ref, potential_ref, *refs):
    fun_dev, support, devices, halo, rows, back, low_cut, high_cut, now = plan
    outs = dict(zip(now, refs[: len(now)]))
    near_ref, cut_ref, home_ref, own_ref, row_ref = refs[len(now) :]
    me = me_ref[0]
    box_dev = fun_dev // 2
    fun_all, box_all = fun_dev * devices, box_dev * devices
    count = near_ref.shape[0]

    start = me * fun_dev - halo * fun_dev
    start = jnp.where(start < 0, start + fun_all, start).astype(jnp.float32)
    at = start + iota((count, 1), 0)
    at = jnp.where(at >= fun_all, at - fun_all, at)
    near = jnp.sum(
        jnp.where(iota((count, fun_all), 1) == at, centers_ref[...].astype(jnp.float32), 0.0), axis=1, keepdims=True
    )
    near = near - (me * box_dev).astype(jnp.float32)
    near = jnp.where(near < -(box_all // 2), near + box_all, near)
    near = jnp.where(near >= box_all // 2, near - box_all, near)
    near_row = spread_over(near, iota((1, count), 1))
    near_ref[...] = jnp.broadcast_to(near, near_ref.shape)

    tries = high_cut - low_cut + 1
    trial = iota((rounded_up(tries, 8), 1), 0)
    cuts = []
    for k in range(-REACH, REACH + 2):
        gap = trial + float(low_cut + k * box_dev) - near_row
        twice = jnp.sum(
            jnp.clip(gap, 0.0, support) + jnp.clip(gap + 1.0, 0.0, support), axis=1, keepdims=True
        )
        goal = float(2 * support * fun_dev * (halo + k))
        passed = jnp.where((twice <= goal) & (trial < tries), 1.0, 0.0)
        cut = jnp.sum(passed) + float(low_cut + k * box_dev)
        cuts.append(cut)
        cut_ref[k + REACH] = cut.astype(jnp.int32)

    potential = potential_ref[...]
    high = potential.astype(jnp.bfloat16)
    low = (potential - high.astype(jnp.float32)).astype(jnp.bfloat16)
    shape = (own_ref.shape[0], box_dev)
    at_high = iota(shape, 0) == iota(shape, 1)
    at_low = iota(shape, 0) - float(shape[0] // 2) == iota(shape, 1)
    own_ref[...] = (times(one_hot(at_high), high) + times(one_hot(at_low), low)).astype(jnp.bfloat16)

    mine = near[halo * fun_dev : (halo + 1) * fun_dev]
    pieces = fun_dev * support
    piece = lax.broadcasted_iota(jnp.int32, (1, pieces), 1)
    of_fun = lax.shift_right_logical(piece, support.bit_length() - 1).astype(jnp.float32)
    step = piece.astype(jnp.float32) - of_fun * support
    mine_row = spread_over(mine, of_fun)
    earlier = iota((fun_dev, pieces), 0) < of_fun
    home, base = jnp.zeros((1, pieces), jnp.float32), 0
    for k in range(-REACH, REACH + 1):
        first, end = cuts[k + REACH], cuts[k + REACH + 1]
        leave = jnp.clip(end - mine, 0.0, support) - jnp.clip(first - mine, 0.0, support)
        leave_at = jnp.sum(jnp.where(earlier, leave, 0.0), axis=0, keepdims=True)
        low_edge = jnp.clip(first - mine_row, 0.0, support)
        goes = (step >= low_edge) & (step < jnp.clip(end - mine_row, 0.0, support))
        row = leave_at + step - low_edge
        home = home + jnp.where(goes, row + float(base), 0.0)
        base += back[k + REACH]
        row_ref[k + REACH : k + REACH + 1] = jnp.where(goes, row, -1.0)
    row_ref[2 * REACH + 1 :] = jnp.full((row_ref.shape[0] - 2 * REACH - 1, pieces), -1.0, jnp.float32)
    home_ref[...] = home
    packed_rows(rows, box_dev, row_ref, flat_ref, own_ref, outs)


def packed_rows(rows, box_dev, row_ref, flat_ref, own_ref, outs):
    for k, out_ref in outs.items():
        sent = out_ref.shape[0]
        row = row_ref[k + REACH : k + REACH + 1]
        value = times(one_hot(iota((sent, row.shape[1]), 0) == row), flat_ref[...])
        if k < 0:
            shape = (sent, own_ref.shape[0])
            part = iota(shape, 0) - float(rows[k + REACH])
            from_col = jnp.where(part < box_dev, part, part - box_dev + float(shape[1] // 2))
            inside = (part >= 0) & (part < 2 * box_dev)
            value = value + times(one_hot(inside & (iota(shape, 1) == from_col)), own_ref[...])
        out_ref[...] = value.astype(jnp.bfloat16)


def picked(start, low, high, first, rows):
    lane = iota((SLOT, rows), 1)
    picks = []
    for b in range(STEP):
        box = first + float(b)
        row = jnp.where((box >= low) & (box < high), start + box, -1.0)
        picks.append(one_hot(lane == row))
    return jnp.concatenate(picks, axis=0)


def table_kernel(plan, cut_ref, near_ref, flat_ref, column_ref, place_ref, active_ref, local_ref):
    fun_dev, support, halo, boxes = plan
    slots = 2 * REACH + 1
    first = cut_ref[REACH].astype(jnp.float32)
    end = cut_ref[REACH + 1].astype(jnp.float32)
    lane = iota((SLOT, 128), 1)
    along = lax.broadcasted_iota(jnp.int32, (1, boxes * SLOT), 1)
    box = lax.shift_right_logical(along, SLOT.bit_length() - 1).astype(jnp.float32)
    of_fun = along.astype(jnp.float32) - box * SLOT
    levels = [1] * (boxes // STEP)
    for e in range(slots):
        at = (halo - REACH + e) * fun_dev
        others = near_ref[at : at + fun_dev, 0:1]
        edge_low = jnp.clip(first - others, 0.0, support)
        edge_high = jnp.clip(end - others, 0.0, support)
        come = edge_high - edge_low
        come_row = spread_over(come, lane[:1])
        come_at = jnp.sum(
            jnp.where(lane[:fun_dev] < iota((fun_dev, 128), 0), come_row, 0.0), axis=1, keepdims=True
        )
        box_low = edge_low + others - first
        box_high = edge_high + others - first
        packed = come_at - box_low
        spare = jnp.zeros((SLOT - fun_dev, 1), jnp.float32)
        if e == REACH:
            own_start = iota((fun_dev, 1), 0) * support + first - others
            own_start = jnp.concatenate([own_start, spare], axis=0)
        packed, box_low, box_high = (
            jnp.concatenate([column, spare], axis=0) for column in (packed, box_low, box_high)
        )
        if e == REACH:
            for g in range(boxes // STEP):
                pick = picked(own_start, box_low, box_high, float(g * STEP), flat_ref.shape[0])
                local_ref[g * STEP : (g + 1) * STEP] = times(pick, flat_ref[...]).astype(jnp.bfloat16).reshape(
                    STEP, SLOT, flat_ref.shape[1]
                )
        column_ref[e * SLOT : (e + 1) * SLOT, :] = jnp.where(
            lane == 0.0, packed, jnp.where(lane == 1.0, box_low, box_high)
        )
        lies = (box >= spread_over(box_low, of_fun)) & (box < spread_over(box_high, of_fun))
        place = jnp.where(lies, spread_over(packed, of_fun) + box, -1.0)
        for g in range(boxes // STEP):
            place_ref[g, e : e + 1, :] = place[:, g * STEP * SLOT : (g + 1) * STEP * SLOT]
            here = (box >= g * STEP) & (box < (g + 1) * STEP) & lies
            used = jnp.sum(jnp.where(here, 1.0, 0.0)).astype(jnp.int32)
            active_ref[e * (boxes // STEP) + g] = used
            level = jnp.where(used > 0, max(1, abs(e - REACH)), 1)
            levels[g] = jnp.maximum(levels[g], level)
    for g in range(boxes // STEP):
        active_ref[slots * (boxes // STEP) + g] = levels[g]
    spare = place_ref.shape[1] - slots
    place_ref[:, slots:, :] = jnp.full((boxes // STEP, spare, STEP * SLOT), -1.0, jnp.float32)


def function_of(shape, dim, fun_dev):
    row = lax.broadcasted_iota(jnp.int32, shape, dim)
    slot = lax.shift_right_logical(row, SLOT.bit_length() - 1)
    in_slot = row - slot * SLOT
    return jnp.where(in_slot < fun_dev, slot * fun_dev + in_slot, -1)


def moved(value, shift):
    return pltpu.roll(value, shift % value.shape[1], 1)


def skewed(value, sign):
    row = lax.broadcasted_iota(jnp.int32, value.shape, 0)
    bit = 1
    while bit < value.shape[0]:
        value = jnp.where((row & bit) != 0, moved(value, sign * bit), value)
        bit *= 2
    return value


def band_lanes(fun_dev, reading):
    window = (2 * REACH + 1) * fun_dev
    return rounded_up(window + reading + fun_dev + max(0, window - reading), 128)


def level_rows(level):
    return (REACH - level) * SLOT, (REACH + level + 1) * SLOT


def unpack_kernel(plan, cut_ref, active_ref, column_ref, own_ref, local_ref, *refs):
    fun_dev, box_dev, reading, volume, rows, back, blocks = plan
    slots = 2 * REACH + 1
    sources = refs[:REACH] + (None,) + refs[REACH : slots - 1]
    window_ref, region_ref = refs[slots - 1 : slots + 1]
    gram_refs = refs[slots + 1 : 2 * slots + 1]
    dense = refs[2 * slots + 1]
    totals = refs[2 * slots + 2 :]
    steps = window_ref.shape[0] // STEP
    width = cut_ref[REACH + 1] - cut_ref[REACH]

    for total in totals:
        total[...] = jnp.zeros_like(total)
    value = None
    for t in range(blocks):
        held = own_ref if t == 0 else sources[REACH + t]
        at = 0 if t == 0 else rows[REACH + t]
        from_row = at // 16 * 16
        held = held[from_row:]
        second = own_ref.shape[0] // 2 if t == 0 else box_dev
        shape = (region_ref.shape[0], held.shape[0])
        row, col = iota(shape, 0), iota(shape, 1)
        box = row - jnp.where(row >= SLOT, float(SLOT), 0.0) + cut_ref[REACH].astype(jnp.float32) - t * box_dev
        wanted = box + jnp.where(row >= SLOT, float(second), 0.0) + float(at - from_row)
        good = (box >= 0) & (box < box_dev) & (row < 2 * SLOT)
        term = times(one_hot(good & (col == wanted)), held)
        value = term if value is None else value + term
    region_ref[...] = value.astype(jnp.bfloat16)

    @pl.loop(0, lax.div(width + STEP - 1, STEP))
    def _(step):
        here_rows = pl.ds(step * STEP, STEP)
        level = active_ref[slots * steps + step]
        window_ref[here_rows, REACH * SLOT : (REACH + 1) * SLOT, :] = local_ref[here_rows]
        for e in range(slots):
            if e == REACH:
                continue
            used = active_ref[e * steps + step] > 0

            @pl.when(used)
            def _():
                start = column_ref[e * SLOT : (e + 1) * SLOT, 0:1]
                low = column_ref[e * SLOT : (e + 1) * SLOT, 1:2]
                high = column_ref[e * SLOT : (e + 1) * SLOT, 2:3]
                pick = picked(start, low, high, (step * STEP).astype(jnp.float32), back[e])
                found = times(pick, sources[e][: back[e]])
                window_ref[here_rows, e * SLOT : (e + 1) * SLOT, :] = found.astype(jnp.bfloat16).reshape(
                    STEP, SLOT, found.shape[-1]
                )

            @pl.when(jnp.logical_not(used) & (level >= abs(e - REACH)))
            def _():
                window_ref[here_rows, e * SLOT : (e + 1) * SLOT, :] = jnp.zeros(
                    (STEP, SLOT, window_ref.shape[-1]), jnp.bfloat16
                )
        for part, total in enumerate(totals):
            @pl.when(level == part + 1)
            def _():
                low, high = level_rows(part + 1)
                value = total[...]
                for b in range(STEP):
                    here = window_ref[step * STEP + b, low:high]
                    value = value + times(here, here, ((1,), (1,)))
                total[...] = value

    wide, lanes = dense.shape
    keep = jnp.where(
        function_of((wide, lanes), 0, fun_dev) == lax.broadcasted_iota(jnp.int32, (wide, lanes), 1), volume, 0.0
    )
    dense[...] = times(totals[-1][...], keep, precision=lax.Precision.HIGHEST)
    for part, total in enumerate(totals[:-1]):
        low, high = level_rows(part + 1)
        dense[low:high] += times(total[...], keep[low:high], precision=lax.Precision.HIGHEST)
    for e in range(slots):
        rows_here = dense[e * SLOT : e * SLOT + fun_dev]
        gram_refs[e][...] = skewed(moved(rows_here, reading - 1 - e * fun_dev), -1)[:, : 2 * reading]


def sum_kernel(reading, *refs):
    gram_ref, mixing_ref = refs[-2:]
    value = refs[0][...]
    for ref in refs[1:-2]:
        value = value + ref[...]
    gram_ref[...] = value
    diagonal = jnp.where(lax.broadcasted_iota(jnp.int32, value.shape, 1) == reading - 1, 1.5, 0.0)
    row = diagonal - 0.5 * value
    spare = jnp.zeros((mixing_ref.shape[0] - row.shape[0], row.shape[1]), jnp.float32)
    mixing_ref[...] = jnp.concatenate([row, spare], axis=0).astype(jnp.bfloat16)


def mix_kernel(plan, cut_ref, active_ref, place_ref, window_ref, *refs):
    fun_dev, reading, band_order = plan
    slots = 2 * REACH + 1
    bands = dict(zip(band_order, refs[:slots]))
    outs = refs[slots : 2 * slots]
    at_boxes = refs[2 * slots : 3 * slots]
    mixed = refs[3 * slots]
    mixings = refs[3 * slots + 1 :]
    steps = window_ref.shape[0] // STEP
    width = cut_ref[REACH + 1] - cut_ref[REACH]
    for out, at_box in zip(outs, at_boxes):
        out[...] = jnp.zeros_like(out)
        at_box[...] = jnp.zeros_like(at_box)
    lanes = band_lanes(fun_dev, reading)
    parts = []
    for e in range(slots):
        band = bands[REACH - e][...].astype(jnp.float32)
        band = jnp.concatenate([band, jnp.zeros((SLOT, lanes - 2 * reading), jnp.float32)], axis=1)
        parts.append(moved(skewed(band, 1), e * fun_dev - (reading - 1)))
    dense = jnp.concatenate(parts, axis=0).astype(jnp.bfloat16)
    for part, mixing in enumerate(mixings):
        low, high = level_rows(part + 1)
        shape = (lanes, mixing.shape[1])
        column = function_of(shape, 1, fun_dev)
        column = jnp.where(column >= 0, column + low // SLOT * fun_dev, -1)
        keep = one_hot(column == lax.broadcasted_iota(jnp.int32, shape, 0))
        mixing[...] = times(dense[low:high], keep).astype(jnp.bfloat16)

    @pl.loop(0, lax.div(width + STEP - 1, STEP))
    def _(step):
        level = active_ref[slots * steps + step]
        for part, mixing in enumerate(mixings):
            @pl.when(level == part + 1)
            def _():
                low, high = level_rows(part + 1)
                for b in range(STEP):
                    here = window_ref[step * STEP + b, low:high]
                    mixed[b, low:high] = times(mixing[...], here).astype(jnp.bfloat16)
        shape = (STEP * SLOT, at_boxes[0].shape[1])
        along = lax.broadcasted_iota(jnp.int32, shape, 0)
        box = lax.shift_right_logical(along, SLOT.bit_length() - 1) + step * STEP
        col = lax.broadcasted_iota(jnp.int32, shape, 1)
        boxes_of = one_hot((col == box) | (col == box + SLOT))
        for e in range(slots):
            @pl.when(active_ref[e * steps + step] > 0)
            def _():
                place = place_ref[step, e : e + 1, :]
                pick = one_hot(iota((outs[e].shape[0], STEP * SLOT), 0) == place)
                part = mixed[:, e * SLOT : (e + 1) * SLOT, :].reshape(STEP * SLOT, mixed.shape[-1])
                outs[e][...] += times(pick, part).astype(jnp.bfloat16)
                at_boxes[e][...] += times(pick, boxes_of).astype(jnp.bfloat16)


def home_rows(bases, home_ref, sources, at, count):
    shape = (count, home_ref.shape[1])
    here = iota(shape, 1) == iota(shape, 0) + float(at)
    row = jnp.sum(jnp.where(here, home_ref[...], 0.0), axis=1, keepdims=True)
    value = None
    for base, source in zip(bases, sources):
        pick = one_hot(iota((count, source.shape[0]), 1) == row - float(base))
        term = times(pick, source[...])
        value = term if value is None else value + term
    return value


def early_kernel(bases, home_ref, *refs):
    sources, out_ref = refs[:-1], refs[-1]
    count = 256
    for at in range(0, out_ref.shape[0], count):
        out_ref[at : at + count] = home_rows(bases, home_ref, sources, at, count).astype(jnp.bfloat16)


def home_kernel(bases, home_ref, early_ref, *refs):
    sources, out_ref, held, sems = refs[:-3], refs[-3], refs[-2], refs[-1]
    copies = []
    count = held.shape[1]
    for part in range(held.shape[0]):
        at = part * count
        value = home_rows(bases, home_ref, sources, at, count) + early_ref[at : at + count].astype(jnp.float32)
        held[part] = value.astype(jnp.bfloat16)
        copy = pltpu.make_async_copy(held.at[part], out_ref.at[pl.ds(at, count)], sems.at[part])
        copy.start()
        copies.append(copy)
    for copy in copies:
        copy.wait()


def on_device(coeffs, centers, kinetic, potential):
    fun_dev, support, points = coeffs.shape
    devices = lax.axis_size(AXES)
    me = lax.axis_index(AXES).astype(jnp.int32).reshape(1)
    box_dev = fun_dev // 2
    volume = 1.0 / (support * points)
    reading = 4 * support
    slots = 2 * REACH + 1
    offsets = list(range(-REACH, REACH + 1))
    first, last = REACH, -REACH
    now = [first] + [sign * k for k in range(1, REACH) for sign in (1, -1)]
    one_way = list(range(REACH, 0, -1)) + list(range(-REACH, 0))
    rows, low_cut, high_cut, boxes, blocks = bounds(fun_dev, support)
    assert blocks <= REACH + 1 and support & (support - 1) == 0
    back = tuple(rounded_up(r, 16) for r in rows)
    rows_of = {k: back[k + REACH] for k in offsets}
    flat = coeffs.reshape(fun_dev * support, points)
    halo = REACH + -(-(reading + 8) // fun_dev)
    count = rounded_up((2 * halo + 2) * fun_dev, 128)
    half = rounded_up(box_dev, 16)
    bf16, f32 = jnp.bfloat16, jnp.float32
    smem = pl.BlockSpec(memory_space=pltpu.SMEM)
    vmem = pl.BlockSpec(memory_space=pltpu.VMEM)
    limit = pltpu.CompilerParams(vmem_limit_bytes=26 * 2**20)

    sent_rows = {k: rounded_up(rows[k + REACH] + (2 * box_dev if k < 0 else 0), 16) for k in offsets if k}
    *packed, near, cut, home_row, own_region = pl.pallas_call(
        functools.partial(pack_kernel, (fun_dev, support, devices, halo, rows, back, low_cut, high_cut, now + [last])),
        out_shape=tuple(jax.ShapeDtypeStruct((sent_rows[k], points), bf16) for k in now + [last])
        + (
            jax.ShapeDtypeStruct((count, 128), f32),
            jax.ShapeDtypeStruct((slots + 1,), jnp.int32),
            jax.ShapeDtypeStruct((1, fun_dev * support), f32),
            jax.ShapeDtypeStruct((2 * half, points), bf16),
        ),
        in_specs=[smem] + [vmem] * 3,
        out_specs=(vmem,) * slots + (smem,) + (vmem,) * 2,
        scratch_shapes=[pltpu.VMEM((8, fun_dev * support), f32)],
        compiler_params=limit,
        name="pack",
    )(me, centers.reshape(1, -1), flat, potential)
    arrived = all_sent(dict(zip(now + [last], packed)), now, last, 1)

    columns, places, active, local = pl.pallas_call(
        functools.partial(table_kernel, (fun_dev, support, halo, boxes)),
        out_shape=(
            jax.ShapeDtypeStruct((slots * SLOT, 128), f32),
            jax.ShapeDtypeStruct((boxes // STEP, 8, STEP * SLOT), f32),
            jax.ShapeDtypeStruct(((slots + 1) * (boxes // STEP),), jnp.int32),
            jax.ShapeDtypeStruct((boxes, SLOT, points), bf16),
        ),
        in_specs=[smem, vmem, vmem],
        out_specs=(vmem, vmem, smem, vmem),
        compiler_params=limit,
        name="tables",
    )(cut, near, flat)

    wide = slots * SLOT
    sources = [arrived[REACH - e] for e in range(slots) if e != REACH]
    read_rows = [rows_of[REACH - e] for e in range(slots)]
    level_sizes = [level_rows(part + 1)[1] - level_rows(part + 1)[0] for part in range(REACH)]
    exact_rows = [rows[2 * REACH - e] for e in range(slots)]
    band = (fun_dev, 2 * reading)
    pieces, region, *grams = pl.pallas_call(
        functools.partial(unpack_kernel, (fun_dev, box_dev, reading, volume, exact_rows, read_rows, blocks)),
        out_shape=(
            jax.ShapeDtypeStruct((boxes, wide, points), bf16),
            jax.ShapeDtypeStruct((128, points), bf16),
        )
        + tuple(jax.ShapeDtypeStruct(band, f32) for _ in range(slots)),
        in_specs=[smem, smem] + [vmem] * (3 + len(sources)),
        out_specs=(vmem,) * (2 + slots),
        scratch_shapes=[pltpu.VMEM((wide, band_lanes(fun_dev, reading)), f32)]
        + [pltpu.VMEM((size, size), f32) for size in level_sizes],
        compiler_params=limit,
        name="unpack",
    )(cut, active, columns, own_region, local, *sources)

    summed = sent({k: grams[REACH + k] for k in one_way}, one_way, 1)
    gram_band, mixing_rows = pl.pallas_call(
        functools.partial(sum_kernel, reading),
        out_shape=(jax.ShapeDtypeStruct(band, f32), jax.ShapeDtypeStruct((SLOT, 2 * reading), bf16)),
        in_specs=[vmem] * slots,
        out_specs=(vmem, vmem),
        compiler_params=limit,
        name="sum",
    )(grams[REACH], *[summed[k] for k in one_way])
    mixing_of = sent({k: mixing_rows for k in one_way}, one_way, 1)
    mixing_of[0] = mixing_rows
    band_order = one_way + [0]

    out_rows = [rows_of[REACH - e] for e in range(slots)]
    shapes = [(r, points) for r in out_rows] + [(r, 128) for r in out_rows]
    mixed = pl.pallas_call(
        functools.partial(mix_kernel, (fun_dev, reading, band_order)),
        out_shape=tuple(jax.ShapeDtypeStruct(shape, bf16) for shape in shapes),
        in_specs=[smem, smem] + [vmem] * (2 + slots),
        out_specs=(vmem,) * len(shapes),
        scratch_shapes=[pltpu.VMEM((STEP, wide, points), bf16)]
        + [pltpu.VMEM((size, size), bf16) for size in level_sizes],
        compiler_params=limit,
        name="mix",
    )(cut, active, places, pieces, *[mixing_of[k] for k in band_order])

    ready = {}
    for k in now + [last, 0]:
        here, at_box = mixed[REACH - k], mixed[slots + REACH - k]
        near_by = jnp.dot(at_box, region, preferred_element_type=f32)
        applied = jnp.dot(here, kinetic, preferred_element_type=f32)
        ready[k] = (applied + near_by * here.astype(f32)).astype(bf16)
    returned = all_sent(ready, now, last, -1)
    returned[0] = ready[0]

    bases = {k: sum(back[: k + REACH]) for k in offsets}
    early, late = [0, first], now[1:] + [last]
    begun = pl.pallas_call(
        functools.partial(early_kernel, [bases[k] for k in early]),
        out_shape=jax.ShapeDtypeStruct(flat.shape, bf16),
        in_specs=[vmem] * (1 + len(early)),
        out_specs=vmem,
        compiler_params=limit,
        name="early",
    )(home_row, *[returned[k] for k in early])
    filtered = pl.pallas_call(
        functools.partial(home_kernel, [bases[k] for k in late]),
        out_shape=jax.ShapeDtypeStruct(flat.shape, bf16),
        in_specs=[vmem] * (2 + len(late)),
        out_specs=pl.BlockSpec(memory_space=pl.ANY),
        scratch_shapes=[
            pltpu.VMEM((flat.shape[0] // 256, 256, points), bf16),
            pltpu.SemaphoreType.DMA((flat.shape[0] // 256,)),
        ],
        compiler_params=limit,
        name="home",
    )(home_row, begun, *[returned[k] for k in late])
    return (filtered.reshape(coeffs.shape), gram_band)


def solution(mesh):
    placed = (P(AXES, None, None), P(), P(), P(AXES, None))
    return jax.shard_map(
        on_device,
        mesh=mesh,
        in_specs=placed,
        out_specs=(P(AXES, None, None), P(AXES, None)),
        check_vma=False,
    )
```

```python
import functools
import itertools

import jax
import jax.numpy as jnp
import numpy as np
from jax import lax
from jax.experimental import pallas as pl
from jax.experimental.pallas import tpu as pltpu
from jax.sharding import PartitionSpec as P

AXES = ("func", "box")
REACH = 3
SLOT = 32
STEP = 8


def passed_along(value, steps):
    count = lax.axis_size(AXES)
    pairs = [(source, (source + steps) % count) for source in range(count)]
    return lax.ppermute(value, AXES, pairs)


def sent(values, keys, sign):
    return {k: passed_along(values[k], sign * k) for k in keys}


def all_sent(values, now, last, sign):
    there = sent(values, now, sign)
    value, there[now[0]] = lax.optimization_barrier((values[last], there[now[0]]))
    there[last] = passed_along(value, sign * last)
    return there


def rounded_up(value, multiple):
    return -(-int(value) // multiple) * multiple


@functools.lru_cache(maxsize=None)
def bounds(fun_dev, support):
    box_dev = fun_dev // 2
    orders = [
        order
        for order in sorted(set(itertools.permutations((1, 1, 2, 4))))
        if np.abs(np.cumsum(np.array(order) - 2)).max() <= 1
    ]
    box_all, fun_all = 12 * support, 24 * support
    assert fun_all % fun_dev == 0
    devices = fun_all // fun_dev
    rows = np.zeros(2 * REACH + 1, np.int64)
    low, high, boxes, end = 10**6, -(10**6), 0, 0
    for picks in itertools.product(orders, repeat=3):
        density = np.repeat(np.concatenate(picks), support)
        centers = np.repeat(np.arange(box_all), density)
        load = sum(np.roll(density, t) for t in range(support))
        below = np.concatenate([[0], np.cumsum(np.tile(load, 3))])
        over = np.clip(np.arange(box_all)[:, None] + support - box_all, 0, None)
        carried = int((over[:, 0] * density).sum())
        below = below - carried
        twice = below[:-1] + below[1:]
        cut = np.array([
            np.searchsorted(twice, 2 * support * fun_dev * (devices + d), side="right")
            for d in range(-REACH - 1, devices + REACH + 2)
        ]) - box_all
        first = REACH + 1
        width = np.diff(cut)
        place = cut - box_dev * (np.arange(len(cut)) - first)
        low, high = min(low, place.min()), max(high, place.max())
        boxes = max(boxes, width.max())
        end = max(end, (place[:-1] + width).max())
        box = centers[:, None] + np.arange(support)
        owner = np.searchsorted(cut, box, side="right") - 1 - first
        device = np.arange(fun_all)[:, None] // fun_dev
        offset = owner - device
        assert np.abs(offset).max() <= REACH
        count = np.bincount((device * (2 * REACH + 1) + offset + REACH).ravel(), minlength=devices * (2 * REACH + 1))
        rows = np.maximum(rows, count.reshape(devices, -1).max(0))
    return (
        tuple(int(r) for r in rows),
        int(low),
        int(high),
        rounded_up(boxes, STEP),
        -(-int(end) // box_dev),
    )


def iota(shape, dim):
    return lax.broadcasted_iota(jnp.int32, shape, dim).astype(jnp.float32)


def one_hot(mask):
    return jnp.where(mask, 1.0, 0.0).astype(jnp.bfloat16)


def spread_over(column, to):
    return jnp.sum(jnp.where(iota((column.shape[0], to.shape[1]), 0) == to, column, 0.0), axis=0, keepdims=True)


def times(a, b, dims=((1,), (0,)), precision=None):
    return lax.dot_general(
        a, b, (dims, ((), ())), precision=precision, preferred_element_type=jnp.float32
    )


def pack_kernel(plan, me_ref, centers_ref, flat_hbm, potential_hbm, *refs):
    fun_dev, support, devices, halo, rows, back, low_cut, high_cut, now = plan
    outs = dict(zip(now, refs[: len(now)]))
    near_ref, cut_ref, home_ref, own_ref, row_ref, flat_ref, potential_ref, sems = refs[len(now) :]
    copies = [
        pltpu.make_async_copy(flat_hbm, flat_ref, sems.at[0]),
        pltpu.make_async_copy(potential_hbm, potential_ref, sems.at[1]),
    ]
    for copy in copies:
        copy.start()
    me = me_ref[0]
    box_dev = fun_dev // 2
    fun_all, box_all = fun_dev * devices, box_dev * devices
    count = near_ref.shape[0]

    start = me * fun_dev - halo * fun_dev
    start = jnp.where(start < 0, start + fun_all, start).astype(jnp.float32)
    at = start + iota((count, 1), 0)
    at = jnp.where(at >= fun_all, at - fun_all, at)
    near = jnp.sum(
        jnp.where(iota((count, fun_all), 1) == at, centers_ref[...].astype(jnp.float32)[None, :], 0.0), axis=1, keepdims=True
    )
    near = near - (me * box_dev).astype(jnp.float32)
    near = jnp.where(near < -(box_all // 2), near + box_all, near)
    near = jnp.where(near >= box_all // 2, near - box_all, near)
    near_row = spread_over(near, iota((1, count), 1))
    near_ref[...] = jnp.broadcast_to(near, near_ref.shape)

    tries = high_cut - low_cut + 1
    trial = iota((rounded_up(tries, 8), 1), 0)
    cuts = []
    for k in range(-REACH, REACH + 2):
        gap = trial + float(low_cut + k * box_dev) - near_row
        twice = jnp.sum(
            jnp.clip(gap, 0.0, support) + jnp.clip(gap + 1.0, 0.0, support), axis=1, keepdims=True
        )
        goal = float(2 * support * fun_dev * (halo + k))
        passed = jnp.where((twice <= goal) & (trial < tries), 1.0, 0.0)
        cut = jnp.sum(passed) + float(low_cut + k * box_dev)
        cuts.append(cut)
        cut_ref[k + REACH] = cut.astype(jnp.int32)

    copies[1].wait()
    potential = potential_ref[...]
    high = potential.astype(jnp.bfloat16)
    low = (potential - high.astype(jnp.float32)).astype(jnp.bfloat16)
    shape = (own_ref.shape[0], box_dev)
    at_high = iota(shape, 0) == iota(shape, 1)
    at_low = iota(shape, 0) - float(shape[0] // 2) == iota(shape, 1)
    own_ref[...] = (times(one_hot(at_high), high) + times(one_hot(at_low), low)).astype(jnp.bfloat16)

    mine = near[halo * fun_dev : (halo + 1) * fun_dev]
    pieces = fun_dev * support
    piece = lax.broadcasted_iota(jnp.int32, (1, pieces), 1)
    of_fun = lax.shift_right_logical(piece, support.bit_length() - 1).astype(jnp.float32)
    step = piece.astype(jnp.float32) - of_fun * support
    mine_row = spread_over(mine, of_fun)
    earlier = iota((fun_dev, pieces), 0) < of_fun
    home, base = jnp.zeros((1, pieces), jnp.float32), 0
    for k in range(-REACH, REACH + 1):
        first, end = cuts[k + REACH], cuts[k + REACH + 1]
        leave = jnp.clip(end - mine, 0.0, support) - jnp.clip(first - mine, 0.0, support)
        leave_at = jnp.sum(jnp.where(earlier, leave, 0.0), axis=0, keepdims=True)
        low_edge = jnp.clip(first - mine_row, 0.0, support)
        goes = (step >= low_edge) & (step < jnp.clip(end - mine_row, 0.0, support))
        row = leave_at + step - low_edge
        home = home + jnp.where(goes, row + float(base), 0.0)
        base += back[k + REACH]
        row_ref[k + REACH : k + REACH + 1] = jnp.where(goes, row, -1.0)
    row_ref[2 * REACH + 1 :] = jnp.full((row_ref.shape[0] - 2 * REACH - 1, pieces), -1.0, jnp.float32)
    home_ref[...] = home
    copies[0].wait()
    packed_rows(rows, box_dev, row_ref, flat_ref, own_ref, outs)


def packed_rows(rows, box_dev, row_ref, flat_ref, own_ref, outs):
    for k, out_ref in outs.items():
        sent = out_ref.shape[0]
        row = row_ref[k + REACH : k + REACH + 1]
        value = times(one_hot(iota((sent, row.shape[1]), 0) == row), flat_ref[...])
        if k < 0:
            shape = (sent, own_ref.shape[0])
            part = iota(shape, 0) - float(rows[k + REACH])
            from_col = jnp.where(part < box_dev, part, part - box_dev + float(shape[1] // 2))
            inside = (part >= 0) & (part < 2 * box_dev)
            value = value + times(one_hot(inside & (iota(shape, 1) == from_col)), own_ref[...])
        out_ref[...] = value.astype(jnp.bfloat16)


def picked(start, low, high, first, rows):
    lane = iota((SLOT, rows), 1)
    picks = []
    for b in range(STEP):
        box = first + float(b)
        row = jnp.where((box >= low) & (box < high), start + box, -1.0)
        picks.append(one_hot(lane == row))
    return jnp.concatenate(picks, axis=0)


def table_kernel(plan, cut_ref, near_ref, flat_ref, column_ref, place_ref, active_ref, local_ref):
    fun_dev, support, halo, boxes = plan
    slots = 2 * REACH + 1
    first = cut_ref[REACH].astype(jnp.float32)
    end = cut_ref[REACH + 1].astype(jnp.float32)
    lane = iota((SLOT, 128), 1)
    along = lax.broadcasted_iota(jnp.int32, (1, boxes * SLOT), 1)
    box = lax.shift_right_logical(along, SLOT.bit_length() - 1).astype(jnp.float32)
    of_fun = along.astype(jnp.float32) - box * SLOT
    levels = [1] * (boxes // STEP)
    for e in range(slots):
        at = (halo - REACH + e) * fun_dev
        others = near_ref[at : at + fun_dev, 0:1]
        edge_low = jnp.clip(first - others, 0.0, support)
        edge_high = jnp.clip(end - others, 0.0, support)
        come = edge_high - edge_low
        come_row = spread_over(come, lane[:1])
        come_at = jnp.sum(
            jnp.where(lane[:fun_dev] < iota((fun_dev, 128), 0), come_row, 0.0), axis=1, keepdims=True
        )
        box_low = edge_low + others - first
        box_high = edge_high + others - first
        packed = come_at - box_low
        spare = jnp.zeros((SLOT - fun_dev, 1), jnp.float32)
        if e == REACH:
            own_start = iota((fun_dev, 1), 0) * support + first - others
            own_start = jnp.concatenate([own_start, spare], axis=0)
        packed, box_low, box_high = (
            jnp.concatenate([column, spare], axis=0) for column in (packed, box_low, box_high)
        )
        if e == REACH:
            for g in range(boxes // STEP):
                pick = picked(own_start, box_low, box_high, float(g * STEP), flat_ref.shape[0])
                local_ref[g * STEP : (g + 1) * STEP] = times(pick, flat_ref[...]).astype(jnp.bfloat16).reshape(
                    STEP, SLOT, flat_ref.shape[1]
                )
        column_ref[e * SLOT : (e + 1) * SLOT, :] = jnp.where(
            lane == 0.0, packed, jnp.where(lane == 1.0, box_low, box_high)
        )
        lies = (box >= spread_over(box_low, of_fun)) & (box < spread_over(box_high, of_fun))
        place = jnp.where(lies, spread_over(packed, of_fun) + box, -1.0)
        for g in range(boxes // STEP):
            place_ref[g, e : e + 1, :] = place[:, g * STEP * SLOT : (g + 1) * STEP * SLOT]
            here = (box >= g * STEP) & (box < (g + 1) * STEP) & lies
            used = jnp.sum(jnp.where(here, 1.0, 0.0)).astype(jnp.int32)
            active_ref[e * (boxes // STEP) + g] = used
            level = jnp.where(used > 0, max(1, abs(e - REACH)), 1)
            levels[g] = jnp.maximum(levels[g], level)
    for g in range(boxes // STEP):
        active_ref[slots * (boxes // STEP) + g] = levels[g]
    spare = place_ref.shape[1] - slots
    place_ref[:, slots:, :] = jnp.full((boxes // STEP, spare, STEP * SLOT), -1.0, jnp.float32)


def function_of(shape, dim, fun_dev):
    row = lax.broadcasted_iota(jnp.int32, shape, dim)
    slot = lax.shift_right_logical(row, SLOT.bit_length() - 1)
    in_slot = row - slot * SLOT
    return jnp.where(in_slot < fun_dev, slot * fun_dev + in_slot, -1)


def moved(value, shift):
    return pltpu.roll(value, shift % value.shape[1], 1)


def skewed(value, sign):
    row = lax.broadcasted_iota(jnp.int32, value.shape, 0)
    bit = 1
    while bit < value.shape[0]:
        value = jnp.where((row & bit) != 0, moved(value, sign * bit), value)
        bit *= 2
    return value


def band_lanes(fun_dev, reading):
    window = (2 * REACH + 1) * fun_dev
    return rounded_up(window + reading + fun_dev + max(0, window - reading), 128)


def level_rows(level):
    return (REACH - level) * SLOT, (REACH + level + 1) * SLOT


def unpack_kernel(plan, cut_ref, active_ref, column_ref, own_ref, local_ref, *refs):
    fun_dev, box_dev, reading, volume, rows, back, blocks = plan
    slots = 2 * REACH + 1
    sources = refs[:REACH] + (None,) + refs[REACH : slots - 1]
    window_ref, region_ref = refs[slots - 1 : slots + 1]
    gram_refs = refs[slots + 1 : 2 * slots + 1]
    dense = refs[2 * slots + 1]
    totals = refs[2 * slots + 2 :]
    steps = window_ref.shape[0] // STEP
    width = cut_ref[REACH + 1] - cut_ref[REACH]

    for total in totals:
        total[...] = jnp.zeros_like(total)
    value = None
    for t in range(blocks):
        held = own_ref if t == 0 else sources[REACH + t]
        at = 0 if t == 0 else rows[REACH + t]
        from_row = at // 16 * 16
        held = held[from_row:]
        second = own_ref.shape[0] // 2 if t == 0 else box_dev
        shape = (region_ref.shape[0], held.shape[0])
        row, col = iota(shape, 0), iota(shape, 1)
        box = row - jnp.where(row >= SLOT, float(SLOT), 0.0) + cut_ref[REACH].astype(jnp.float32) - t * box_dev
        wanted = box + jnp.where(row >= SLOT, float(second), 0.0) + float(at - from_row)
        good = (box >= 0) & (box < box_dev) & (row < 2 * SLOT)
        term = times(one_hot(good & (col == wanted)), held)
        value = term if value is None else value + term
    region_ref[...] = value.astype(jnp.bfloat16)

    @pl.loop(0, lax.div(width + STEP - 1, STEP))
    def _(step):
        here_rows = pl.ds(step * STEP, STEP)
        level = active_ref[slots * steps + step]
        window_ref[here_rows, REACH * SLOT : (REACH + 1) * SLOT, :] = local_ref[here_rows]
        for e in range(slots):
            if e == REACH:
                continue
            used = active_ref[e * steps + step] > 0

            @pl.when(used)
            def _():
                start = column_ref[e * SLOT : (e + 1) * SLOT, 0:1]
                low = column_ref[e * SLOT : (e + 1) * SLOT, 1:2]
                high = column_ref[e * SLOT : (e + 1) * SLOT, 2:3]
                pick = picked(start, low, high, (step * STEP).astype(jnp.float32), back[e])
                found = times(pick, sources[e][: back[e]])
                window_ref[here_rows, e * SLOT : (e + 1) * SLOT, :] = found.astype(jnp.bfloat16).reshape(
                    STEP, SLOT, found.shape[-1]
                )

            @pl.when(jnp.logical_not(used) & (level >= abs(e - REACH)))
            def _():
                window_ref[here_rows, e * SLOT : (e + 1) * SLOT, :] = jnp.zeros(
                    (STEP, SLOT, window_ref.shape[-1]), jnp.bfloat16
                )
        for part, total in enumerate(totals):
            @pl.when(level == part + 1)
            def _():
                low, high = level_rows(part + 1)
                value = total[...]
                for b in range(STEP):
                    here = window_ref[step * STEP + b, low:high]
                    value = value + times(here, here, ((1,), (1,)))
                total[...] = value

    wide, lanes = dense.shape
    keep = jnp.where(
        function_of((wide, lanes), 0, fun_dev) == lax.broadcasted_iota(jnp.int32, (wide, lanes), 1), volume, 0.0
    )
    dense[...] = times(totals[-1][...], keep, precision=lax.Precision.HIGHEST)
    for part, total in enumerate(totals[:-1]):
        low, high = level_rows(part + 1)
        dense[low:high] += times(total[...], keep[low:high], precision=lax.Precision.HIGHEST)
    for e in range(slots):
        rows_here = dense[e * SLOT : e * SLOT + fun_dev]
        gram_refs[e][...] = skewed(moved(rows_here, reading - 1 - e * fun_dev), -1)[:, : 2 * reading]


def sum_kernel(reading, *refs):
    gram_ref, mixing_ref = refs[-2:]
    value = refs[0][...]
    for ref in refs[1:-2]:
        value = value + ref[...]
    gram_ref[...] = value
    diagonal = jnp.where(lax.broadcasted_iota(jnp.int32, value.shape, 1) == reading - 1, 1.5, 0.0)
    row = diagonal - 0.5 * value
    spare = jnp.zeros((mixing_ref.shape[0] - row.shape[0], row.shape[1]), jnp.float32)
    mixing_ref[...] = jnp.concatenate([row, spare], axis=0).astype(jnp.bfloat16)


def mix_kernel(plan, cut_ref, active_ref, place_ref, window_ref, region_ref, kinetic_ref, *refs):
    fun_dev, reading, band_order = plan
    slots = 2 * REACH + 1
    bands = dict(zip(band_order, refs[:slots]))
    outs = refs[slots : 2 * slots]
    at_boxes = refs[2 * slots : 3 * slots]
    mixed = refs[3 * slots]
    mixings = refs[3 * slots + 1 :]
    steps = window_ref.shape[0] // STEP
    width = cut_ref[REACH + 1] - cut_ref[REACH]
    for out, at_box in zip(outs, at_boxes):
        out[...] = jnp.zeros_like(out)
        at_box[...] = jnp.zeros_like(at_box)
    lanes = band_lanes(fun_dev, reading)
    parts = []
    for e in range(slots):
        band = bands[REACH - e][...].astype(jnp.float32)
        band = jnp.concatenate([band, jnp.zeros((SLOT, lanes - 2 * reading), jnp.float32)], axis=1)
        parts.append(moved(skewed(band, 1), e * fun_dev - (reading - 1)))
    dense = jnp.concatenate(parts, axis=0).astype(jnp.bfloat16)
    for part, mixing in enumerate(mixings):
        low, high = level_rows(part + 1)
        shape = (lanes, mixing.shape[1])
        column = function_of(shape, 1, fun_dev)
        column = jnp.where(column >= 0, column + low // SLOT * fun_dev, -1)
        keep = one_hot(column == lax.broadcasted_iota(jnp.int32, shape, 0))
        mixing[...] = times(dense[low:high], keep).astype(jnp.bfloat16)

    @pl.loop(0, lax.div(width + STEP - 1, STEP))
    def _(step):
        level = active_ref[slots * steps + step]
        for part, mixing in enumerate(mixings):
            @pl.when(level == part + 1)
            def _():
                low, high = level_rows(part + 1)
                for b in range(STEP):
                    here = window_ref[step * STEP + b, low:high]
                    mixed[b, low:high] = times(mixing[...], here).astype(jnp.bfloat16)
        shape = (STEP * SLOT, at_boxes[0].shape[1])
        along = lax.broadcasted_iota(jnp.int32, shape, 0)
        box = lax.shift_right_logical(along, SLOT.bit_length() - 1) + step * STEP
        col = lax.broadcasted_iota(jnp.int32, shape, 1)
        boxes_of = one_hot((col == box) | (col == box + SLOT))
        for e in range(slots):
            @pl.when(active_ref[e * steps + step] > 0)
            def _():
                place = place_ref[step, e : e + 1, :]
                pick = one_hot(iota((outs[e].shape[0], STEP * SLOT), 0) == place)
                part = mixed[:, e * SLOT : (e + 1) * SLOT, :].reshape(STEP * SLOT, mixed.shape[-1])
                outs[e][...] += times(pick, part).astype(jnp.bfloat16)
                at_boxes[e][...] += times(pick, boxes_of).astype(jnp.bfloat16)

    for e in (REACH - 1, REACH + 1):
        here = outs[e][...]
        applied = times(here, kinetic_ref[...])
        near_by = times(at_boxes[e][...], region_ref[...])
        outs[e][...] = (applied + near_by * here.astype(jnp.float32)).astype(jnp.bfloat16)


def home_rows(bases, home_ref, sources, at, count):
    shape = (count, home_ref.shape[1])
    here = iota(shape, 1) == iota(shape, 0) + float(at)
    row = jnp.sum(jnp.where(here, home_ref[...], 0.0), axis=1, keepdims=True)
    value = None
    for base, source in zip(bases, sources):
        pick = one_hot(iota((count, source.shape[0]), 1) == row - float(base))
        term = times(pick, source[...])
        value = term if value is None else value + term
    return value


def early_kernel(bases, home_ref, *refs):
    sources, out_ref = refs[:-1], refs[-1]
    count = 256
    for at in range(0, out_ref.shape[0], count):
        out_ref[at : at + count] = home_rows(bases, home_ref, sources, at, count).astype(jnp.bfloat16)


def home_kernel(bases, home_ref, early_ref, *refs):
    sources, out_ref, held, sems = refs[:-3], refs[-3], refs[-2], refs[-1]
    copies = []
    count = held.shape[1]
    for part in range(held.shape[0]):
        at = part * count
        value = home_rows(bases, home_ref, sources, at, count) + early_ref[at : at + count].astype(jnp.float32)
        held[part] = value.astype(jnp.bfloat16)
        copy = pltpu.make_async_copy(held.at[part], out_ref.at[pl.ds(at, count)], sems.at[part])
        copy.start()
        copies.append(copy)
    for copy in copies:
        copy.wait()


def on_device(coeffs, centers, kinetic, potential):
    fun_dev, support, points = coeffs.shape
    devices = lax.axis_size(AXES)
    me = lax.axis_index(AXES).astype(jnp.int32).reshape(1)
    box_dev = fun_dev // 2
    volume = 1.0 / (support * points)
    reading = 4 * support
    slots = 2 * REACH + 1
    offsets = list(range(-REACH, REACH + 1))
    last = -REACH
    now = [sign * k for k in range(1, REACH) for sign in (-1, 1)] + [REACH]
    one_way = list(range(REACH, 0, -1)) + list(range(-REACH, 0))
    rows, low_cut, high_cut, boxes, blocks = bounds(fun_dev, support)
    assert blocks <= REACH + 1 and support & (support - 1) == 0
    back = tuple(rounded_up(r, 16) for r in rows)
    rows_of = {k: back[k + REACH] for k in offsets}
    flat = coeffs.reshape(fun_dev * support, points)
    halo = REACH + -(-(reading + 8) // fun_dev)
    count = rounded_up((2 * halo + 2) * fun_dev, 128)
    half = rounded_up(box_dev, 16)
    bf16, f32 = jnp.bfloat16, jnp.float32
    smem = pl.BlockSpec(memory_space=pltpu.SMEM)
    vmem = pl.BlockSpec(memory_space=pltpu.VMEM)
    limit = pltpu.CompilerParams(vmem_limit_bytes=26 * 2**20)

    sent_rows = {k: rounded_up(rows[k + REACH] + (2 * box_dev if k < 0 else 0), 16) for k in offsets if k}
    *packed, near, cut, home_row, own_region = pl.pallas_call(
        functools.partial(pack_kernel, (fun_dev, support, devices, halo, rows, back, low_cut, high_cut, now + [last])),
        out_shape=tuple(jax.ShapeDtypeStruct((sent_rows[k], points), bf16) for k in now + [last])
        + (
            jax.ShapeDtypeStruct((count, 128), f32),
            jax.ShapeDtypeStruct((slots + 1,), jnp.int32),
            jax.ShapeDtypeStruct((1, fun_dev * support), f32),
            jax.ShapeDtypeStruct((2 * half, points), bf16),
        ),
        in_specs=[smem, vmem] + [pl.BlockSpec(memory_space=pltpu.HBM)] * 2,
        out_specs=(vmem,) * slots + (smem,) + (vmem,) * 2,
        scratch_shapes=[
            pltpu.VMEM((8, fun_dev * support), f32),
            pltpu.VMEM(flat.shape, bf16),
            pltpu.VMEM(potential.shape, f32),
            pltpu.SemaphoreType.DMA((2,)),
        ],
        compiler_params=pltpu.CompilerParams(vmem_limit_bytes=52 * 2**20),
        name="pack",
    )(me, centers, flat, potential)
    arrived = all_sent(dict(zip(now + [last], packed)), now, last, 1)

    columns, places, active, local = pl.pallas_call(
        functools.partial(table_kernel, (fun_dev, support, halo, boxes)),
        out_shape=(
            jax.ShapeDtypeStruct((slots * SLOT, 128), f32),
            jax.ShapeDtypeStruct((boxes // STEP, 8, STEP * SLOT), f32),
            jax.ShapeDtypeStruct(((slots + 1) * (boxes // STEP),), jnp.int32),
            jax.ShapeDtypeStruct((boxes, SLOT, points), bf16),
        ),
        in_specs=[smem, vmem, vmem],
        out_specs=(vmem, vmem, smem, vmem),
        compiler_params=limit,
        name="tables",
    )(cut, near, flat)

    wide = slots * SLOT
    sources = [arrived[REACH - e] for e in range(slots) if e != REACH]
    read_rows = [rows_of[REACH - e] for e in range(slots)]
    level_sizes = [level_rows(part + 1)[1] - level_rows(part + 1)[0] for part in range(REACH)]
    exact_rows = [rows[2 * REACH - e] for e in range(slots)]
    band = (fun_dev, 2 * reading)
    pieces, region, *grams = pl.pallas_call(
        functools.partial(unpack_kernel, (fun_dev, box_dev, reading, volume, exact_rows, read_rows, blocks)),
        out_shape=(
            jax.ShapeDtypeStruct((boxes, wide, points), bf16),
            jax.ShapeDtypeStruct((128, points), bf16),
        )
        + tuple(jax.ShapeDtypeStruct(band, f32) for _ in range(slots)),
        in_specs=[smem, smem] + [vmem] * (3 + len(sources)),
        out_specs=(vmem,) * (2 + slots),
        scratch_shapes=[pltpu.VMEM((wide, band_lanes(fun_dev, reading)), f32)]
        + [pltpu.VMEM((size, size), f32) for size in level_sizes],
        compiler_params=limit,
        name="unpack",
    )(cut, active, columns, own_region, local, *sources)

    summed = sent({k: grams[REACH + k] for k in one_way}, one_way, 1)
    gram_band, mixing_rows = pl.pallas_call(
        functools.partial(sum_kernel, reading),
        out_shape=(jax.ShapeDtypeStruct(band, f32), jax.ShapeDtypeStruct((SLOT, 2 * reading), bf16)),
        in_specs=[vmem] * slots,
        out_specs=(vmem, vmem),
        compiler_params=limit,
        name="sum",
    )(grams[REACH], *[summed[k] for k in one_way])
    mixing_of = sent({k: mixing_rows for k in one_way}, one_way, 1)
    mixing_of[0] = mixing_rows
    band_order = one_way + [0]

    out_rows = [rows_of[REACH - e] for e in range(slots)]
    shapes = [(r, points) for r in out_rows] + [(r, 128) for r in out_rows]
    mixed = pl.pallas_call(
        functools.partial(mix_kernel, (fun_dev, reading, band_order)),
        out_shape=tuple(jax.ShapeDtypeStruct(shape, bf16) for shape in shapes),
        in_specs=[smem, smem] + [vmem] * (4 + slots),
        out_specs=(vmem,) * len(shapes),
        scratch_shapes=[pltpu.VMEM((STEP, wide, points), bf16)]
        + [pltpu.VMEM((size, size), bf16) for size in level_sizes],
        compiler_params=limit,
        name="mix",
    )(cut, active, places, pieces, region, kinetic, *[mixing_of[k] for k in band_order])

    ready = {}
    for k in now + [last, 0]:
        here, at_box = mixed[REACH - k], mixed[slots + REACH - k]
        if abs(k) == 1:
            ready[k] = here
            continue
        near_by = jnp.dot(at_box, region, preferred_element_type=f32)
        applied = jnp.dot(here, kinetic, preferred_element_type=f32)
        ready[k] = (applied + near_by * here.astype(f32)).astype(bf16)
    returned = all_sent(ready, now, last, -1)
    returned[0] = ready[0]

    bases = {k: sum(back[: k + REACH]) for k in offsets}
    early, late = [0] + now[:2], now[2:] + [last]
    begun = pl.pallas_call(
        functools.partial(early_kernel, [bases[k] for k in early]),
        out_shape=jax.ShapeDtypeStruct(flat.shape, bf16),
        in_specs=[vmem] * (1 + len(early)),
        out_specs=vmem,
        compiler_params=limit,
        name="early",
    )(home_row, *[returned[k] for k in early])
    filtered = pl.pallas_call(
        functools.partial(home_kernel, [bases[k] for k in late]),
        out_shape=jax.ShapeDtypeStruct(flat.shape, bf16),
        in_specs=[vmem] * (2 + len(late)),
        out_specs=pl.BlockSpec(memory_space=pl.ANY),
        scratch_shapes=[
            pltpu.VMEM((flat.shape[0] // 256, 256, points), bf16),
            pltpu.SemaphoreType.DMA((flat.shape[0] // 256,)),
        ],
        compiler_params=limit,
        name="home",
    )(home_row, begun, *[returned[k] for k in late])
    return (filtered.reshape(coeffs.shape), gram_band)


def solution(mesh):
    placed = (P(AXES, None, None), P(), P(), P(AXES, None))
    return jax.shard_map(
        on_device,
        mesh=mesh,
        in_specs=placed,
        out_specs=(P(AXES, None, None), P(AXES, None)),
        check_vma=False,
    )
```

```python
import functools
import itertools

import jax
import jax.numpy as jnp
import numpy as np
from jax import lax
from jax.experimental import pallas as pl
from jax.experimental.pallas import tpu as pltpu
from jax.sharding import PartitionSpec as P

AXES = ("func", "box")
REACH = 3
SLOT = 32
STEP = 8


def passed_along(value, steps):
    count = lax.axis_size(AXES)
    pairs = [(source, (source + steps) % count) for source in range(count)]
    return lax.ppermute(value, AXES, pairs)


def sent(values, keys, sign):
    return {k: passed_along(values[k], sign * k) for k in keys}


def all_sent(values, now, last, sign):
    there = sent(values, now, sign)
    value, there[now[0]] = lax.optimization_barrier((values[last], there[now[0]]))
    there[last] = passed_along(value, sign * last)
    return there


def rounded_up(value, multiple):
    return -(-int(value) // multiple) * multiple


@functools.lru_cache(maxsize=None)
def bounds(fun_dev, support):
    box_dev = fun_dev // 2
    orders = [
        order
        for order in sorted(set(itertools.permutations((1, 1, 2, 4))))
        if np.abs(np.cumsum(np.array(order) - 2)).max() <= 1
    ]
    box_all, fun_all = 12 * support, 24 * support
    assert fun_all % fun_dev == 0
    devices = fun_all // fun_dev
    rows = np.zeros(2 * REACH + 1, np.int64)
    low, high, boxes, end = 10**6, -(10**6), 0, 0
    for picks in itertools.product(orders, repeat=3):
        density = np.repeat(np.concatenate(picks), support)
        centers = np.repeat(np.arange(box_all), density)
        load = sum(np.roll(density, t) for t in range(support))
        below = np.concatenate([[0], np.cumsum(np.tile(load, 3))])
        over = np.clip(np.arange(box_all)[:, None] + support - box_all, 0, None)
        carried = int((over[:, 0] * density).sum())
        below = below - carried
        twice = below[:-1] + below[1:]
        cut = np.array([
            np.searchsorted(twice, 2 * support * fun_dev * (devices + d), side="right")
            for d in range(-REACH - 1, devices + REACH + 2)
        ]) - box_all
        first = REACH + 1
        width = np.diff(cut)
        place = cut - box_dev * (np.arange(len(cut)) - first)
        low, high = min(low, place.min()), max(high, place.max())
        boxes = max(boxes, width.max())
        end = max(end, (place[:-1] + width).max())
        box = centers[:, None] + np.arange(support)
        owner = np.searchsorted(cut, box, side="right") - 1 - first
        device = np.arange(fun_all)[:, None] // fun_dev
        offset = owner - device
        assert np.abs(offset).max() <= REACH
        count = np.bincount((device * (2 * REACH + 1) + offset + REACH).ravel(), minlength=devices * (2 * REACH + 1))
        rows = np.maximum(rows, count.reshape(devices, -1).max(0))
    return (
        tuple(int(r) for r in rows),
        int(low),
        int(high),
        rounded_up(boxes, STEP),
        -(-int(end) // box_dev),
    )


def iota(shape, dim):
    return lax.broadcasted_iota(jnp.int32, shape, dim).astype(jnp.float32)


def one_hot(mask):
    return jnp.where(mask, 1.0, 0.0).astype(jnp.bfloat16)


def spread_over(column, to):
    return jnp.sum(jnp.where(iota((column.shape[0], to.shape[1]), 0) == to, column, 0.0), axis=0, keepdims=True)


def times(a, b, dims=((1,), (0,)), precision=None):
    return lax.dot_general(
        a, b, (dims, ((), ())), precision=precision, preferred_element_type=jnp.float32
    )


def pack_kernel(plan, me_ref, centers_ref, flat_hbm, *refs):
    fun_dev, support, devices, halo, back, low_cut, high_cut, now = plan
    outs = dict(zip(now, refs[: len(now)]))
    near_ref, cut_ref, home_ref, row_ref, flat_ref, sem = refs[len(now) :]
    copy = pltpu.make_async_copy(flat_hbm, flat_ref, sem)
    copy.start()
    me = me_ref[0]
    box_dev = fun_dev // 2
    fun_all, box_all = fun_dev * devices, box_dev * devices
    count = near_ref.shape[0]

    start = me * fun_dev - halo * fun_dev
    start = jnp.where(start < 0, start + fun_all, start).astype(jnp.float32)
    at = start + iota((count, 1), 0)
    at = jnp.where(at >= fun_all, at - fun_all, at)
    near = jnp.sum(
        jnp.where(iota((count, fun_all), 1) == at, centers_ref[...].astype(jnp.float32)[None, :], 0.0), axis=1, keepdims=True
    )
    near = near - (me * box_dev).astype(jnp.float32)
    near = jnp.where(near < -(box_all // 2), near + box_all, near)
    near = jnp.where(near >= box_all // 2, near - box_all, near)
    near_row = spread_over(near, iota((1, count), 1))
    near_ref[...] = jnp.broadcast_to(near, near_ref.shape)

    tries = high_cut - low_cut + 1
    trial = iota((rounded_up(tries, 8), 1), 0)
    cuts = []
    for k in range(-REACH, REACH + 2):
        gap = trial + float(low_cut + k * box_dev) - near_row
        twice = jnp.sum(
            jnp.clip(gap, 0.0, support) + jnp.clip(gap + 1.0, 0.0, support), axis=1, keepdims=True
        )
        goal = float(2 * support * fun_dev * (halo + k))
        passed = jnp.where((twice <= goal) & (trial < tries), 1.0, 0.0)
        cut = jnp.sum(passed) + float(low_cut + k * box_dev)
        cuts.append(cut)
        cut_ref[k + REACH] = cut.astype(jnp.int32)

    mine = near[halo * fun_dev : (halo + 1) * fun_dev]
    pieces = fun_dev * support
    piece = lax.broadcasted_iota(jnp.int32, (1, pieces), 1)
    of_fun = lax.shift_right_logical(piece, support.bit_length() - 1).astype(jnp.float32)
    step = piece.astype(jnp.float32) - of_fun * support
    mine_row = spread_over(mine, of_fun)
    earlier = iota((fun_dev, pieces), 0) < of_fun
    home, base = jnp.zeros((1, pieces), jnp.float32), 0
    for k in range(-REACH, REACH + 1):
        first, end = cuts[k + REACH], cuts[k + REACH + 1]
        leave = jnp.clip(end - mine, 0.0, support) - jnp.clip(first - mine, 0.0, support)
        leave_at = jnp.sum(jnp.where(earlier, leave, 0.0), axis=0, keepdims=True)
        low_edge = jnp.clip(first - mine_row, 0.0, support)
        goes = (step >= low_edge) & (step < jnp.clip(end - mine_row, 0.0, support))
        row = leave_at + step - low_edge
        home = home + jnp.where(goes, row + float(base), 0.0)
        base += back[k + REACH]
        row_ref[k + REACH : k + REACH + 1] = jnp.where(goes, row, -1.0)
    row_ref[2 * REACH + 1 :] = jnp.full((row_ref.shape[0] - 2 * REACH - 1, pieces), -1.0, jnp.float32)
    home_ref[...] = home
    copy.wait()
    for k, out_ref in outs.items():
        row = row_ref[k + REACH : k + REACH + 1]
        pick = one_hot(iota((out_ref.shape[0], pieces), 0) == row)
        out_ref[...] = times(pick, flat_ref[...]).astype(jnp.bfloat16)


def picked(start, low, high, first, rows):
    lane = iota((SLOT, rows), 1)
    picks = []
    for b in range(STEP):
        box = first + float(b)
        row = jnp.where((box >= low) & (box < high), start + box, -1.0)
        picks.append(one_hot(lane == row))
    return jnp.concatenate(picks, axis=0)


def table_kernel(plan, cut_ref, near_ref, flat_ref, column_ref, place_ref, active_ref, local_ref):
    fun_dev, support, halo, boxes = plan
    slots = 2 * REACH + 1
    first = cut_ref[REACH].astype(jnp.float32)
    end = cut_ref[REACH + 1].astype(jnp.float32)
    lane = iota((SLOT, 128), 1)
    along = lax.broadcasted_iota(jnp.int32, (1, boxes * SLOT), 1)
    box = lax.shift_right_logical(along, SLOT.bit_length() - 1).astype(jnp.float32)
    of_fun = along.astype(jnp.float32) - box * SLOT
    levels = [1] * (boxes // STEP)
    for e in range(slots):
        at = (halo - REACH + e) * fun_dev
        others = near_ref[at : at + fun_dev, 0:1]
        edge_low = jnp.clip(first - others, 0.0, support)
        edge_high = jnp.clip(end - others, 0.0, support)
        come = edge_high - edge_low
        come_row = spread_over(come, lane[:1])
        come_at = jnp.sum(
            jnp.where(lane[:fun_dev] < iota((fun_dev, 128), 0), come_row, 0.0), axis=1, keepdims=True
        )
        box_low = edge_low + others - first
        box_high = edge_high + others - first
        packed = come_at - box_low
        spare = jnp.zeros((SLOT - fun_dev, 1), jnp.float32)
        if e == REACH:
            own_start = iota((fun_dev, 1), 0) * support + first - others
            own_start = jnp.concatenate([own_start, spare], axis=0)
        packed, box_low, box_high = (
            jnp.concatenate([column, spare], axis=0) for column in (packed, box_low, box_high)
        )
        if e == REACH:
            for g in range(boxes // STEP):
                pick = picked(own_start, box_low, box_high, float(g * STEP), flat_ref.shape[0])
                local_ref[g * STEP : (g + 1) * STEP] = times(pick, flat_ref[...]).astype(jnp.bfloat16).reshape(
                    STEP, SLOT, flat_ref.shape[1]
                )
        column_ref[e * SLOT : (e + 1) * SLOT, :] = jnp.where(
            lane == 0.0, packed, jnp.where(lane == 1.0, box_low, box_high)
        )
        lies = (box >= spread_over(box_low, of_fun)) & (box < spread_over(box_high, of_fun))
        place = jnp.where(lies, spread_over(packed, of_fun) + box, -1.0)
        for g in range(boxes // STEP):
            place_ref[g, e : e + 1, :] = place[:, g * STEP * SLOT : (g + 1) * STEP * SLOT]
            here = (box >= g * STEP) & (box < (g + 1) * STEP) & lies
            used = jnp.sum(jnp.where(here, 1.0, 0.0)).astype(jnp.int32)
            active_ref[e * (boxes // STEP) + g] = used
            level = jnp.where(used > 0, max(1, abs(e - REACH)), 1)
            levels[g] = jnp.maximum(levels[g], level)
    for g in range(boxes // STEP):
        active_ref[slots * (boxes // STEP) + g] = levels[g]
    spare = place_ref.shape[1] - slots
    place_ref[:, slots:, :] = jnp.full((boxes // STEP, spare, STEP * SLOT), -1.0, jnp.float32)


def function_of(shape, dim, fun_dev):
    row = lax.broadcasted_iota(jnp.int32, shape, dim)
    slot = lax.shift_right_logical(row, SLOT.bit_length() - 1)
    in_slot = row - slot * SLOT
    return jnp.where(in_slot < fun_dev, slot * fun_dev + in_slot, -1)


def moved(value, shift):
    return pltpu.roll(value, shift % value.shape[1], 1)


def skewed(value, sign):
    row = lax.broadcasted_iota(jnp.int32, value.shape, 0)
    bit = 1
    while bit < value.shape[0]:
        value = jnp.where((row & bit) != 0, moved(value, sign * bit), value)
        bit *= 2
    return value


def band_lanes(fun_dev, reading):
    window = (2 * REACH + 1) * fun_dev
    return rounded_up(window + reading + fun_dev + max(0, window - reading), 128)


def level_rows(level):
    return (REACH - level) * SLOT, (REACH + level + 1) * SLOT


def unpack_kernel(plan, cut_ref, active_ref, column_ref, potential_ref, local_ref, *refs):
    fun_dev, reading, volume, back = plan
    slots = 2 * REACH + 1
    sources = refs[:REACH] + (None,) + refs[REACH : slots - 1]
    window_ref = refs[slots - 1]
    gram_refs = refs[slots : 2 * slots]
    dense = refs[2 * slots]
    totals = refs[2 * slots + 1 :]
    steps = window_ref.shape[0] // STEP
    width = cut_ref[REACH + 1] - cut_ref[REACH]

    for total in totals:
        total[...] = jnp.zeros_like(total)
    @pl.loop(0, lax.div(width + STEP - 1, STEP))
    def _(step):
        here_rows = pl.ds(step * STEP, STEP)
        level = active_ref[slots * steps + step]
        window_ref[here_rows, REACH * SLOT : (REACH + 1) * SLOT, :] = local_ref[here_rows]
        for e in range(slots):
            if e == REACH:
                continue
            used = active_ref[e * steps + step] > 0

            @pl.when(used)
            def _():
                start = column_ref[e * SLOT : (e + 1) * SLOT, 0:1]
                low = column_ref[e * SLOT : (e + 1) * SLOT, 1:2]
                high = column_ref[e * SLOT : (e + 1) * SLOT, 2:3]
                pick = picked(start, low, high, (step * STEP).astype(jnp.float32), back[e])
                found = times(pick, sources[e][: back[e]])
                window_ref[here_rows, e * SLOT : (e + 1) * SLOT, :] = found.astype(jnp.bfloat16).reshape(
                    STEP, SLOT, found.shape[-1]
                )

            @pl.when(jnp.logical_not(used) & (level >= abs(e - REACH)))
            def _():
                window_ref[here_rows, e * SLOT : (e + 1) * SLOT, :] = jnp.zeros(
                    (STEP, SLOT, window_ref.shape[-1]), jnp.bfloat16
                )
        for part, total in enumerate(totals):
            @pl.when(level == part + 1)
            def _():
                low, high = level_rows(part + 1)
                value = total[...]
                for b in range(STEP):
                    here = window_ref[step * STEP + b, low:high]
                    value = value + times(here, here, ((1,), (1,)))
                total[...] = value

    wide, lanes = dense.shape
    keep = jnp.where(
        function_of((wide, lanes), 0, fun_dev) == lax.broadcasted_iota(jnp.int32, (wide, lanes), 1), volume, 0.0
    )
    dense[...] = times(totals[-1][...], keep, precision=lax.Precision.HIGHEST)
    for part, total in enumerate(totals[:-1]):
        low, high = level_rows(part + 1)
        dense[low:high] += times(total[...], keep[low:high], precision=lax.Precision.HIGHEST)
    for e in range(slots):
        rows_here = dense[e * SLOT : e * SLOT + fun_dev]
        gram_refs[e][:fun_dev] = skewed(moved(rows_here, reading - 1 - e * fun_dev), -1)[:, : 2 * reading]
        if e < REACH:
            box_dev, points = potential_ref.shape
            gram_refs[e][fun_dev:] = jnp.zeros((gram_refs[e].shape[0] - fun_dev, 2 * reading), jnp.float32)
            for q in range(points // (2 * reading)):
                at = fun_dev + q * 16
                gram_refs[e][at : at + box_dev] = potential_ref[:, q * 2 * reading : (q + 1) * 2 * reading]


def region_kernel(fun_dev, cut_ref, potential_ref, *refs):
    blocks, region_ref = refs[:-1], refs[-1]
    box_dev = potential_ref.shape[0]
    first = cut_ref[REACH].astype(jnp.float32)
    shape = (region_ref.shape[0], box_dev)
    row, col = iota(shape, 0), iota(shape, 1)
    lanes = blocks[0].shape[1]
    for q in range(potential_ref.shape[1] // lanes):
        value = None
        for t in range(1 + len(blocks)):
            if t == 0:
                held = potential_ref[:, q * lanes : (q + 1) * lanes]
            else:
                held = blocks[t - 1][fun_dev + q * 16 : fun_dev + q * 16 + box_dev]
            high = held.astype(jnp.bfloat16)
            low = (held - high.astype(jnp.float32)).astype(jnp.bfloat16)
            at_high = (row < SLOT) & (col == first + row - t * box_dev)
            at_low = (row >= SLOT) & (row < 2 * SLOT) & (col == first + row - SLOT - t * box_dev)
            term = times(one_hot(at_high), high) + times(one_hot(at_low), low)
            value = term if value is None else value + term
        region_ref[:, q * lanes : (q + 1) * lanes] = value.astype(jnp.bfloat16)


def sum_kernel(reading, *refs):
    gram_ref, mixing_ref = refs[-2:]
    count = gram_ref.shape[0]
    value = refs[0][...]
    for ref in refs[1:-2]:
        value = value + ref[:count]
    gram_ref[...] = value
    diagonal = jnp.where(lax.broadcasted_iota(jnp.int32, value.shape, 1) == reading - 1, 1.5, 0.0)
    row = diagonal - 0.5 * value
    spare = jnp.zeros((mixing_ref.shape[0] - row.shape[0], row.shape[1]), jnp.float32)
    mixing_ref[...] = jnp.concatenate([row, spare], axis=0).astype(jnp.bfloat16)


def mix_kernel(plan, cut_ref, active_ref, place_ref, window_ref, region_ref, kinetic_ref, *refs):
    fun_dev, reading, band_order = plan
    slots = 2 * REACH + 1
    bands = dict(zip(band_order, refs[:slots]))
    outs = refs[slots : 2 * slots]
    at_boxes = refs[2 * slots : 3 * slots]
    mixed = refs[3 * slots]
    mixings = refs[3 * slots + 1 :]
    steps = window_ref.shape[0] // STEP
    width = cut_ref[REACH + 1] - cut_ref[REACH]
    for out, at_box in zip(outs, at_boxes):
        out[...] = jnp.zeros_like(out)
        at_box[...] = jnp.zeros_like(at_box)
    lanes = band_lanes(fun_dev, reading)
    parts = []
    for e in range(slots):
        band = bands[REACH - e][...].astype(jnp.float32)
        band = jnp.concatenate([band, jnp.zeros((SLOT, lanes - 2 * reading), jnp.float32)], axis=1)
        parts.append(moved(skewed(band, 1), e * fun_dev - (reading - 1)))
    dense = jnp.concatenate(parts, axis=0).astype(jnp.bfloat16)
    for part, mixing in enumerate(mixings):
        low, high = level_rows(part + 1)
        shape = (lanes, mixing.shape[1])
        column = function_of(shape, 1, fun_dev)
        column = jnp.where(column >= 0, column + low // SLOT * fun_dev, -1)
        keep = one_hot(column == lax.broadcasted_iota(jnp.int32, shape, 0))
        mixing[...] = times(dense[low:high], keep).astype(jnp.bfloat16)

    @pl.loop(0, lax.div(width + STEP - 1, STEP))
    def _(step):
        level = active_ref[slots * steps + step]
        for part, mixing in enumerate(mixings):
            @pl.when(level == part + 1)
            def _():
                low, high = level_rows(part + 1)
                for b in range(STEP):
                    here = window_ref[step * STEP + b, low:high]
                    mixed[b, low:high] = times(mixing[...], here).astype(jnp.bfloat16)
        shape = (STEP * SLOT, at_boxes[0].shape[1])
        along = lax.broadcasted_iota(jnp.int32, shape, 0)
        box = lax.shift_right_logical(along, SLOT.bit_length() - 1) + step * STEP
        col = lax.broadcasted_iota(jnp.int32, shape, 1)
        boxes_of = one_hot((col == box) | (col == box + SLOT))
        for e in range(slots):
            @pl.when(active_ref[e * steps + step] > 0)
            def _():
                place = place_ref[step, e : e + 1, :]
                pick = one_hot(iota((outs[e].shape[0], STEP * SLOT), 0) == place)
                part = mixed[:, e * SLOT : (e + 1) * SLOT, :].reshape(STEP * SLOT, mixed.shape[-1])
                outs[e][...] += times(pick, part).astype(jnp.bfloat16)
                at_boxes[e][...] += times(pick, boxes_of).astype(jnp.bfloat16)

    for e in range(slots):
        if e == REACH:
            continue
        here = outs[e][...]
        applied = times(here, kinetic_ref[...])
        near_by = times(at_boxes[e][...], region_ref[...])
        outs[e][...] = (applied + near_by * here.astype(jnp.float32)).astype(jnp.bfloat16)


def home_rows(bases, home_ref, sources, at, count):
    shape = (count, home_ref.shape[1])
    here = iota(shape, 1) == iota(shape, 0) + float(at)
    row = jnp.sum(jnp.where(here, home_ref[...], 0.0), axis=1, keepdims=True)
    value = None
    for base, group in bases:
        parts = [sources[at][...] for at in group]
        held = parts[0] if len(parts) == 1 else jnp.concatenate(parts, axis=0)
        pick = one_hot(iota((count, held.shape[0]), 1) == row - float(base))
        term = times(pick, held)
        value = term if value is None else value + term
    return value


def early_kernel(bases, home_ref, *refs):
    sources, out_ref = refs[:-1], refs[-1]
    count = 256
    for at in range(0, out_ref.shape[0], count):
        out_ref[at : at + count] = home_rows(bases, home_ref, sources, at, count).astype(jnp.bfloat16)


def home_kernel(bases, home_ref, early_ref, *refs):
    sources, out_ref, held, sems = refs[:-3], refs[-3], refs[-2], refs[-1]
    copies = []
    count = held.shape[1]
    for part in range(held.shape[0]):
        at = part * count
        value = home_rows(bases, home_ref, sources, at, count) + early_ref[at : at + count].astype(jnp.float32)
        held[part] = value.astype(jnp.bfloat16)
        copy = pltpu.make_async_copy(held.at[part], out_ref.at[pl.ds(at, count)], sems.at[part])
        copy.start()
        copies.append(copy)
    for copy in copies:
        copy.wait()


def on_device(coeffs, centers, kinetic, potential):
    fun_dev, support, points = coeffs.shape
    devices = lax.axis_size(AXES)
    me = lax.axis_index(AXES).astype(jnp.int32).reshape(1)
    box_dev = fun_dev // 2
    volume = 1.0 / (support * points)
    reading = 4 * support
    slots = 2 * REACH + 1
    offsets = list(range(-REACH, REACH + 1))
    last = -REACH
    now = [sign * k for k in range(1, REACH) for sign in (-1, 1)] + [REACH]
    one_way = list(range(REACH, 0, -1)) + list(range(-REACH, 0))
    rows, low_cut, high_cut, boxes, blocks = bounds(fun_dev, support)
    assert blocks <= REACH + 1 and support & (support - 1) == 0
    back = tuple(rounded_up(r, 16) for r in rows)
    rows_of = {k: back[k + REACH] for k in offsets}
    flat = coeffs.reshape(fun_dev * support, points)
    halo = REACH + -(-(reading + 8) // fun_dev)
    count = rounded_up((2 * halo + 2) * fun_dev, 128)
    bf16, f32 = jnp.bfloat16, jnp.float32
    smem = pl.BlockSpec(memory_space=pltpu.SMEM)
    vmem = pl.BlockSpec(memory_space=pltpu.VMEM)
    limit = pltpu.CompilerParams(vmem_limit_bytes=26 * 2**20)

    *packed, near, cut, home_row = pl.pallas_call(
        functools.partial(pack_kernel, (fun_dev, support, devices, halo, back, low_cut, high_cut, now + [last])),
        out_shape=tuple(jax.ShapeDtypeStruct((rows_of[k], points), bf16) for k in now + [last])
        + (
            jax.ShapeDtypeStruct((count, 128), f32),
            jax.ShapeDtypeStruct((slots + 1,), jnp.int32),
            jax.ShapeDtypeStruct((1, fun_dev * support), f32),
        ),
        in_specs=[smem, vmem, pl.BlockSpec(memory_space=pltpu.HBM)],
        out_specs=(vmem,) * slots + (smem, vmem),
        scratch_shapes=[
            pltpu.VMEM((8, fun_dev * support), f32),
            pltpu.VMEM(flat.shape, bf16),
            pltpu.SemaphoreType.DMA,
        ],
        compiler_params=pltpu.CompilerParams(vmem_limit_bytes=52 * 2**20),
        name="pack",
    )(me, centers, flat)
    arrived = all_sent(dict(zip(now + [last], packed)), now, last, 1)

    columns, places, active, local = pl.pallas_call(
        functools.partial(table_kernel, (fun_dev, support, halo, boxes)),
        out_shape=(
            jax.ShapeDtypeStruct((slots * SLOT, 128), f32),
            jax.ShapeDtypeStruct((boxes // STEP, 8, STEP * SLOT), f32),
            jax.ShapeDtypeStruct(((slots + 1) * (boxes // STEP),), jnp.int32),
            jax.ShapeDtypeStruct((boxes, SLOT, points), bf16),
        ),
        in_specs=[smem, vmem, vmem],
        out_specs=(vmem, vmem, smem, vmem),
        compiler_params=limit,
        name="tables",
    )(cut, near, flat)

    wide = slots * SLOT
    sources = [arrived[REACH - e] for e in range(slots) if e != REACH]
    read_rows = [rows_of[REACH - e] for e in range(slots)]
    level_sizes = [level_rows(part + 1)[1] - level_rows(part + 1)[0] for part in range(REACH)]
    level_sizes = [level_rows(part + 1)[1] - level_rows(part + 1)[0] for part in range(REACH)]
    exact_rows = [rows[2 * REACH - e] for e in range(slots)]
    band = (fun_dev, 2 * reading)
    with_potential = (fun_dev + 16 * (points // (2 * reading)), 2 * reading)
    assert box_dev <= 16
    pieces, *grams = pl.pallas_call(
        functools.partial(unpack_kernel, (fun_dev, reading, volume, read_rows)),
        out_shape=(jax.ShapeDtypeStruct((boxes, wide, points), bf16),)
        + tuple(jax.ShapeDtypeStruct(with_potential if e < REACH else band, f32) for e in range(slots)),
        in_specs=[smem, smem] + [vmem] * (3 + len(sources)),
        out_specs=(vmem,) * (1 + slots),
        scratch_shapes=[pltpu.VMEM((wide, band_lanes(fun_dev, reading)), f32)]
        + [pltpu.VMEM((size, size), f32) for size in level_sizes],
        compiler_params=limit,
        name="unpack",
    )(cut, active, columns, potential, local, *sources)

    summed = sent({k: grams[REACH + k] for k in one_way}, one_way, 1)
    gram_band, mixing_rows = pl.pallas_call(
        functools.partial(sum_kernel, reading),
        out_shape=(jax.ShapeDtypeStruct(band, f32), jax.ShapeDtypeStruct((SLOT, 2 * reading), bf16)),
        in_specs=[vmem] * slots,
        out_specs=(vmem, vmem),
        compiler_params=limit,
        name="sum",
    )(grams[REACH], *[summed[k] for k in one_way])
    region = pl.pallas_call(
        functools.partial(region_kernel, fun_dev),
        out_shape=jax.ShapeDtypeStruct((128, points), bf16),
        in_specs=[smem] + [vmem] * blocks,
        out_specs=vmem,
        compiler_params=limit,
        name="region",
    )(cut, potential, *[summed[-t] for t in range(1, blocks)])
    mixing_of = sent({k: mixing_rows for k in one_way}, one_way, 1)
    mixing_of[0] = mixing_rows
    band_order = one_way + [0]

    out_rows = [rows_of[REACH - e] for e in range(slots)]
    shapes = [(r, points) for r in out_rows] + [(r, 128) for r in out_rows]
    mixed = pl.pallas_call(
        functools.partial(mix_kernel, (fun_dev, reading, band_order)),
        out_shape=tuple(jax.ShapeDtypeStruct(shape, bf16) for shape in shapes),
        in_specs=[smem, smem] + [vmem] * (4 + slots),
        out_specs=(vmem,) * len(shapes),
        scratch_shapes=[pltpu.VMEM((STEP, wide, points), bf16)]
        + [pltpu.VMEM((size, size), bf16) for size in level_sizes],
        compiler_params=limit,
        name="mix",
    )(cut, active, places, pieces, region, kinetic, *[mixing_of[k] for k in band_order])

    ready = {k: mixed[REACH - k] for k in now + [last]}
    here, at_box = mixed[REACH], mixed[slots + REACH]
    near_by = jnp.dot(at_box, region, preferred_element_type=f32)
    applied = jnp.dot(here, kinetic, preferred_element_type=f32)
    returned = all_sent(ready, now, last, -1)
    returned[0] = (applied + near_by * here.astype(f32)).astype(bf16)

    bases = {k: sum(back[: k + REACH]) for k in offsets}
    early, late = [0, -1, 1], [k for k in offsets if abs(k) > 1]
    early_groups = [(bases[k], [at]) for at, k in enumerate(early)]
    late_groups = [(bases[-REACH], list(range(REACH - 1))), (bases[2], list(range(REACH - 1, 2 * REACH - 2)))]
    begun = pl.pallas_call(
        functools.partial(early_kernel, early_groups),
        out_shape=jax.ShapeDtypeStruct(flat.shape, bf16),
        in_specs=[vmem] * (1 + len(early)),
        out_specs=vmem,
        compiler_params=limit,
        name="early",
    )(home_row, *[returned[k] for k in early])
    filtered = pl.pallas_call(
        functools.partial(home_kernel, late_groups),
        out_shape=jax.ShapeDtypeStruct(flat.shape, bf16),
        in_specs=[vmem] * (2 + len(late)),
        out_specs=pl.BlockSpec(memory_space=pl.ANY),
        scratch_shapes=[
            pltpu.VMEM((flat.shape[0] // 256, 256, points), bf16),
            pltpu.SemaphoreType.DMA((flat.shape[0] // 256,)),
        ],
        compiler_params=limit,
        name="home",
    )(home_row, begun, *[returned[k] for k in late])
    return (filtered.reshape(coeffs.shape), gram_band)


def solution(mesh):
    placed = (P(AXES, None, None), P(), P(), P(AXES, None))
    return jax.shard_map(
        on_device,
        mesh=mesh,
        in_specs=placed,
        out_specs=(P(AXES, None, None), P(AXES, None)),
        check_vma=False,
    )
```

```python
import functools
import itertools

import jax
import jax.numpy as jnp
import numpy as np
from jax import lax
from jax.experimental import pallas as pl
from jax.experimental.pallas import tpu as pltpu
from jax.sharding import PartitionSpec as P

AXES = ("func", "box")
REACH = 3
SLOT = 32
STEP = 8


def passed_along(value, steps):
    count = lax.axis_size(AXES)
    pairs = [(source, (source + steps) % count) for source in range(count)]
    return lax.ppermute(value, AXES, pairs)


def sent(values, keys, sign):
    return {k: passed_along(values[k], sign * k) for k in keys}


def all_sent(values, now, last, sign):
    there = sent(values, now, sign)
    value, there[now[0]] = lax.optimization_barrier((values[last], there[now[0]]))
    there[last] = passed_along(value, sign * last)
    return there


def rounded_up(value, multiple):
    return -(-int(value) // multiple) * multiple


@functools.lru_cache(maxsize=None)
def bounds(fun_dev, support):
    box_dev = fun_dev // 2
    orders = [
        order
        for order in sorted(set(itertools.permutations((1, 1, 2, 4))))
        if np.abs(np.cumsum(np.array(order) - 2)).max() <= 1
    ]
    box_all, fun_all = 12 * support, 24 * support
    assert fun_all % fun_dev == 0
    devices = fun_all // fun_dev
    rows = np.zeros(2 * REACH + 1, np.int64)
    low, high, boxes, end = 10**6, -(10**6), 0, 0
    for picks in itertools.product(orders, repeat=3):
        density = np.repeat(np.concatenate(picks), support)
        centers = np.repeat(np.arange(box_all), density)
        load = sum(np.roll(density, t) for t in range(support))
        below = np.concatenate([[0], np.cumsum(np.tile(load, 3))])
        over = np.clip(np.arange(box_all)[:, None] + support - box_all, 0, None)
        carried = int((over[:, 0] * density).sum())
        below = below - carried
        twice = below[:-1] + below[1:]
        cut = np.array([
            np.searchsorted(twice, 2 * support * fun_dev * (devices + d), side="right")
            for d in range(-REACH - 1, devices + REACH + 2)
        ]) - box_all
        first = REACH + 1
        width = np.diff(cut)
        place = cut - box_dev * (np.arange(len(cut)) - first)
        low, high = min(low, place.min()), max(high, place.max())
        boxes = max(boxes, width.max())
        end = max(end, (place[:-1] + width).max())
        box = centers[:, None] + np.arange(support)
        owner = np.searchsorted(cut, box, side="right") - 1 - first
        device = np.arange(fun_all)[:, None] // fun_dev
        offset = owner - device
        assert np.abs(offset).max() <= REACH
        count = np.bincount((device * (2 * REACH + 1) + offset + REACH).ravel(), minlength=devices * (2 * REACH + 1))
        rows = np.maximum(rows, count.reshape(devices, -1).max(0))
    return (
        tuple(int(r) for r in rows),
        int(low),
        int(high),
        rounded_up(boxes, STEP),
        -(-int(end) // box_dev),
    )


def iota(shape, dim):
    return lax.broadcasted_iota(jnp.int32, shape, dim).astype(jnp.float32)


def one_hot(mask):
    return jnp.where(mask, 1.0, 0.0).astype(jnp.bfloat16)


def spread_over(column, to):
    return jnp.sum(jnp.where(iota((column.shape[0], to.shape[1]), 0) == to, column, 0.0), axis=0, keepdims=True)


def times(a, b, dims=((1,), (0,)), precision=None):
    return lax.dot_general(
        a, b, (dims, ((), ())), precision=precision, preferred_element_type=jnp.float32
    )


def pack_kernel(plan, me_ref, centers_ref, flat_hbm, *refs):
    fun_dev, support, devices, halo, back, low_cut, high_cut, now = plan
    outs = dict(zip(now, refs[: len(now)]))
    near_ref, cut_ref, home_ref, row_ref, flat_ref, sem = refs[len(now) :]
    copy = pltpu.make_async_copy(flat_hbm, flat_ref, sem)
    copy.start()
    me = me_ref[0]
    box_dev = fun_dev // 2
    fun_all, box_all = fun_dev * devices, box_dev * devices
    count = near_ref.shape[0]

    start = me * fun_dev - halo * fun_dev
    start = jnp.where(start < 0, start + fun_all, start).astype(jnp.float32)
    at = start + iota((count, 1), 0)
    at = jnp.where(at >= fun_all, at - fun_all, at)
    near = jnp.sum(
        jnp.where(iota((count, fun_all), 1) == at, centers_ref[...].astype(jnp.float32)[None, :], 0.0), axis=1, keepdims=True
    )
    near = near - (me * box_dev).astype(jnp.float32)
    near = jnp.where(near < -(box_all // 2), near + box_all, near)
    near = jnp.where(near >= box_all // 2, near - box_all, near)
    near_row = spread_over(near, iota((1, count), 1))
    near_ref[...] = jnp.broadcast_to(near, near_ref.shape)

    tries = high_cut - low_cut + 1
    trial = iota((rounded_up(tries, 8), 1), 0)
    cuts = []
    for k in range(-REACH, REACH + 2):
        gap = trial + float(low_cut + k * box_dev) - near_row
        twice = jnp.sum(
            jnp.clip(gap, 0.0, support) + jnp.clip(gap + 1.0, 0.0, support), axis=1, keepdims=True
        )
        goal = float(2 * support * fun_dev * (halo + k))
        passed = jnp.where((twice <= goal) & (trial < tries), 1.0, 0.0)
        cut = jnp.sum(passed) + float(low_cut + k * box_dev)
        cuts.append(cut)
        cut_ref[k + REACH] = cut.astype(jnp.int32)

    mine = near[halo * fun_dev : (halo + 1) * fun_dev]
    pieces = fun_dev * support
    piece = lax.broadcasted_iota(jnp.int32, (1, pieces), 1)
    of_fun = lax.shift_right_logical(piece, support.bit_length() - 1).astype(jnp.float32)
    step = piece.astype(jnp.float32) - of_fun * support
    mine_row = spread_over(mine, of_fun)
    earlier = iota((fun_dev, pieces), 0) < of_fun
    home, base = jnp.zeros((1, pieces), jnp.float32), 0
    for k in range(-REACH, REACH + 1):
        first, end = cuts[k + REACH], cuts[k + REACH + 1]
        leave = jnp.clip(end - mine, 0.0, support) - jnp.clip(first - mine, 0.0, support)
        leave_at = jnp.sum(jnp.where(earlier, leave, 0.0), axis=0, keepdims=True)
        low_edge = jnp.clip(first - mine_row, 0.0, support)
        goes = (step >= low_edge) & (step < jnp.clip(end - mine_row, 0.0, support))
        row = leave_at + step - low_edge
        home = home + jnp.where(goes, row + float(base), 0.0)
        base += back[k + REACH]
        row_ref[k + REACH : k + REACH + 1] = jnp.where(goes, row, -1.0)
    row_ref[2 * REACH + 1 :] = jnp.full((row_ref.shape[0] - 2 * REACH - 1, pieces), -1.0, jnp.float32)
    home_ref[...] = home
    copy.wait()
    for k, out_ref in outs.items():
        row = row_ref[k + REACH : k + REACH + 1]
        pick = one_hot(iota((out_ref.shape[0], pieces), 0) == row)
        out_ref[...] = times(pick, flat_ref[...]).astype(jnp.bfloat16)


def picked(start, low, high, first, rows):
    lane = iota((SLOT, rows), 1)
    picks = []
    for b in range(STEP):
        box = first + float(b)
        row = jnp.where((box >= low) & (box < high), start + box, -1.0)
        picks.append(one_hot(lane == row))
    return jnp.concatenate(picks, axis=0)


def table_kernel(plan, cut_ref, near_ref, flat_ref, column_ref, place_ref, active_ref, local_ref):
    fun_dev, support, halo, boxes = plan
    slots = 2 * REACH + 1
    first = cut_ref[REACH].astype(jnp.float32)
    end = cut_ref[REACH + 1].astype(jnp.float32)
    lane = iota((SLOT, 128), 1)
    along = lax.broadcasted_iota(jnp.int32, (1, boxes * SLOT), 1)
    box = lax.shift_right_logical(along, SLOT.bit_length() - 1).astype(jnp.float32)
    of_fun = along.astype(jnp.float32) - box * SLOT
    levels = [1] * (boxes // STEP)
    for e in range(slots):
        at = (halo - REACH + e) * fun_dev
        others = near_ref[at : at + fun_dev, 0:1]
        edge_low = jnp.clip(first - others, 0.0, support)
        edge_high = jnp.clip(end - others, 0.0, support)
        come = edge_high - edge_low
        come_row = spread_over(come, lane[:1])
        come_at = jnp.sum(
            jnp.where(lane[:fun_dev] < iota((fun_dev, 128), 0), come_row, 0.0), axis=1, keepdims=True
        )
        box_low = edge_low + others - first
        box_high = edge_high + others - first
        packed = come_at - box_low
        spare = jnp.zeros((SLOT - fun_dev, 1), jnp.float32)
        if e == REACH:
            own_start = iota((fun_dev, 1), 0) * support + first - others
            own_start = jnp.concatenate([own_start, spare], axis=0)
        packed, box_low, box_high = (
            jnp.concatenate([column, spare], axis=0) for column in (packed, box_low, box_high)
        )
        if e == REACH:
            for g in range(boxes // STEP):
                pick = picked(own_start, box_low, box_high, float(g * STEP), flat_ref.shape[0])
                local_ref[g * STEP : (g + 1) * STEP] = times(pick, flat_ref[...]).astype(jnp.bfloat16).reshape(
                    STEP, SLOT, flat_ref.shape[1]
                )
        column_ref[e * SLOT : (e + 1) * SLOT, :] = jnp.where(
            lane == 0.0, packed, jnp.where(lane == 1.0, box_low, box_high)
        )
        lies = (box >= spread_over(box_low, of_fun)) & (box < spread_over(box_high, of_fun))
        place = jnp.where(lies, spread_over(packed, of_fun) + box, -1.0)
        for g in range(boxes // STEP):
            place_ref[g, e : e + 1, :] = place[:, g * STEP * SLOT : (g + 1) * STEP * SLOT]
            here = (box >= g * STEP) & (box < (g + 1) * STEP) & lies
            used = jnp.sum(jnp.where(here, 1.0, 0.0)).astype(jnp.int32)
            active_ref[e * (boxes // STEP) + g] = used
            level = jnp.where(used > 0, max(1, abs(e - REACH)), 1)
            levels[g] = jnp.maximum(levels[g], level)
    for g in range(boxes // STEP):
        active_ref[slots * (boxes // STEP) + g] = levels[g]
    spare = place_ref.shape[1] - slots
    place_ref[:, slots:, :] = jnp.full((boxes // STEP, spare, STEP * SLOT), -1.0, jnp.float32)


def function_of(shape, dim, fun_dev):
    row = lax.broadcasted_iota(jnp.int32, shape, dim)
    slot = lax.shift_right_logical(row, SLOT.bit_length() - 1)
    in_slot = row - slot * SLOT
    return jnp.where(in_slot < fun_dev, slot * fun_dev + in_slot, -1)


def moved(value, shift):
    return pltpu.roll(value, shift % value.shape[1], 1)


def skewed(value, sign):
    row = lax.broadcasted_iota(jnp.int32, value.shape, 0)
    bit = 1
    while bit < value.shape[0]:
        value = jnp.where((row & bit) != 0, moved(value, sign * bit), value)
        bit *= 2
    return value


def band_lanes(fun_dev, reading):
    window = (2 * REACH + 1) * fun_dev
    return rounded_up(window + reading + fun_dev + max(0, window - reading), 128)


def level_rows(level):
    return (REACH - level) * SLOT, (REACH + level + 1) * SLOT


def unpack_kernel(plan, cut_ref, active_ref, column_ref, potential_ref, local_ref, *refs):
    fun_dev, reading, volume, back = plan
    slots = 2 * REACH + 1
    sources = refs[:REACH] + (None,) + refs[REACH : slots - 1]
    window_ref = refs[slots - 1]
    gram_refs = refs[slots : 2 * slots]
    dense = refs[2 * slots]
    totals = refs[2 * slots + 1 :]
    steps = window_ref.shape[0] // STEP
    width = cut_ref[REACH + 1] - cut_ref[REACH]

    for total in totals:
        total[...] = jnp.zeros_like(total)
    @pl.loop(0, lax.div(width + STEP - 1, STEP))
    def _(step):
        here_rows = pl.ds(step * STEP, STEP)
        level = active_ref[slots * steps + step]
        window_ref[here_rows, REACH * SLOT : (REACH + 1) * SLOT, :] = local_ref[here_rows]
        for e in range(slots):
            if e == REACH:
                continue
            used = active_ref[e * steps + step] > 0

            @pl.when(used)
            def _():
                start = column_ref[e * SLOT : (e + 1) * SLOT, 0:1]
                low = column_ref[e * SLOT : (e + 1) * SLOT, 1:2]
                high = column_ref[e * SLOT : (e + 1) * SLOT, 2:3]
                pick = picked(start, low, high, (step * STEP).astype(jnp.float32), back[e])
                found = times(pick, sources[e][: back[e]])
                window_ref[here_rows, e * SLOT : (e + 1) * SLOT, :] = found.astype(jnp.bfloat16).reshape(
                    STEP, SLOT, found.shape[-1]
                )

            @pl.when(jnp.logical_not(used) & (level >= abs(e - REACH)))
            def _():
                window_ref[here_rows, e * SLOT : (e + 1) * SLOT, :] = jnp.zeros(
                    (STEP, SLOT, window_ref.shape[-1]), jnp.bfloat16
                )
        for part, total in enumerate(totals):
            @pl.when(level == part + 1)
            def _():
                low, high = level_rows(part + 1)
                value = total[...]
                for b in range(STEP):
                    here = window_ref[step * STEP + b, low:high]
                    value = value + times(here, here, ((1,), (1,)))
                total[...] = value

    wide, lanes = dense.shape
    keep = jnp.where(
        function_of((wide, lanes), 0, fun_dev) == lax.broadcasted_iota(jnp.int32, (wide, lanes), 1), volume, 0.0
    )
    dense[...] = times(totals[-1][...], keep, precision=lax.Precision.HIGHEST)
    for part, total in enumerate(totals[:-1]):
        low, high = level_rows(part + 1)
        dense[low:high] += times(total[...], keep[low:high], precision=lax.Precision.HIGHEST)
    for e in range(slots):
        rows_here = dense[e * SLOT : e * SLOT + fun_dev]
        gram_refs[e][:fun_dev] = skewed(moved(rows_here, reading - 1 - e * fun_dev), -1)[:, : 2 * reading]
        if e < REACH:
            box_dev, points = potential_ref.shape
            gram_refs[e][fun_dev:] = jnp.zeros((gram_refs[e].shape[0] - fun_dev, 2 * reading), jnp.float32)
            for q in range(points // (2 * reading)):
                at = fun_dev + q * 16
                gram_refs[e][at : at + box_dev] = potential_ref[:, q * 2 * reading : (q + 1) * 2 * reading]


def region_kernel(fun_dev, cut_ref, potential_ref, *refs):
    blocks, region_ref = refs[:-1], refs[-1]
    box_dev = potential_ref.shape[0]
    first = cut_ref[REACH].astype(jnp.float32)
    shape = (region_ref.shape[0], box_dev)
    row, col = iota(shape, 0), iota(shape, 1)
    lanes = blocks[0].shape[1]
    for q in range(potential_ref.shape[1] // lanes):
        value = None
        for t in range(1 + len(blocks)):
            if t == 0:
                held = potential_ref[:, q * lanes : (q + 1) * lanes]
            else:
                held = blocks[t - 1][fun_dev + q * 16 : fun_dev + q * 16 + box_dev]
            high = held.astype(jnp.bfloat16)
            low = (held - high.astype(jnp.float32)).astype(jnp.bfloat16)
            at_high = (row < SLOT) & (col == first + row - t * box_dev)
            at_low = (row >= SLOT) & (row < 2 * SLOT) & (col == first + row - SLOT - t * box_dev)
            term = times(one_hot(at_high), high) + times(one_hot(at_low), low)
            value = term if value is None else value + term
        region_ref[:, q * lanes : (q + 1) * lanes] = value.astype(jnp.bfloat16)


def sum_kernel(reading, *refs):
    gram_ref, mixing_ref = refs[-2:]
    count = gram_ref.shape[0]
    value = refs[0][...]
    for ref in refs[1:-2]:
        value = value + ref[:count]
    gram_ref[...] = value
    diagonal = jnp.where(lax.broadcasted_iota(jnp.int32, value.shape, 1) == reading - 1, 1.5, 0.0)
    row = diagonal - 0.5 * value
    spare = jnp.zeros((mixing_ref.shape[0] - row.shape[0], row.shape[1]), jnp.float32)
    mixing_ref[...] = jnp.concatenate([row, spare], axis=0).astype(jnp.bfloat16)


def in_level(group, level):
    at = [place for place, e in enumerate(group) if abs(e - REACH) <= level]
    assert not at or at == list(range(at[0], at[-1] + 1))
    return (at[0], at[-1] + 1) if at else (0, 0)


def mix_kernel(plan, cut_ref, active_ref, place_ref, window_ref, region_ref, kinetic_ref, *refs):
    fun_dev, reading, group, whole = plan
    count = len(group)
    bands = refs[:count]
    outs = refs[count : 2 * count]
    at_boxes = refs[2 * count : 3 * count]
    mixed = refs[3 * count]
    mixings = dict(zip([v for v in range(1, REACH + 1) if in_level(group, v)[1]], refs[3 * count + 1 :]))
    slots = 2 * REACH + 1
    steps = window_ref.shape[0] // STEP
    width = cut_ref[REACH + 1] - cut_ref[REACH]
    for out, at_box in zip(outs, at_boxes):
        out[...] = jnp.zeros_like(out)
        at_box[...] = jnp.zeros_like(at_box)
    lanes = band_lanes(fun_dev, reading)
    parts = []
    for e, band_ref in zip(group, bands):
        band = band_ref[...].astype(jnp.float32)
        band = jnp.concatenate([band, jnp.zeros((SLOT, lanes - 2 * reading), jnp.float32)], axis=1)
        parts.append(moved(skewed(band, 1), e * fun_dev - (reading - 1)).astype(jnp.bfloat16))
    for level, mixing in mixings.items():
        start, end = in_level(group, level)
        shape = (lanes, mixing.shape[1])
        column = function_of(shape, 1, fun_dev)
        column = jnp.where(column >= 0, column + level_rows(level)[0] // SLOT * fun_dev, -1)
        keep = one_hot(column == lax.broadcasted_iota(jnp.int32, shape, 0))
        mixing[...] = times(jnp.concatenate(parts[start:end], axis=0), keep).astype(jnp.bfloat16)

    @pl.loop(0, lax.div(width + STEP - 1, STEP))
    def _(step):
        for level, mixing in mixings.items():
            @pl.when(active_ref[slots * steps + step] == level)
            def _():
                low, high = level_rows(level)
                start, end = in_level(group, level)
                for b in range(STEP):
                    here = window_ref[step * STEP + b, low:high]
                    mixed[b, start * SLOT : end * SLOT] = times(mixing[...], here).astype(jnp.bfloat16)
        shape = (STEP * SLOT, at_boxes[0].shape[1])
        along = lax.broadcasted_iota(jnp.int32, shape, 0)
        box = lax.shift_right_logical(along, SLOT.bit_length() - 1) + step * STEP
        col = lax.broadcasted_iota(jnp.int32, shape, 1)
        boxes_of = one_hot((col == box) | (col == box + SLOT))
        for at, e in enumerate(group):
            @pl.when(active_ref[e * steps + step] > 0)
            def _():
                place = place_ref[step, e : e + 1, :]
                pick = one_hot(iota((outs[at].shape[0], STEP * SLOT), 0) == place)
                part = mixed[:, at * SLOT : (at + 1) * SLOT, :].reshape(STEP * SLOT, mixed.shape[-1])
                outs[at][...] += times(pick, part).astype(jnp.bfloat16)
                at_boxes[at][...] += times(pick, boxes_of).astype(jnp.bfloat16)

    for at, e in enumerate(group):
        if e in whole:
            here = outs[at][...]
            applied = times(here, kinetic_ref[...])
            near_by = times(at_boxes[at][...], region_ref[...])
            outs[at][...] = (applied + near_by * here.astype(jnp.float32)).astype(jnp.bfloat16)


def home_rows(bases, home_ref, sources, at, count):
    shape = (count, home_ref.shape[1])
    here = iota(shape, 1) == iota(shape, 0) + float(at)
    row = jnp.sum(jnp.where(here, home_ref[...], 0.0), axis=1, keepdims=True)
    value = None
    for base, group in bases:
        parts = [sources[at][...] for at in group]
        held = parts[0] if len(parts) == 1 else jnp.concatenate(parts, axis=0)
        pick = one_hot(iota((count, held.shape[0]), 1) == row - float(base))
        term = times(pick, held)
        value = term if value is None else value + term
    return value


def early_kernel(bases, home_ref, *refs):
    sources, out_ref = refs[:-1], refs[-1]
    count = 256
    for at in range(0, out_ref.shape[0], count):
        out_ref[at : at + count] = home_rows(bases, home_ref, sources, at, count).astype(jnp.bfloat16)


def home_kernel(bases, home_ref, early_ref, *refs):
    sources, out_ref, held, sems = refs[:-3], refs[-3], refs[-2], refs[-1]
    copies = []
    count = held.shape[1]
    for part in range(held.shape[0]):
        at = part * count
        value = home_rows(bases, home_ref, sources, at, count) + early_ref[at : at + count].astype(jnp.float32)
        held[part] = value.astype(jnp.bfloat16)
        copy = pltpu.make_async_copy(held.at[part], out_ref.at[pl.ds(at, count)], sems.at[part])
        copy.start()
        copies.append(copy)
    for copy in copies:
        copy.wait()


def on_device(coeffs, centers, kinetic, potential):
    fun_dev, support, points = coeffs.shape
    devices = lax.axis_size(AXES)
    me = lax.axis_index(AXES).astype(jnp.int32).reshape(1)
    box_dev = fun_dev // 2
    volume = 1.0 / (support * points)
    reading = 4 * support
    slots = 2 * REACH + 1
    offsets = list(range(-REACH, REACH + 1))
    last = -REACH
    now = [sign * k for k in range(1, REACH) for sign in (-1, 1)] + [REACH]
    one_way = list(range(REACH, 0, -1)) + list(range(-REACH, 0))
    rows, low_cut, high_cut, boxes, blocks = bounds(fun_dev, support)
    assert blocks <= REACH + 1 and support & (support - 1) == 0
    back = tuple(rounded_up(r, 16) for r in rows)
    rows_of = {k: back[k + REACH] for k in offsets}
    flat = coeffs.reshape(fun_dev * support, points)
    halo = REACH + -(-(reading + 8) // fun_dev)
    count = rounded_up((2 * halo + 2) * fun_dev, 128)
    bf16, f32 = jnp.bfloat16, jnp.float32
    smem = pl.BlockSpec(memory_space=pltpu.SMEM)
    vmem = pl.BlockSpec(memory_space=pltpu.VMEM)
    limit = pltpu.CompilerParams(vmem_limit_bytes=26 * 2**20)

    *packed, near, cut, home_row = pl.pallas_call(
        functools.partial(pack_kernel, (fun_dev, support, devices, halo, back, low_cut, high_cut, now + [last])),
        out_shape=tuple(jax.ShapeDtypeStruct((rows_of[k], points), bf16) for k in now + [last])
        + (
            jax.ShapeDtypeStruct((count, 128), f32),
            jax.ShapeDtypeStruct((slots + 1,), jnp.int32),
            jax.ShapeDtypeStruct((1, fun_dev * support), f32),
        ),
        in_specs=[smem, vmem, pl.BlockSpec(memory_space=pltpu.HBM)],
        out_specs=(vmem,) * slots + (smem, vmem),
        scratch_shapes=[
            pltpu.VMEM((8, fun_dev * support), f32),
            pltpu.VMEM(flat.shape, bf16),
            pltpu.SemaphoreType.DMA,
        ],
        compiler_params=pltpu.CompilerParams(vmem_limit_bytes=52 * 2**20),
        name="pack",
    )(me, centers, flat)
    arrived = all_sent(dict(zip(now + [last], packed)), now, last, 1)

    columns, places, active, local = pl.pallas_call(
        functools.partial(table_kernel, (fun_dev, support, halo, boxes)),
        out_shape=(
            jax.ShapeDtypeStruct((slots * SLOT, 128), f32),
            jax.ShapeDtypeStruct((boxes // STEP, 8, STEP * SLOT), f32),
            jax.ShapeDtypeStruct(((slots + 1) * (boxes // STEP),), jnp.int32),
            jax.ShapeDtypeStruct((boxes, SLOT, points), bf16),
        ),
        in_specs=[smem, vmem, vmem],
        out_specs=(vmem, vmem, smem, vmem),
        compiler_params=limit,
        name="tables",
    )(cut, near, flat)

    wide = slots * SLOT
    sources = [arrived[REACH - e] for e in range(slots) if e != REACH]
    read_rows = [rows_of[REACH - e] for e in range(slots)]
    level_sizes = [level_rows(part + 1)[1] - level_rows(part + 1)[0] for part in range(REACH)]
    level_sizes = [level_rows(part + 1)[1] - level_rows(part + 1)[0] for part in range(REACH)]
    exact_rows = [rows[2 * REACH - e] for e in range(slots)]
    band = (fun_dev, 2 * reading)
    with_potential = (fun_dev + 16 * (points // (2 * reading)), 2 * reading)
    assert box_dev <= 16
    pieces, *grams = pl.pallas_call(
        functools.partial(unpack_kernel, (fun_dev, reading, volume, read_rows)),
        out_shape=(jax.ShapeDtypeStruct((boxes, wide, points), bf16),)
        + tuple(jax.ShapeDtypeStruct(with_potential if e < REACH else band, f32) for e in range(slots)),
        in_specs=[smem, smem] + [vmem] * (3 + len(sources)),
        out_specs=(vmem,) * (1 + slots),
        scratch_shapes=[pltpu.VMEM((wide, band_lanes(fun_dev, reading)), f32)]
        + [pltpu.VMEM((size, size), f32) for size in level_sizes],
        compiler_params=limit,
        name="unpack",
    )(cut, active, columns, potential, local, *sources)

    summed = sent({k: grams[REACH + k] for k in one_way}, one_way, 1)
    gram_band, mixing_rows = pl.pallas_call(
        functools.partial(sum_kernel, reading),
        out_shape=(jax.ShapeDtypeStruct(band, f32), jax.ShapeDtypeStruct((SLOT, 2 * reading), bf16)),
        in_specs=[vmem] * slots,
        out_specs=(vmem, vmem),
        compiler_params=limit,
        name="sum",
    )(grams[REACH], *[summed[k] for k in one_way])
    region = pl.pallas_call(
        functools.partial(region_kernel, fun_dev),
        out_shape=jax.ShapeDtypeStruct((128, points), bf16),
        in_specs=[smem] + [vmem] * blocks,
        out_specs=vmem,
        compiler_params=limit,
        name="region",
    )(cut, potential, *[summed[-t] for t in range(1, blocks)])
    mixing_of = sent({k: mixing_rows for k in one_way}, one_way, 1)
    mixing_of[0] = mixing_rows

    ready, at_boxes = {}, {}
    for group, whole in [([2, -2, REACH, -REACH], [2, -2, REACH, -REACH]), ([0, 1, -1], [1, -1])]:
        group, whole = sorted(REACH - k for k in group), [REACH - k for k in whole]
        shapes = [(rows_of[REACH - e], points) for e in group] + [(rows_of[REACH - e], 128) for e in group]
        sizes = [
            ((in_level(group, v)[1] - in_level(group, v)[0]) * SLOT, level_sizes[v - 1])
            for v in range(1, REACH + 1)
            if in_level(group, v)[1]
        ]
        if ready:
            cut, *held = lax.optimization_barrier((cut, *[ready[k] for k in ready]))
            ready = dict(zip(ready, held))
        mixed = pl.pallas_call(
            functools.partial(mix_kernel, (fun_dev, reading, group, whole)),
            out_shape=tuple(jax.ShapeDtypeStruct(shape, bf16) for shape in shapes),
            in_specs=[smem, smem] + [vmem] * (4 + len(group)),
            out_specs=(vmem,) * len(shapes),
            scratch_shapes=[pltpu.VMEM((STEP, len(group) * SLOT, points), bf16)]
            + [pltpu.VMEM(size, bf16) for size in sizes],
            compiler_params=limit,
            cost_estimate=pl.CostEstimate(
                flops=8 * wide * len(group) * SLOT * boxes * points, bytes_accessed=40 * 2**20, transcendentals=0
            ),
            name="mix",
        )(cut, active, places, pieces, region, kinetic, *[mixing_of[REACH - e] for e in group])
        for at, e in enumerate(group):
            ready[REACH - e], at_boxes[REACH - e] = mixed[at], mixed[len(group) + at]
            if e not in whole:
                near_by = jnp.dot(at_boxes[REACH - e], region, preferred_element_type=f32)
                applied = jnp.dot(mixed[at], kinetic, preferred_element_type=f32)
                ready[REACH - e] = (applied + near_by * mixed[at].astype(f32)).astype(bf16)
    returned = all_sent(ready, [2, -2, 1, -1, REACH], -REACH, -1)
    returned[0] = ready[0]

    bases = {k: sum(back[: k + REACH]) for k in offsets}
    early, late = [0, -1, 1], [k for k in offsets if abs(k) > 1]
    early_groups = [(bases[k], [at]) for at, k in enumerate(early)]
    late_groups = [(bases[-REACH], list(range(REACH - 1))), (bases[2], list(range(REACH - 1, 2 * REACH - 2)))]
    begun = pl.pallas_call(
        functools.partial(early_kernel, early_groups),
        out_shape=jax.ShapeDtypeStruct(flat.shape, bf16),
        in_specs=[vmem] * (1 + len(early)),
        out_specs=vmem,
        compiler_params=limit,
        name="early",
    )(home_row, *[returned[k] for k in early])
    filtered = pl.pallas_call(
        functools.partial(home_kernel, late_groups),
        out_shape=jax.ShapeDtypeStruct(flat.shape, bf16),
        in_specs=[vmem] * (2 + len(late)),
        out_specs=pl.BlockSpec(memory_space=pl.ANY),
        scratch_shapes=[
            pltpu.VMEM((flat.shape[0] // 256, 256, points), bf16),
            pltpu.SemaphoreType.DMA((flat.shape[0] // 256,)),
        ],
        compiler_params=limit,
        name="home",
    )(home_row, begun, *[returned[k] for k in late])
    return (filtered.reshape(coeffs.shape), gram_band)


def solution(mesh):
    placed = (P(AXES, None, None), P(), P(), P(AXES, None))
    return jax.shard_map(
        on_device,
        mesh=mesh,
        in_specs=placed,
        out_specs=(P(AXES, None, None), P(AXES, None)),
        check_vma=False,
    )
```

```python
import functools
import itertools

import jax
import jax.numpy as jnp
import numpy as np
from jax import lax
from jax.experimental import pallas as pl
from jax.experimental.pallas import tpu as pltpu
from jax.sharding import PartitionSpec as P

AXES = ("func", "box")
REACH = 3
SLOT = 32
STEP = 8


def passed_along(value, steps):
    count = lax.axis_size(AXES)
    pairs = [(source, (source + steps) % count) for source in range(count)]
    return lax.ppermute(value, AXES, pairs)


def sent(values, keys, sign):
    return {k: passed_along(values[k], sign * k) for k in keys}


def all_sent(values, now, last, sign):
    there = sent(values, now, sign)
    value, there[now[0]] = lax.optimization_barrier((values[last], there[now[0]]))
    there[last] = passed_along(value, sign * last)
    return there


def rounded_up(value, multiple):
    return -(-int(value) // multiple) * multiple


@functools.lru_cache(maxsize=None)
def bounds(fun_dev, support):
    box_dev = fun_dev // 2
    orders = [
        order
        for order in sorted(set(itertools.permutations((1, 1, 2, 4))))
        if np.abs(np.cumsum(np.array(order) - 2)).max() <= 1
    ]
    box_all, fun_all = 12 * support, 24 * support
    assert fun_all % fun_dev == 0
    devices = fun_all // fun_dev
    rows = np.zeros(2 * REACH + 1, np.int64)
    low, high, boxes, end = 10**6, -(10**6), 0, 0
    for picks in itertools.product(orders, repeat=3):
        density = np.repeat(np.concatenate(picks), support)
        centers = np.repeat(np.arange(box_all), density)
        load = sum(np.roll(density, t) for t in range(support))
        below = np.concatenate([[0], np.cumsum(np.tile(load, 3))])
        over = np.clip(np.arange(box_all)[:, None] + support - box_all, 0, None)
        carried = int((over[:, 0] * density).sum())
        below = below - carried
        twice = below[:-1] + below[1:]
        cut = np.array([
            np.searchsorted(twice, 2 * support * fun_dev * (devices + d), side="right")
            for d in range(-REACH - 1, devices + REACH + 2)
        ]) - box_all
        first = REACH + 1
        width = np.diff(cut)
        place = cut - box_dev * (np.arange(len(cut)) - first)
        low, high = min(low, place.min()), max(high, place.max())
        boxes = max(boxes, width.max())
        end = max(end, (place[:-1] + width).max())
        box = centers[:, None] + np.arange(support)
        owner = np.searchsorted(cut, box, side="right") - 1 - first
        device = np.arange(fun_all)[:, None] // fun_dev
        offset = owner - device
        assert np.abs(offset).max() <= REACH
        count = np.bincount((device * (2 * REACH + 1) + offset + REACH).ravel(), minlength=devices * (2 * REACH + 1))
        rows = np.maximum(rows, count.reshape(devices, -1).max(0))
    return (
        tuple(int(r) for r in rows),
        int(low),
        int(high),
        rounded_up(boxes, STEP),
        -(-int(end) // box_dev),
    )


def iota(shape, dim):
    return lax.broadcasted_iota(jnp.int32, shape, dim).astype(jnp.float32)


def one_hot(mask):
    return jnp.where(mask, 1.0, 0.0).astype(jnp.bfloat16)


def spread_over(column, to):
    return jnp.sum(jnp.where(iota((column.shape[0], to.shape[1]), 0) == to, column, 0.0), axis=0, keepdims=True)


def times(a, b, dims=((1,), (0,)), precision=None):
    return lax.dot_general(
        a, b, (dims, ((), ())), precision=precision, preferred_element_type=jnp.float32
    )


def pack_kernel(plan, me_ref, centers_ref, flat_hbm, potential_hbm, *refs):
    fun_dev, support, devices, halo, rows, back, low_cut, high_cut, now = plan
    outs = dict(zip(now, refs[: len(now)]))
    near_ref, cut_ref, home_ref, own_ref, row_ref, flat_ref, potential_ref, sems = refs[len(now) :]
    copies = [
        pltpu.make_async_copy(flat_hbm, flat_ref, sems.at[0]),
        pltpu.make_async_copy(potential_hbm, potential_ref, sems.at[1]),
    ]
    for copy in copies:
        copy.start()
    me = me_ref[0]
    box_dev = fun_dev // 2
    fun_all, box_all = fun_dev * devices, box_dev * devices
    count = near_ref.shape[0]

    start = me * fun_dev - halo * fun_dev
    start = jnp.where(start < 0, start + fun_all, start).astype(jnp.float32)
    at = start + iota((count, 1), 0)
    at = jnp.where(at >= fun_all, at - fun_all, at)
    near = jnp.sum(
        jnp.where(iota((count, fun_all), 1) == at, centers_ref[...].astype(jnp.float32)[None, :], 0.0), axis=1, keepdims=True
    )
    near = near - (me * box_dev).astype(jnp.float32)
    near = jnp.where(near < -(box_all // 2), near + box_all, near)
    near = jnp.where(near >= box_all // 2, near - box_all, near)
    near_row = spread_over(near, iota((1, count), 1))
    near_ref[...] = jnp.broadcast_to(near, near_ref.shape)

    tries = high_cut - low_cut + 1
    trial = iota((rounded_up(tries, 8), 1), 0)
    cuts = []
    for k in range(-REACH, REACH + 2):
        gap = trial + float(low_cut + k * box_dev) - near_row
        twice = jnp.sum(
            jnp.clip(gap, 0.0, support) + jnp.clip(gap + 1.0, 0.0, support), axis=1, keepdims=True
        )
        goal = float(2 * support * fun_dev * (halo + k))
        passed = jnp.where((twice <= goal) & (trial < tries), 1.0, 0.0)
        cut = jnp.sum(passed) + float(low_cut + k * box_dev)
        cuts.append(cut)
        cut_ref[k + REACH] = cut.astype(jnp.int32)

    copies[1].wait()
    potential = potential_ref[...]
    high = potential.astype(jnp.bfloat16)
    low = (potential - high.astype(jnp.float32)).astype(jnp.bfloat16)
    shape = (own_ref.shape[0], box_dev)
    at_high = iota(shape, 0) == iota(shape, 1)
    at_low = iota(shape, 0) - float(shape[0] // 2) == iota(shape, 1)
    own_ref[...] = (times(one_hot(at_high), high) + times(one_hot(at_low), low)).astype(jnp.bfloat16)

    mine = near[halo * fun_dev : (halo + 1) * fun_dev]
    pieces = fun_dev * support
    piece = lax.broadcasted_iota(jnp.int32, (1, pieces), 1)
    of_fun = lax.shift_right_logical(piece, support.bit_length() - 1).astype(jnp.float32)
    step = piece.astype(jnp.float32) - of_fun * support
    mine_row = spread_over(mine, of_fun)
    earlier = iota((fun_dev, pieces), 0) < of_fun
    home, base = jnp.zeros((1, pieces), jnp.float32), 0
    for k in range(-REACH, REACH + 1):
        first, end = cuts[k + REACH], cuts[k + REACH + 1]
        leave = jnp.clip(end - mine, 0.0, support) - jnp.clip(first - mine, 0.0, support)
        leave_at = jnp.sum(jnp.where(earlier, leave, 0.0), axis=0, keepdims=True)
        low_edge = jnp.clip(first - mine_row, 0.0, support)
        goes = (step >= low_edge) & (step < jnp.clip(end - mine_row, 0.0, support))
        row = leave_at + step - low_edge
        home = home + jnp.where(goes, row + float(base), 0.0)
        base += back[k + REACH]
        row_ref[k + REACH : k + REACH + 1] = jnp.where(goes, row, -1.0)
    row_ref[2 * REACH + 1 :] = jnp.full((row_ref.shape[0] - 2 * REACH - 1, pieces), -1.0, jnp.float32)
    home_ref[...] = home
    copies[0].wait()
    packed_rows(rows, box_dev, row_ref, flat_ref, own_ref, outs)


def packed_rows(rows, box_dev, row_ref, flat_ref, own_ref, outs):
    for k, out_ref in outs.items():
        sent = out_ref.shape[0]
        row = row_ref[k + REACH : k + REACH + 1]
        value = times(one_hot(iota((sent, row.shape[1]), 0) == row), flat_ref[...])
        if k < 0:
            shape = (sent, own_ref.shape[0])
            part = iota(shape, 0) - float(rows[k + REACH])
            from_col = jnp.where(part < box_dev, part, part - box_dev + float(shape[1] // 2))
            inside = (part >= 0) & (part < 2 * box_dev)
            value = value + times(one_hot(inside & (iota(shape, 1) == from_col)), own_ref[...])
        out_ref[...] = value.astype(jnp.bfloat16)


def picked(start, low, high, first, rows):
    lane = iota((SLOT, rows), 1)
    picks = []
    for b in range(STEP):
        box = first + float(b)
        row = jnp.where((box >= low) & (box < high), start + box, -1.0)
        picks.append(one_hot(lane == row))
    return jnp.concatenate(picks, axis=0)


def table_kernel(plan, cut_ref, near_ref, flat_ref, column_ref, place_ref, active_ref, local_ref):
    fun_dev, support, halo, boxes = plan
    slots = 2 * REACH + 1
    first = cut_ref[REACH].astype(jnp.float32)
    end = cut_ref[REACH + 1].astype(jnp.float32)
    lane = iota((SLOT, 128), 1)
    along = lax.broadcasted_iota(jnp.int32, (1, boxes * SLOT), 1)
    box = lax.shift_right_logical(along, SLOT.bit_length() - 1).astype(jnp.float32)
    of_fun = along.astype(jnp.float32) - box * SLOT
    levels = [1] * (boxes // STEP)
    for e in range(slots):
        at = (halo - REACH + e) * fun_dev
        others = near_ref[at : at + fun_dev, 0:1]
        edge_low = jnp.clip(first - others, 0.0, support)
        edge_high = jnp.clip(end - others, 0.0, support)
        come = edge_high - edge_low
        come_row = spread_over(come, lane[:1])
        come_at = jnp.sum(
            jnp.where(lane[:fun_dev] < iota((fun_dev, 128), 0), come_row, 0.0), axis=1, keepdims=True
        )
        box_low = edge_low + others - first
        box_high = edge_high + others - first
        packed = come_at - box_low
        spare = jnp.zeros((SLOT - fun_dev, 1), jnp.float32)
        if e == REACH:
            own_start = iota((fun_dev, 1), 0) * support + first - others
            own_start = jnp.concatenate([own_start, spare], axis=0)
        packed, box_low, box_high = (
            jnp.concatenate([column, spare], axis=0) for column in (packed, box_low, box_high)
        )
        if e == REACH:
            for g in range(boxes // STEP):
                pick = picked(own_start, box_low, box_high, float(g * STEP), flat_ref.shape[0])
                local_ref[g * STEP : (g + 1) * STEP] = times(pick, flat_ref[...]).astype(jnp.bfloat16).reshape(
                    STEP, SLOT, flat_ref.shape[1]
                )
        column_ref[e * SLOT : (e + 1) * SLOT, :] = jnp.where(
            lane == 0.0, packed, jnp.where(lane == 1.0, box_low, box_high)
        )
        lies = (box >= spread_over(box_low, of_fun)) & (box < spread_over(box_high, of_fun))
        place = jnp.where(lies, spread_over(packed, of_fun) + box, -1.0)
        for g in range(boxes // STEP):
            place_ref[g, e : e + 1, :] = place[:, g * STEP * SLOT : (g + 1) * STEP * SLOT]
            here = (box >= g * STEP) & (box < (g + 1) * STEP) & lies
            used = jnp.sum(jnp.where(here, 1.0, 0.0)).astype(jnp.int32)
            active_ref[e * (boxes // STEP) + g] = used
            level = jnp.where(used > 0, max(1, abs(e - REACH)), 1)
            levels[g] = jnp.maximum(levels[g], level)
    for g in range(boxes // STEP):
        active_ref[slots * (boxes // STEP) + g] = levels[g]
    spare = place_ref.shape[1] - slots
    place_ref[:, slots:, :] = jnp.full((boxes // STEP, spare, STEP * SLOT), -1.0, jnp.float32)


def function_of(shape, dim, fun_dev):
    row = lax.broadcasted_iota(jnp.int32, shape, dim)
    slot = lax.shift_right_logical(row, SLOT.bit_length() - 1)
    in_slot = row - slot * SLOT
    return jnp.where(in_slot < fun_dev, slot * fun_dev + in_slot, -1)


def moved(value, shift):
    return pltpu.roll(value, shift % value.shape[1], 1)


def skewed(value, sign):
    row = lax.broadcasted_iota(jnp.int32, value.shape, 0)
    bit = 1
    while bit < value.shape[0]:
        value = jnp.where((row & bit) != 0, moved(value, sign * bit), value)
        bit *= 2
    return value


def band_lanes(fun_dev, reading):
    window = (2 * REACH + 1) * fun_dev
    return rounded_up(window + reading + fun_dev + max(0, window - reading), 128)


def level_rows(level):
    return (REACH - level) * SLOT, (REACH + level + 1) * SLOT


def unpack_kernel(plan, cut_ref, active_ref, column_ref, own_ref, local_ref, *refs):
    fun_dev, box_dev, reading, volume, rows, back, blocks = plan
    slots = 2 * REACH + 1
    sources = refs[:REACH] + (None,) + refs[REACH : slots - 1]
    window_ref, region_ref = refs[slots - 1 : slots + 1]
    gram_refs = refs[slots + 1 : 2 * slots + 1]
    dense = refs[2 * slots + 1]
    totals = refs[2 * slots + 2 :]
    steps = window_ref.shape[0] // STEP
    width = cut_ref[REACH + 1] - cut_ref[REACH]

    for total in totals:
        total[...] = jnp.zeros_like(total)
    value = None
    for t in range(blocks):
        held = own_ref if t == 0 else sources[REACH + t]
        at = 0 if t == 0 else rows[REACH + t]
        from_row = at // 16 * 16
        held = held[from_row:]
        second = own_ref.shape[0] // 2 if t == 0 else box_dev
        shape = (region_ref.shape[0], held.shape[0])
        row, col = iota(shape, 0), iota(shape, 1)
        box = row - jnp.where(row >= SLOT, float(SLOT), 0.0) + cut_ref[REACH].astype(jnp.float32) - t * box_dev
        wanted = box + jnp.where(row >= SLOT, float(second), 0.0) + float(at - from_row)
        good = (box >= 0) & (box < box_dev) & (row < 2 * SLOT)
        term = times(one_hot(good & (col == wanted)), held)
        value = term if value is None else value + term
    region_ref[...] = value.astype(jnp.bfloat16)

    @pl.loop(0, lax.div(width + STEP - 1, STEP))
    def _(step):
        here_rows = pl.ds(step * STEP, STEP)
        level = active_ref[slots * steps + step]
        window_ref[here_rows, REACH * SLOT : (REACH + 1) * SLOT, :] = local_ref[here_rows]
        for e in range(slots):
            if e == REACH:
                continue
            used = active_ref[e * steps + step] > 0

            @pl.when(used)
            def _():
                start = column_ref[e * SLOT : (e + 1) * SLOT, 0:1]
                low = column_ref[e * SLOT : (e + 1) * SLOT, 1:2]
                high = column_ref[e * SLOT : (e + 1) * SLOT, 2:3]
                pick = picked(start, low, high, (step * STEP).astype(jnp.float32), back[e])
                found = times(pick, sources[e][: back[e]])
                window_ref[here_rows, e * SLOT : (e + 1) * SLOT, :] = found.astype(jnp.bfloat16).reshape(
                    STEP, SLOT, found.shape[-1]
                )

            @pl.when(jnp.logical_not(used) & (level >= abs(e - REACH)))
            def _():
                window_ref[here_rows, e * SLOT : (e + 1) * SLOT, :] = jnp.zeros(
                    (STEP, SLOT, window_ref.shape[-1]), jnp.bfloat16
                )
        for part, total in enumerate(totals):
            @pl.when(level == part + 1)
            def _():
                low, high = level_rows(part + 1)
                value = total[...]
                for b in range(STEP):
                    here = window_ref[step * STEP + b, low:high]
                    value = value + times(here, here, ((1,), (1,)))
                total[...] = value

    wide, lanes = dense.shape
    keep = jnp.where(
        function_of((wide, lanes), 0, fun_dev) == lax.broadcasted_iota(jnp.int32, (wide, lanes), 1), volume, 0.0
    )
    dense[...] = times(totals[-1][...], keep, precision=lax.Precision.HIGHEST)
    for part, total in enumerate(totals[:-1]):
        low, high = level_rows(part + 1)
        dense[low:high] += times(total[...], keep[low:high], precision=lax.Precision.HIGHEST)
    for e in range(slots):
        rows_here = dense[e * SLOT : e * SLOT + fun_dev]
        gram_refs[e][...] = skewed(moved(rows_here, reading - 1 - e * fun_dev), -1)[:, : 2 * reading]


def sum_kernel(reading, *refs):
    gram_ref, mixing_ref = refs[-2:]
    value = refs[0][...]
    for ref in refs[1:-2]:
        value = value + ref[...]
    gram_ref[...] = value
    diagonal = jnp.where(lax.broadcasted_iota(jnp.int32, value.shape, 1) == reading - 1, 1.5, 0.0)
    row = diagonal - 0.5 * value
    spare = jnp.zeros((mixing_ref.shape[0] - row.shape[0], row.shape[1]), jnp.float32)
    mixing_ref[...] = jnp.concatenate([row, spare], axis=0).astype(jnp.bfloat16)


def in_level(group, level):
    at = [place for place, e in enumerate(group) if abs(e - REACH) <= level]
    assert not at or at == list(range(at[0], at[-1] + 1))
    return (at[0], at[-1] + 1) if at else (0, 0)


def mix_kernel(plan, cut_ref, active_ref, place_ref, window_ref, region_ref, kinetic_ref, *refs):
    fun_dev, reading, group, whole = plan
    count = len(group)
    bands = refs[:count]
    outs = refs[count : 2 * count]
    at_boxes = refs[2 * count : 3 * count]
    mixed = refs[3 * count]
    mixings = dict(zip([v for v in range(1, REACH + 1) if in_level(group, v)[1]], refs[3 * count + 1 :]))
    slots = 2 * REACH + 1
    steps = window_ref.shape[0] // STEP
    width = cut_ref[REACH + 1] - cut_ref[REACH]
    for out, at_box in zip(outs, at_boxes):
        out[...] = jnp.zeros_like(out)
        at_box[...] = jnp.zeros_like(at_box)
    lanes = band_lanes(fun_dev, reading)
    parts = []
    for e, band_ref in zip(group, bands):
        band = band_ref[...].astype(jnp.float32)
        band = jnp.concatenate([band, jnp.zeros((SLOT, lanes - 2 * reading), jnp.float32)], axis=1)
        parts.append(moved(skewed(band, 1), e * fun_dev - (reading - 1)).astype(jnp.bfloat16))
    for level, mixing in mixings.items():
        start, end = in_level(group, level)
        shape = (lanes, mixing.shape[1])
        column = function_of(shape, 1, fun_dev)
        column = jnp.where(column >= 0, column + level_rows(level)[0] // SLOT * fun_dev, -1)
        keep = one_hot(column == lax.broadcasted_iota(jnp.int32, shape, 0))
        mixing[...] = times(jnp.concatenate(parts[start:end], axis=0), keep).astype(jnp.bfloat16)

    @pl.loop(0, lax.div(width + STEP - 1, STEP))
    def _(step):
        for level, mixing in mixings.items():
            @pl.when(active_ref[slots * steps + step] == level)
            def _():
                low, high = level_rows(level)
                start, end = in_level(group, level)
                for b in range(STEP):
                    here = window_ref[step * STEP + b, low:high]
                    mixed[b, start * SLOT : end * SLOT] = times(mixing[...], here).astype(jnp.bfloat16)
        shape = (STEP * SLOT, at_boxes[0].shape[1])
        along = lax.broadcasted_iota(jnp.int32, shape, 0)
        box = lax.shift_right_logical(along, SLOT.bit_length() - 1) + step * STEP
        col = lax.broadcasted_iota(jnp.int32, shape, 1)
        boxes_of = one_hot((col == box) | (col == box + SLOT))
        for at, e in enumerate(group):
            @pl.when(active_ref[e * steps + step] > 0)
            def _():
                place = place_ref[step, e : e + 1, :]
                pick = one_hot(iota((outs[at].shape[0], STEP * SLOT), 0) == place)
                part = mixed[:, at * SLOT : (at + 1) * SLOT, :].reshape(STEP * SLOT, mixed.shape[-1])
                outs[at][...] += times(pick, part).astype(jnp.bfloat16)
                at_boxes[at][...] += times(pick, boxes_of).astype(jnp.bfloat16)

    for at, e in enumerate(group):
        if e in whole:
            here = outs[at][...]
            applied = times(here, kinetic_ref[...])
            near_by = times(at_boxes[at][...], region_ref[...])
            outs[at][...] = (applied + near_by * here.astype(jnp.float32)).astype(jnp.bfloat16)


def home_rows(bases, home_ref, sources, at, count):
    shape = (count, home_ref.shape[1])
    here = iota(shape, 1) == iota(shape, 0) + float(at)
    row = jnp.sum(jnp.where(here, home_ref[...], 0.0), axis=1, keepdims=True)
    value = None
    for base, group in bases:
        parts = [sources[at][...] for at in group]
        held = parts[0] if len(parts) == 1 else jnp.concatenate(parts, axis=0)
        pick = one_hot(iota((count, held.shape[0]), 1) == row - float(base))
        term = times(pick, held)
        value = term if value is None else value + term
    return value


def early_kernel(bases, home_ref, *refs):
    sources, out_ref = refs[:-1], refs[-1]
    count = 256
    for at in range(0, out_ref.shape[0], count):
        out_ref[at : at + count] = home_rows(bases, home_ref, sources, at, count).astype(jnp.bfloat16)


def home_kernel(bases, home_ref, early_ref, *refs):
    sources, out_ref, held, sems = refs[:-3], refs[-3], refs[-2], refs[-1]
    copies = []
    count = held.shape[1]
    for part in range(held.shape[0]):
        at = part * count
        value = home_rows(bases, home_ref, sources, at, count) + early_ref[at : at + count].astype(jnp.float32)
        held[part] = value.astype(jnp.bfloat16)
        copy = pltpu.make_async_copy(held.at[part], out_ref.at[pl.ds(at, count)], sems.at[part])
        copy.start()
        copies.append(copy)
    for copy in copies:
        copy.wait()


def on_device(coeffs, centers, kinetic, potential):
    fun_dev, support, points = coeffs.shape
    devices = lax.axis_size(AXES)
    me = lax.axis_index(AXES).astype(jnp.int32).reshape(1)
    box_dev = fun_dev // 2
    volume = 1.0 / (support * points)
    reading = 4 * support
    slots = 2 * REACH + 1
    offsets = list(range(-REACH, REACH + 1))
    last = -REACH
    now = [sign * k for k in range(1, REACH) for sign in (-1, 1)] + [REACH]
    one_way = list(range(REACH, 0, -1)) + list(range(-REACH, 0))
    rows, low_cut, high_cut, boxes, blocks = bounds(fun_dev, support)
    assert blocks <= REACH + 1 and support & (support - 1) == 0
    back = tuple(rounded_up(r, 16) for r in rows)
    rows_of = {k: back[k + REACH] for k in offsets}
    flat = coeffs.reshape(fun_dev * support, points)
    halo = REACH + -(-(reading + 8) // fun_dev)
    count = rounded_up((2 * halo + 2) * fun_dev, 128)
    bf16, f32 = jnp.bfloat16, jnp.float32
    smem = pl.BlockSpec(memory_space=pltpu.SMEM)
    vmem = pl.BlockSpec(memory_space=pltpu.VMEM)
    limit = pltpu.CompilerParams(vmem_limit_bytes=26 * 2**20)

    half = rounded_up(box_dev, 16)
    sent_rows = {k: rounded_up(rows[k + REACH] + (2 * box_dev if k < 0 else 0), 16) for k in offsets if k}
    *packed, near, cut, home_row, own_region = pl.pallas_call(
        functools.partial(pack_kernel, (fun_dev, support, devices, halo, rows, back, low_cut, high_cut, now + [last])),
        out_shape=tuple(jax.ShapeDtypeStruct((sent_rows[k], points), bf16) for k in now + [last])
        + (
            jax.ShapeDtypeStruct((count, 128), f32),
            jax.ShapeDtypeStruct((slots + 1,), jnp.int32),
            jax.ShapeDtypeStruct((1, fun_dev * support), f32),
            jax.ShapeDtypeStruct((2 * half, points), bf16),
        ),
        in_specs=[smem, vmem] + [pl.BlockSpec(memory_space=pltpu.HBM)] * 2,
        out_specs=(vmem,) * slots + (smem,) + (vmem,) * 2,
        scratch_shapes=[
            pltpu.VMEM((8, fun_dev * support), f32),
            pltpu.VMEM(flat.shape, bf16),
            pltpu.VMEM(potential.shape, f32),
            pltpu.SemaphoreType.DMA((2,)),
        ],
        compiler_params=pltpu.CompilerParams(vmem_limit_bytes=52 * 2**20),
        name="pack",
    )(me, centers, flat, potential)
    arrived = all_sent(dict(zip(now + [last], packed)), now, last, 1)

    columns, places, active, local = pl.pallas_call(
        functools.partial(table_kernel, (fun_dev, support, halo, boxes)),
        out_shape=(
            jax.ShapeDtypeStruct((slots * SLOT, 128), f32),
            jax.ShapeDtypeStruct((boxes // STEP, 8, STEP * SLOT), f32),
            jax.ShapeDtypeStruct(((slots + 1) * (boxes // STEP),), jnp.int32),
            jax.ShapeDtypeStruct((boxes, SLOT, points), bf16),
        ),
        in_specs=[smem, vmem, vmem],
        out_specs=(vmem, vmem, smem, vmem),
        compiler_params=limit,
        name="tables",
    )(cut, near, flat)

    wide = slots * SLOT
    sources = [arrived[REACH - e] for e in range(slots) if e != REACH]
    read_rows = [rows_of[REACH - e] for e in range(slots)]
    level_sizes = [level_rows(part + 1)[1] - level_rows(part + 1)[0] for part in range(REACH)]
    level_sizes = [level_rows(part + 1)[1] - level_rows(part + 1)[0] for part in range(REACH)]
    exact_rows = [rows[2 * REACH - e] for e in range(slots)]
    band = (fun_dev, 2 * reading)
    exact_rows = [rows[2 * REACH - e] for e in range(slots)]
    pieces, region, *grams = pl.pallas_call(
        functools.partial(unpack_kernel, (fun_dev, box_dev, reading, volume, exact_rows, read_rows, blocks)),
        out_shape=(
            jax.ShapeDtypeStruct((boxes, wide, points), bf16),
            jax.ShapeDtypeStruct((128, points), bf16),
        )
        + tuple(jax.ShapeDtypeStruct(band, f32) for _ in range(slots)),
        in_specs=[smem, smem] + [vmem] * (3 + len(sources)),
        out_specs=(vmem,) * (2 + slots),
        scratch_shapes=[pltpu.VMEM((wide, band_lanes(fun_dev, reading)), f32)]
        + [pltpu.VMEM((size, size), f32) for size in level_sizes],
        compiler_params=limit,
        name="unpack",
    )(cut, active, columns, own_region, local, *sources)

    summed = sent({k: grams[REACH + k] for k in one_way}, one_way, 1)
    gram_band, mixing_rows = pl.pallas_call(
        functools.partial(sum_kernel, reading),
        out_shape=(jax.ShapeDtypeStruct(band, f32), jax.ShapeDtypeStruct((SLOT, 2 * reading), bf16)),
        in_specs=[vmem] * slots,
        out_specs=(vmem, vmem),
        compiler_params=limit,
        name="sum",
    )(grams[REACH], *[summed[k] for k in one_way])
    mixing_of = sent({k: mixing_rows for k in one_way}, one_way, 1)
    mixing_of[0] = mixing_rows

    ready, at_boxes = {}, {}
    for group, whole in [([2, -2, REACH, -REACH], [2, -2, REACH, -REACH]), ([0, 1, -1], [1, -1])]:
        group, whole = sorted(REACH - k for k in group), [REACH - k for k in whole]
        shapes = [(rows_of[REACH - e], points) for e in group] + [(rows_of[REACH - e], 128) for e in group]
        sizes = [
            ((in_level(group, v)[1] - in_level(group, v)[0]) * SLOT, level_sizes[v - 1])
            for v in range(1, REACH + 1)
            if in_level(group, v)[1]
        ]
        if ready:
            cut, *held = lax.optimization_barrier((cut, *[ready[k] for k in ready]))
            ready = dict(zip(ready, held))
        mixed = pl.pallas_call(
            functools.partial(mix_kernel, (fun_dev, reading, group, whole)),
            out_shape=tuple(jax.ShapeDtypeStruct(shape, bf16) for shape in shapes),
            in_specs=[smem, smem] + [vmem] * (4 + len(group)),
            out_specs=(vmem,) * len(shapes),
            scratch_shapes=[pltpu.VMEM((STEP, len(group) * SLOT, points), bf16)]
            + [pltpu.VMEM(size, bf16) for size in sizes],
            compiler_params=limit,
            cost_estimate=pl.CostEstimate(
                flops=8 * wide * len(group) * SLOT * boxes * points, bytes_accessed=40 * 2**20, transcendentals=0
            ),
            name="mix",
        )(cut, active, places, pieces, region, kinetic, *[mixing_of[REACH - e] for e in group])
        for at, e in enumerate(group):
            ready[REACH - e], at_boxes[REACH - e] = mixed[at], mixed[len(group) + at]
            if e not in whole:
                near_by = jnp.dot(at_boxes[REACH - e], region, preferred_element_type=f32)
                applied = jnp.dot(mixed[at], kinetic, preferred_element_type=f32)
                ready[REACH - e] = (applied + near_by * mixed[at].astype(f32)).astype(bf16)
    returned = all_sent(ready, [2, -2, 1, -1, REACH], -REACH, -1)
    returned[0] = ready[0]

    bases = {k: sum(back[: k + REACH]) for k in offsets}
    early, late = [0, 2, REACH, -2], [-1, 1, -REACH]
    assert bases[REACH] == bases[2] + rows_of[2]
    early_groups = [(bases[0], [0]), (bases[2], [1, 2]), (bases[-2], [3])]
    late_groups = [(bases[k], [at]) for at, k in enumerate(late)]
    begun = pl.pallas_call(
        functools.partial(early_kernel, early_groups),
        out_shape=jax.ShapeDtypeStruct(flat.shape, bf16),
        in_specs=[vmem] * (1 + len(early)),
        out_specs=vmem,
        compiler_params=limit,
        name="early",
    )(home_row, *[returned[k] for k in early])
    filtered = pl.pallas_call(
        functools.partial(home_kernel, late_groups),
        out_shape=jax.ShapeDtypeStruct(flat.shape, bf16),
        in_specs=[vmem] * (2 + len(late)),
        out_specs=pl.BlockSpec(memory_space=pl.ANY),
        scratch_shapes=[
            pltpu.VMEM((flat.shape[0] // 256, 256, points), bf16),
            pltpu.SemaphoreType.DMA((flat.shape[0] // 256,)),
        ],
        compiler_params=limit,
        name="home",
    )(home_row, begun, *[returned[k] for k in late])
    return (filtered.reshape(coeffs.shape), gram_band)


def solution(mesh):
    placed = (P(AXES, None, None), P(), P(), P(AXES, None))
    return jax.shard_map(
        on_device,
        mesh=mesh,
        in_specs=placed,
        out_specs=(P(AXES, None, None), P(AXES, None)),
        check_vma=False,
    )
```

```python
import functools
import itertools

import jax
import jax.numpy as jnp
import numpy as np
from jax import lax
from jax.experimental import pallas as pl
from jax.experimental.pallas import tpu as pltpu
from jax.sharding import PartitionSpec as P

AXES = ("func", "box")
REACH = 3
SLOT = 32
STEP = 8


def passed_along(value, steps):
    count = lax.axis_size(AXES)
    pairs = [(source, (source + steps) % count) for source in range(count)]
    return lax.ppermute(value, AXES, pairs)


def half_of(device, k):
    return (device // (k & -k)) % 2


def swapped(value, k, part):
    count = lax.axis_size(AXES)
    assert count % (2 * (k & -k)) == 0
    pairs = [(d, (d + (k if half_of(d, k) == part else -k)) % count) for d in range(count)]
    return lax.ppermute(value, AXES, pairs)


def sent(values, keys, sign):
    return {k: passed_along(values[k], sign * k) for k in keys}


def all_sent(values, now, last, sign):
    there = sent(values, now, sign)
    value, there[now[0]] = lax.optimization_barrier((values[last], there[now[0]]))
    there[last] = passed_along(value, sign * last)
    return there


def rounded_up(value, multiple):
    return -(-int(value) // multiple) * multiple


@functools.lru_cache(maxsize=None)
def bounds(fun_dev, support):
    box_dev = fun_dev // 2
    orders = [
        order
        for order in sorted(set(itertools.permutations((1, 1, 2, 4))))
        if np.abs(np.cumsum(np.array(order) - 2)).max() <= 1
    ]
    box_all, fun_all = 12 * support, 24 * support
    assert fun_all % fun_dev == 0
    devices = fun_all // fun_dev
    rows = np.zeros(2 * REACH + 1, np.int64)
    low, high, boxes, end = 10**6, -(10**6), 0, 0
    for picks in itertools.product(orders, repeat=3):
        density = np.repeat(np.concatenate(picks), support)
        centers = np.repeat(np.arange(box_all), density)
        load = sum(np.roll(density, t) for t in range(support))
        below = np.concatenate([[0], np.cumsum(np.tile(load, 3))])
        over = np.clip(np.arange(box_all)[:, None] + support - box_all, 0, None)
        carried = int((over[:, 0] * density).sum())
        below = below - carried
        twice = below[:-1] + below[1:]
        cut = np.array([
            np.searchsorted(twice, 2 * support * fun_dev * (devices + d), side="right")
            for d in range(-REACH - 1, devices + REACH + 2)
        ]) - box_all
        first = REACH + 1
        width = np.diff(cut)
        place = cut - box_dev * (np.arange(len(cut)) - first)
        low, high = min(low, place.min()), max(high, place.max())
        boxes = max(boxes, width.max())
        end = max(end, (place[:-1] + width).max())
        box = centers[:, None] + np.arange(support)
        owner = np.searchsorted(cut, box, side="right") - 1 - first
        device = np.arange(fun_all)[:, None] // fun_dev
        offset = owner - device
        assert np.abs(offset).max() <= REACH
        count = np.bincount((device * (2 * REACH + 1) + offset + REACH).ravel(), minlength=devices * (2 * REACH + 1))
        rows = np.maximum(rows, count.reshape(devices, -1).max(0))
    return (
        tuple(int(r) for r in rows),
        int(low),
        int(high),
        rounded_up(boxes, STEP),
        -(-int(end) // box_dev),
    )


def iota(shape, dim):
    return lax.broadcasted_iota(jnp.int32, shape, dim).astype(jnp.float32)


def one_hot(mask):
    return jnp.where(mask, 1.0, 0.0).astype(jnp.bfloat16)


def spread_over(column, to):
    return jnp.sum(jnp.where(iota((column.shape[0], to.shape[1]), 0) == to, column, 0.0), axis=0, keepdims=True)


def times(a, b, dims=((1,), (0,)), precision=None):
    return lax.dot_general(
        a, b, (dims, ((), ())), precision=precision, preferred_element_type=jnp.float32
    )


def pack_kernel(plan, me_ref, centers_ref, flat_hbm, potential_hbm, *refs):
    fun_dev, support, devices, halo, rows, back, low_cut, high_cut, now = plan
    outs = dict(zip(now, refs[: len(now)]))
    near_ref, cut_ref, home_ref, own_ref, row_ref, flat_ref, potential_ref, sems = refs[len(now) :]
    copies = [
        pltpu.make_async_copy(flat_hbm, flat_ref, sems.at[0]),
        pltpu.make_async_copy(potential_hbm, potential_ref, sems.at[1]),
    ]
    for copy in copies:
        copy.start()
    me = me_ref[0]
    box_dev = fun_dev // 2
    fun_all, box_all = fun_dev * devices, box_dev * devices
    count = near_ref.shape[0]

    start = me * fun_dev - halo * fun_dev
    start = jnp.where(start < 0, start + fun_all, start).astype(jnp.float32)
    at = start + iota((count, 1), 0)
    at = jnp.where(at >= fun_all, at - fun_all, at)
    near = jnp.sum(
        jnp.where(iota((count, fun_all), 1) == at, centers_ref[...].astype(jnp.float32)[None, :], 0.0), axis=1, keepdims=True
    )
    near = near - (me * box_dev).astype(jnp.float32)
    near = jnp.where(near < -(box_all // 2), near + box_all, near)
    near = jnp.where(near >= box_all // 2, near - box_all, near)
    near_row = spread_over(near, iota((1, count), 1))
    near_ref[...] = jnp.broadcast_to(near, near_ref.shape)

    tries = high_cut - low_cut + 1
    trial = iota((rounded_up(tries, 8), 1), 0)
    cuts = []
    for k in range(-REACH, REACH + 2):
        gap = trial + float(low_cut + k * box_dev) - near_row
        twice = jnp.sum(
            jnp.clip(gap, 0.0, support) + jnp.clip(gap + 1.0, 0.0, support), axis=1, keepdims=True
        )
        goal = float(2 * support * fun_dev * (halo + k))
        passed = jnp.where((twice <= goal) & (trial < tries), 1.0, 0.0)
        cut = jnp.sum(passed) + float(low_cut + k * box_dev)
        cuts.append(cut)
        cut_ref[k + REACH] = cut.astype(jnp.int32)

    copies[1].wait()
    potential = potential_ref[...]
    high = potential.astype(jnp.bfloat16)
    low = (potential - high.astype(jnp.float32)).astype(jnp.bfloat16)
    shape = (own_ref.shape[0], box_dev)
    at_high = iota(shape, 0) == iota(shape, 1)
    at_low = iota(shape, 0) - float(shape[0] // 2) == iota(shape, 1)
    own_ref[...] = (times(one_hot(at_high), high) + times(one_hot(at_low), low)).astype(jnp.bfloat16)

    mine = near[halo * fun_dev : (halo + 1) * fun_dev]
    pieces = fun_dev * support
    piece = lax.broadcasted_iota(jnp.int32, (1, pieces), 1)
    of_fun = lax.shift_right_logical(piece, support.bit_length() - 1).astype(jnp.float32)
    step = piece.astype(jnp.float32) - of_fun * support
    mine_row = spread_over(mine, of_fun)
    earlier = iota((fun_dev, pieces), 0) < of_fun
    home, base = jnp.zeros((1, pieces), jnp.float32), 0
    for k in range(-REACH, REACH + 1):
        first, end = cuts[k + REACH], cuts[k + REACH + 1]
        leave = jnp.clip(end - mine, 0.0, support) - jnp.clip(first - mine, 0.0, support)
        leave_at = jnp.sum(jnp.where(earlier, leave, 0.0), axis=0, keepdims=True)
        low_edge = jnp.clip(first - mine_row, 0.0, support)
        goes = (step >= low_edge) & (step < jnp.clip(end - mine_row, 0.0, support))
        row = leave_at + step - low_edge
        home = home + jnp.where(goes, row + float(base), 0.0)
        base += back[k + REACH]
        row_ref[k + REACH : k + REACH + 1] = jnp.where(goes, row, -1.0)
    row_ref[2 * REACH + 1 :] = jnp.full((row_ref.shape[0] - 2 * REACH - 1, pieces), -1.0, jnp.float32)
    home_ref[...] = home
    copies[0].wait()
    packed_rows(rows, box_dev, row_ref, flat_ref, own_ref, outs)


def packed_rows(rows, box_dev, row_ref, flat_ref, own_ref, outs):
    for k, out_ref in outs.items():
        sent = out_ref.shape[0]
        row = row_ref[k + REACH : k + REACH + 1]
        value = times(one_hot(iota((sent, row.shape[1]), 0) == row), flat_ref[...])
        if k < 0:
            shape = (sent, own_ref.shape[0])
            part = iota(shape, 0) - float(rows[k + REACH])
            from_col = jnp.where(part < box_dev, part, part - box_dev + float(shape[1] // 2))
            inside = (part >= 0) & (part < 2 * box_dev)
            value = value + times(one_hot(inside & (iota(shape, 1) == from_col)), own_ref[...])
        out_ref[...] = value.astype(jnp.bfloat16)


def picked(start, low, high, first, rows):
    lane = iota((SLOT, rows), 1)
    picks = []
    for b in range(STEP):
        box = first + float(b)
        row = jnp.where((box >= low) & (box < high), start + box, -1.0)
        picks.append(one_hot(lane == row))
    return jnp.concatenate(picks, axis=0)


def table_kernel(plan, cut_ref, near_ref, flat_ref, column_ref, place_ref, active_ref, local_ref):
    fun_dev, support, halo, boxes = plan
    slots = 2 * REACH + 1
    first = cut_ref[REACH].astype(jnp.float32)
    end = cut_ref[REACH + 1].astype(jnp.float32)
    lane = iota((SLOT, 128), 1)
    along = lax.broadcasted_iota(jnp.int32, (1, boxes * SLOT), 1)
    box = lax.shift_right_logical(along, SLOT.bit_length() - 1).astype(jnp.float32)
    of_fun = along.astype(jnp.float32) - box * SLOT
    levels = [1] * (boxes // STEP)
    for e in range(slots):
        at = (halo - REACH + e) * fun_dev
        others = near_ref[at : at + fun_dev, 0:1]
        edge_low = jnp.clip(first - others, 0.0, support)
        edge_high = jnp.clip(end - others, 0.0, support)
        come = edge_high - edge_low
        come_row = spread_over(come, lane[:1])
        come_at = jnp.sum(
            jnp.where(lane[:fun_dev] < iota((fun_dev, 128), 0), come_row, 0.0), axis=1, keepdims=True
        )
        box_low = edge_low + others - first
        box_high = edge_high + others - first
        packed = come_at - box_low
        spare = jnp.zeros((SLOT - fun_dev, 1), jnp.float32)
        if e == REACH:
            own_start = iota((fun_dev, 1), 0) * support + first - others
            own_start = jnp.concatenate([own_start, spare], axis=0)
        packed, box_low, box_high = (
            jnp.concatenate([column, spare], axis=0) for column in (packed, box_low, box_high)
        )
        if e == REACH:
            for g in range(boxes // STEP):
                pick = picked(own_start, box_low, box_high, float(g * STEP), flat_ref.shape[0])
                local_ref[g * STEP : (g + 1) * STEP] = times(pick, flat_ref[...]).astype(jnp.bfloat16).reshape(
                    STEP, SLOT, flat_ref.shape[1]
                )
        column_ref[e * SLOT : (e + 1) * SLOT, :] = jnp.where(
            lane == 0.0, packed, jnp.where(lane == 1.0, box_low, box_high)
        )
        lies = (box >= spread_over(box_low, of_fun)) & (box < spread_over(box_high, of_fun))
        place = jnp.where(lies, spread_over(packed, of_fun) + box, -1.0)
        for g in range(boxes // STEP):
            place_ref[g, e : e + 1, :] = place[:, g * STEP * SLOT : (g + 1) * STEP * SLOT]
            here = (box >= g * STEP) & (box < (g + 1) * STEP) & lies
            used = jnp.sum(jnp.where(here, 1.0, 0.0)).astype(jnp.int32)
            active_ref[e * (boxes // STEP) + g] = used
            level = jnp.where(used > 0, max(1, abs(e - REACH)), 1)
            levels[g] = jnp.maximum(levels[g], level)
    for g in range(boxes // STEP):
        active_ref[slots * (boxes // STEP) + g] = levels[g]
    spare = place_ref.shape[1] - slots
    place_ref[:, slots:, :] = jnp.full((boxes // STEP, spare, STEP * SLOT), -1.0, jnp.float32)


def function_of(shape, dim, fun_dev):
    row = lax.broadcasted_iota(jnp.int32, shape, dim)
    slot = lax.shift_right_logical(row, SLOT.bit_length() - 1)
    in_slot = row - slot * SLOT
    return jnp.where(in_slot < fun_dev, slot * fun_dev + in_slot, -1)


def moved(value, shift):
    return pltpu.roll(value, shift % value.shape[1], 1)


def skewed(value, sign):
    row = lax.broadcasted_iota(jnp.int32, value.shape, 0)
    bit = 1
    while bit < value.shape[0]:
        value = jnp.where((row & bit) != 0, moved(value, sign * bit), value)
        bit *= 2
    return value


def band_lanes(fun_dev, reading):
    window = (2 * REACH + 1) * fun_dev
    return rounded_up(window + reading + fun_dev + max(0, window - reading), 128)


def level_rows(level):
    return (REACH - level) * SLOT, (REACH + level + 1) * SLOT


def unpack_kernel(plan, cut_ref, me_ref, active_ref, column_ref, own_ref, local_ref, *refs):
    fun_dev, box_dev, reading, volume, rows, back, blocks = plan
    slots = 2 * REACH + 1
    sources = refs[:REACH] + (None,) + refs[REACH : slots - 1]
    window_ref, region_ref = refs[slots - 1 : slots + 1]
    gram_refs = refs[slots + 1 : 2 * slots + 1]
    dense = refs[2 * slots + 1]
    totals = refs[2 * slots + 2 :]
    steps = window_ref.shape[0] // STEP
    width = cut_ref[REACH + 1] - cut_ref[REACH]

    for total in totals:
        total[...] = jnp.zeros_like(total)
    value = None
    for t in range(blocks):
        held = own_ref if t == 0 else sources[REACH + t]
        at = 0 if t == 0 else rows[REACH + t]
        from_row = at // 16 * 16
        held = held[from_row:]
        second = own_ref.shape[0] // 2 if t == 0 else box_dev
        shape = (region_ref.shape[0], held.shape[0])
        row, col = iota(shape, 0), iota(shape, 1)
        box = row - jnp.where(row >= SLOT, float(SLOT), 0.0) + cut_ref[REACH].astype(jnp.float32) - t * box_dev
        wanted = box + jnp.where(row >= SLOT, float(second), 0.0) + float(at - from_row)
        good = (box >= 0) & (box < box_dev) & (row < 2 * SLOT)
        term = times(one_hot(good & (col == wanted)), held)
        value = term if value is None else value + term
    region_ref[...] = value.astype(jnp.bfloat16)

    @pl.loop(0, lax.div(width + STEP - 1, STEP))
    def _(step):
        here_rows = pl.ds(step * STEP, STEP)
        level = active_ref[slots * steps + step]
        window_ref[here_rows, REACH * SLOT : (REACH + 1) * SLOT, :] = local_ref[here_rows]
        for e in range(slots):
            if e == REACH:
                continue
            used = active_ref[e * steps + step] > 0

            @pl.when(used)
            def _():
                start = column_ref[e * SLOT : (e + 1) * SLOT, 0:1]
                low = column_ref[e * SLOT : (e + 1) * SLOT, 1:2]
                high = column_ref[e * SLOT : (e + 1) * SLOT, 2:3]
                pick = picked(start, low, high, (step * STEP).astype(jnp.float32), back[e])
                found = times(pick, sources[e][: back[e]])
                window_ref[here_rows, e * SLOT : (e + 1) * SLOT, :] = found.astype(jnp.bfloat16).reshape(
                    STEP, SLOT, found.shape[-1]
                )

            @pl.when(jnp.logical_not(used) & (level >= abs(e - REACH)))
            def _():
                window_ref[here_rows, e * SLOT : (e + 1) * SLOT, :] = jnp.zeros(
                    (STEP, SLOT, window_ref.shape[-1]), jnp.bfloat16
                )
        for part, total in enumerate(totals):
            @pl.when(level == part + 1)
            def _():
                low, high = level_rows(part + 1)
                value = total[...]
                for b in range(STEP):
                    here = window_ref[step * STEP + b, low:high]
                    value = value + times(here, here, ((1,), (1,)))
                total[...] = value

    wide, lanes = dense.shape
    keep = jnp.where(
        function_of((wide, lanes), 0, fun_dev) == lax.broadcasted_iota(jnp.int32, (wide, lanes), 1), volume, 0.0
    )
    dense[...] = times(totals[-1][...], keep, precision=lax.Precision.HIGHEST)
    for part, total in enumerate(totals[:-1]):
        low, high = level_rows(part + 1)
        dense[low:high] += times(total[...], keep[low:high], precision=lax.Precision.HIGHEST)
    bands = []
    for e in range(slots):
        rows_here = dense[e * SLOT : e * SLOT + fun_dev]
        bands.append(skewed(moved(rows_here, reading - 1 - e * fun_dev), -1)[:, : 2 * reading])
    gram_refs[0][...] = bands[REACH]
    for k in range(1, REACH + 1):
        half = lax.rem(lax.div(me_ref[0], k & -k), 2)
        for part in range(2):
            ahead, behind = (REACH + k, REACH - k) if part == 0 else (REACH - k, REACH + k)

            @pl.when(half == part)
            def _():
                gram_refs[2 * k - 1][...] = bands[ahead]
                gram_refs[2 * k][...] = bands[behind]


def sum_kernel(reading, *refs):
    gram_ref, mixing_ref = refs[-2:]
    value = refs[0][...]
    for ref in refs[1:-2]:
        value = value + ref[...]
    gram_ref[...] = value
    diagonal = jnp.where(lax.broadcasted_iota(jnp.int32, value.shape, 1) == reading - 1, 1.5, 0.0)
    row = diagonal - 0.5 * value
    spare = jnp.zeros((mixing_ref.shape[0] - row.shape[0], row.shape[1]), jnp.float32)
    mixing_ref[...] = jnp.concatenate([row, spare], axis=0).astype(jnp.bfloat16)


def in_level(group, level):
    at = [place for place, e in enumerate(group) if abs(e - REACH) <= level]
    assert not at or at == list(range(at[0], at[-1] + 1))
    return (at[0], at[-1] + 1) if at else (0, 0)


def mix_kernel(plan, cut_ref, me_ref, active_ref, place_ref, window_ref, region_ref, kinetic_ref, *refs):
    fun_dev, reading, group, whole, swaps = plan
    count = len(group)
    bands = dict(zip(swaps, refs[:count]))
    outs = refs[count : 2 * count]
    at_boxes = refs[2 * count : 3 * count]
    mixed = refs[3 * count]
    mixings = dict(zip([v for v in range(1, REACH + 1) if in_level(group, v)[1]], refs[3 * count + 1 :]))
    slots = 2 * REACH + 1
    steps = window_ref.shape[0] // STEP
    width = cut_ref[REACH + 1] - cut_ref[REACH]
    for out, at_box in zip(outs, at_boxes):
        out[...] = jnp.zeros_like(out)
        at_box[...] = jnp.zeros_like(at_box)
    lanes = band_lanes(fun_dev, reading)
    parts = []
    for e in group:
        k = abs(e - REACH)
        band = bands[k, 0][...].astype(jnp.float32)
        if k:
            half = lax.rem(lax.div(me_ref[0], k & -k), 2).astype(jnp.float32)
            other = half if e > REACH else 1.0 - half
            band = band * (1.0 - other) + bands[k, 1][...].astype(jnp.float32) * other
        band = jnp.concatenate([band, jnp.zeros((SLOT, lanes - 2 * reading), jnp.float32)], axis=1)
        parts.append(moved(skewed(band, 1), e * fun_dev - (reading - 1)).astype(jnp.bfloat16))
    for level, mixing in mixings.items():
        start, end = in_level(group, level)
        shape = (lanes, mixing.shape[1])
        column = function_of(shape, 1, fun_dev)
        column = jnp.where(column >= 0, column + level_rows(level)[0] // SLOT * fun_dev, -1)
        keep = one_hot(column == lax.broadcasted_iota(jnp.int32, shape, 0))
        mixing[...] = times(jnp.concatenate(parts[start:end], axis=0), keep).astype(jnp.bfloat16)

    @pl.loop(0, lax.div(width + STEP - 1, STEP))
    def _(step):
        for level, mixing in mixings.items():
            @pl.when(active_ref[slots * steps + step] == level)
            def _():
                low, high = level_rows(level)
                start, end = in_level(group, level)
                for b in range(STEP):
                    here = window_ref[step * STEP + b, low:high]
                    mixed[b, start * SLOT : end * SLOT] = times(mixing[...], here).astype(jnp.bfloat16)
        shape = (STEP * SLOT, at_boxes[0].shape[1])
        along = lax.broadcasted_iota(jnp.int32, shape, 0)
        box = lax.shift_right_logical(along, SLOT.bit_length() - 1) + step * STEP
        col = lax.broadcasted_iota(jnp.int32, shape, 1)
        boxes_of = one_hot((col == box) | (col == box + SLOT))
        for at, e in enumerate(group):
            @pl.when(active_ref[e * steps + step] > 0)
            def _():
                place = place_ref[step, e : e + 1, :]
                pick = one_hot(iota((outs[at].shape[0], STEP * SLOT), 0) == place)
                part = mixed[:, at * SLOT : (at + 1) * SLOT, :].reshape(STEP * SLOT, mixed.shape[-1])
                outs[at][...] += times(pick, part).astype(jnp.bfloat16)
                at_boxes[at][...] += times(pick, boxes_of).astype(jnp.bfloat16)

    for at, e in enumerate(group):
        if e in whole:
            here = outs[at][...]
            applied = times(here, kinetic_ref[...])
            near_by = times(at_boxes[at][...], region_ref[...])
            outs[at][...] = (applied + near_by * here.astype(jnp.float32)).astype(jnp.bfloat16)


def home_rows(bases, home_ref, sources, at, count):
    shape = (count, home_ref.shape[1])
    here = iota(shape, 1) == iota(shape, 0) + float(at)
    row = jnp.sum(jnp.where(here, home_ref[...], 0.0), axis=1, keepdims=True)
    value = None
    for base, group in bases:
        parts = [sources[at][...] for at in group]
        held = parts[0] if len(parts) == 1 else jnp.concatenate(parts, axis=0)
        pick = one_hot(iota((count, held.shape[0]), 1) == row - float(base))
        term = times(pick, held)
        value = term if value is None else value + term
    return value


def early_kernel(bases, home_ref, *refs):
    sources, out_ref = refs[:-1], refs[-1]
    count = 256
    for at in range(0, out_ref.shape[0], count):
        out_ref[at : at + count] = home_rows(bases, home_ref, sources, at, count).astype(jnp.bfloat16)


def home_kernel(bases, home_ref, early_ref, *refs):
    sources, out_ref, held, sems = refs[:-3], refs[-3], refs[-2], refs[-1]
    copies = []
    count = held.shape[1]
    for part in range(held.shape[0]):
        at = part * count
        value = home_rows(bases, home_ref, sources, at, count) + early_ref[at : at + count].astype(jnp.float32)
        held[part] = value.astype(jnp.bfloat16)
        copy = pltpu.make_async_copy(held.at[part], out_ref.at[pl.ds(at, count)], sems.at[part])
        copy.start()
        copies.append(copy)
    for copy in copies:
        copy.wait()


def on_device(coeffs, centers, kinetic, potential):
    fun_dev, support, points = coeffs.shape
    devices = lax.axis_size(AXES)
    me = lax.axis_index(AXES).astype(jnp.int32).reshape(1)
    box_dev = fun_dev // 2
    volume = 1.0 / (support * points)
    reading = 4 * support
    slots = 2 * REACH + 1
    offsets = list(range(-REACH, REACH + 1))
    last = -REACH
    now = [sign * k for k in range(1, REACH) for sign in (-1, 1)] + [REACH]
    rows, low_cut, high_cut, boxes, blocks = bounds(fun_dev, support)
    assert blocks <= REACH + 1 and support & (support - 1) == 0
    back = tuple(rounded_up(r, 16) for r in rows)
    rows_of = {k: back[k + REACH] for k in offsets}
    flat = coeffs.reshape(fun_dev * support, points)
    halo = REACH + -(-(reading + 8) // fun_dev)
    count = rounded_up((2 * halo + 2) * fun_dev, 128)
    bf16, f32 = jnp.bfloat16, jnp.float32
    smem = pl.BlockSpec(memory_space=pltpu.SMEM)
    vmem = pl.BlockSpec(memory_space=pltpu.VMEM)
    limit = pltpu.CompilerParams(vmem_limit_bytes=26 * 2**20)

    half = rounded_up(box_dev, 16)
    sent_rows = {k: rounded_up(rows[k + REACH] + (2 * box_dev if k < 0 else 0), 16) for k in offsets if k}
    *packed, near, cut, home_row, own_region = pl.pallas_call(
        functools.partial(pack_kernel, (fun_dev, support, devices, halo, rows, back, low_cut, high_cut, now + [last])),
        out_shape=tuple(jax.ShapeDtypeStruct((sent_rows[k], points), bf16) for k in now + [last])
        + (
            jax.ShapeDtypeStruct((count, 128), f32),
            jax.ShapeDtypeStruct((slots + 1,), jnp.int32),
            jax.ShapeDtypeStruct((1, fun_dev * support), f32),
            jax.ShapeDtypeStruct((2 * half, points), bf16),
        ),
        in_specs=[smem, vmem] + [pl.BlockSpec(memory_space=pltpu.HBM)] * 2,
        out_specs=(vmem,) * slots + (smem,) + (vmem,) * 2,
        scratch_shapes=[
            pltpu.VMEM((8, fun_dev * support), f32),
            pltpu.VMEM(flat.shape, bf16),
            pltpu.VMEM(potential.shape, f32),
            pltpu.SemaphoreType.DMA((2,)),
        ],
        compiler_params=pltpu.CompilerParams(vmem_limit_bytes=52 * 2**20),
        name="pack",
    )(me, centers, flat, potential)
    arrived = all_sent(dict(zip(now + [last], packed)), now, last, 1)

    columns, places, active, local = pl.pallas_call(
        functools.partial(table_kernel, (fun_dev, support, halo, boxes)),
        out_shape=(
            jax.ShapeDtypeStruct((slots * SLOT, 128), f32),
            jax.ShapeDtypeStruct((boxes // STEP, 8, STEP * SLOT), f32),
            jax.ShapeDtypeStruct(((slots + 1) * (boxes // STEP),), jnp.int32),
            jax.ShapeDtypeStruct((boxes, SLOT, points), bf16),
        ),
        in_specs=[smem, vmem, vmem],
        out_specs=(vmem, vmem, smem, vmem),
        compiler_params=limit,
        name="tables",
    )(cut, near, flat)

    wide = slots * SLOT
    sources = [arrived[REACH - e] for e in range(slots) if e != REACH]
    read_rows = [rows_of[REACH - e] for e in range(slots)]
    level_sizes = [level_rows(part + 1)[1] - level_rows(part + 1)[0] for part in range(REACH)]
    level_sizes = [level_rows(part + 1)[1] - level_rows(part + 1)[0] for part in range(REACH)]
    exact_rows = [rows[2 * REACH - e] for e in range(slots)]
    band = (fun_dev, 2 * reading)
    exact_rows = [rows[2 * REACH - e] for e in range(slots)]
    pieces, region, *grams = pl.pallas_call(
        functools.partial(unpack_kernel, (fun_dev, box_dev, reading, volume, exact_rows, read_rows, blocks)),
        out_shape=(
            jax.ShapeDtypeStruct((boxes, wide, points), bf16),
            jax.ShapeDtypeStruct((128, points), bf16),
        )
        + tuple(jax.ShapeDtypeStruct(band, f32) for _ in range(slots)),
        in_specs=[smem] * 3 + [vmem] * (3 + len(sources)),
        out_specs=(vmem,) * (2 + slots),
        scratch_shapes=[pltpu.VMEM((wide, band_lanes(fun_dev, reading)), f32)]
        + [pltpu.VMEM((size, size), f32) for size in level_sizes],
        compiler_params=limit,
        name="unpack",
    )(cut, me, active, columns, own_region, local, *sources)

    swaps = [(k, 0) for k in range(1, REACH + 1)] + [(k, 1) for k in range(REACH, 0, -1)]
    summed = [swapped(grams[2 * k - 1 + part], k, part) for k, part in swaps]
    gram_band, mixing_rows = pl.pallas_call(
        functools.partial(sum_kernel, reading),
        out_shape=(jax.ShapeDtypeStruct(band, f32), jax.ShapeDtypeStruct((SLOT, 2 * reading), bf16)),
        in_specs=[vmem] * slots,
        out_specs=(vmem, vmem),
        compiler_params=limit,
        name="sum",
    )(grams[0], *summed)
    mixing_of = {swap: swapped(mixing_rows, *swap) for swap in swaps}

    mixing_of[0, 0] = mixing_rows
    ready, at_boxes = {}, {}
    for group, whole in [([2, -2, REACH, -REACH], [2, -2, REACH, -REACH]), ([0, 1, -1], [1, -1])]:
        group, whole = sorted(REACH - k for k in group), [REACH - k for k in whole]
        shapes = [(rows_of[REACH - e], points) for e in group] + [(rows_of[REACH - e], 128) for e in group]
        far = {abs(e - REACH) for e in group}
        group_swaps = [swap for swap in [(0, 0)] + swaps if swap[0] in far]
        sizes = [
            ((in_level(group, v)[1] - in_level(group, v)[0]) * SLOT, level_sizes[v - 1])
            for v in range(1, REACH + 1)
            if in_level(group, v)[1]
        ]
        if ready:
            cut, *held = lax.optimization_barrier((cut, *[ready[k] for k in ready]))
            ready = dict(zip(ready, held))
        mixed = pl.pallas_call(
            functools.partial(mix_kernel, (fun_dev, reading, group, whole, group_swaps)),
            out_shape=tuple(jax.ShapeDtypeStruct(shape, bf16) for shape in shapes),
            in_specs=[smem] * 3 + [vmem] * (4 + len(group)),
            out_specs=(vmem,) * len(shapes),
            scratch_shapes=[pltpu.VMEM((STEP, len(group) * SLOT, points), bf16)]
            + [pltpu.VMEM(size, bf16) for size in sizes],
            compiler_params=limit,
            cost_estimate=pl.CostEstimate(
                flops=8 * wide * len(group) * SLOT * boxes * points, bytes_accessed=40 * 2**20, transcendentals=0
            ),
            name="mix",
        )(cut, me, active, places, pieces, region, kinetic, *[mixing_of[swap] for swap in group_swaps])
        for at, e in enumerate(group):
            ready[REACH - e], at_boxes[REACH - e] = mixed[at], mixed[len(group) + at]
            if e not in whole:
                near_by = jnp.dot(at_boxes[REACH - e], region, preferred_element_type=f32)
                applied = jnp.dot(mixed[at], kinetic, preferred_element_type=f32)
                ready[REACH - e] = (applied + near_by * mixed[at].astype(f32)).astype(bf16)
    returned = all_sent(ready, [2, -2, 1, -1, REACH], -REACH, -1)
    returned[0] = ready[0]

    bases = {k: sum(back[: k + REACH]) for k in offsets}
    early, late = [0, 2, REACH, -2], [-1, 1, -REACH]
    assert bases[REACH] == bases[2] + rows_of[2]
    early_groups = [(bases[0], [0]), (bases[2], [1, 2]), (bases[-2], [3])]
    late_groups = [(bases[k], [at]) for at, k in enumerate(late)]
    begun = pl.pallas_call(
        functools.partial(early_kernel, early_groups),
        out_shape=jax.ShapeDtypeStruct(flat.shape, bf16),
        in_specs=[vmem] * (1 + len(early)),
        out_specs=vmem,
        compiler_params=limit,
        name="early",
    )(home_row, *[returned[k] for k in early])
    filtered = pl.pallas_call(
        functools.partial(home_kernel, late_groups),
        out_shape=jax.ShapeDtypeStruct(flat.shape, bf16),
        in_specs=[vmem] * (2 + len(late)),
        out_specs=pl.BlockSpec(memory_space=pl.ANY),
        scratch_shapes=[
            pltpu.VMEM((flat.shape[0] // 256, 256, points), bf16),
            pltpu.SemaphoreType.DMA((flat.shape[0] // 256,)),
        ],
        compiler_params=limit,
        name="home",
    )(home_row, begun, *[returned[k] for k in late])
    return (filtered.reshape(coeffs.shape), gram_band)


def solution(mesh):
    placed = (P(AXES, None, None), P(), P(), P(AXES, None))
    return jax.shard_map(
        on_device,
        mesh=mesh,
        in_specs=placed,
        out_specs=(P(AXES, None, None), P(AXES, None)),
        check_vma=False,
    )
```

```python
import functools
import itertools

import jax
import jax.numpy as jnp
import numpy as np
from jax import lax
from jax.experimental import pallas as pl
from jax.experimental.pallas import tpu as pltpu
from jax.sharding import PartitionSpec as P

AXES = ("func", "box")
REACH = 3
SLOT = 32
STEP = 8


def passed_along(value, steps):
    count = lax.axis_size(AXES)
    pairs = [(source, (source + steps) % count) for source in range(count)]
    return lax.ppermute(value, AXES, pairs)


def half_of(device, k):
    return (device // (k & -k)) % 2


def swapped(value, k, part):
    count = lax.axis_size(AXES)
    assert count % (2 * (k & -k)) == 0
    pairs = [(d, (d + (k if half_of(d, k) == part else -k)) % count) for d in range(count)]
    return lax.ppermute(value, AXES, pairs)


def sent(values, keys, sign):
    return {k: passed_along(values[k], sign * k) for k in keys}


def all_sent(values, now, last, sign):
    there = sent(values, now, sign)
    value, there[now[0]] = lax.optimization_barrier((values[last], there[now[0]]))
    there[last] = passed_along(value, sign * last)
    return there


def rounded_up(value, multiple):
    return -(-int(value) // multiple) * multiple


@functools.lru_cache(maxsize=None)
def bounds(fun_dev, support):
    box_dev = fun_dev // 2
    orders = [
        order
        for order in sorted(set(itertools.permutations((1, 1, 2, 4))))
        if np.abs(np.cumsum(np.array(order) - 2)).max() <= 1
    ]
    box_all, fun_all = 12 * support, 24 * support
    assert fun_all % fun_dev == 0
    devices = fun_all // fun_dev
    rows = np.zeros(2 * REACH + 1, np.int64)
    low, high, boxes, end = 10**6, -(10**6), 0, 0
    for picks in itertools.product(orders, repeat=3):
        density = np.repeat(np.concatenate(picks), support)
        centers = np.repeat(np.arange(box_all), density)
        load = sum(np.roll(density, t) for t in range(support))
        below = np.concatenate([[0], np.cumsum(np.tile(load, 3))])
        over = np.clip(np.arange(box_all)[:, None] + support - box_all, 0, None)
        carried = int((over[:, 0] * density).sum())
        below = below - carried
        twice = below[:-1] + below[1:]
        cut = np.array([
            np.searchsorted(twice, 2 * support * fun_dev * (devices + d), side="right")
            for d in range(-REACH - 1, devices + REACH + 2)
        ]) - box_all
        first = REACH + 1
        width = np.diff(cut)
        place = cut - box_dev * (np.arange(len(cut)) - first)
        low, high = min(low, place.min()), max(high, place.max())
        boxes = max(boxes, width.max())
        end = max(end, (place[:-1] + width).max())
        box = centers[:, None] + np.arange(support)
        owner = np.searchsorted(cut, box, side="right") - 1 - first
        device = np.arange(fun_all)[:, None] // fun_dev
        offset = owner - device
        assert np.abs(offset).max() <= REACH
        count = np.bincount((device * (2 * REACH + 1) + offset + REACH).ravel(), minlength=devices * (2 * REACH + 1))
        rows = np.maximum(rows, count.reshape(devices, -1).max(0))
    return (
        tuple(int(r) for r in rows),
        int(low),
        int(high),
        rounded_up(boxes, STEP),
        -(-int(end) // box_dev),
    )


def iota(shape, dim):
    return lax.broadcasted_iota(jnp.int32, shape, dim).astype(jnp.float32)


def one_hot(mask):
    return jnp.where(mask, 1.0, 0.0).astype(jnp.bfloat16)


def spread_over(column, to):
    return jnp.sum(jnp.where(iota((column.shape[0], to.shape[1]), 0) == to, column, 0.0), axis=0, keepdims=True)


def times(a, b, dims=((1,), (0,)), precision=None):
    return lax.dot_general(
        a, b, (dims, ((), ())), precision=precision, preferred_element_type=jnp.float32
    )


def pack_kernel(plan, me_ref, centers_ref, flat_hbm, potential_hbm, *refs):
    fun_dev, support, devices, halo, rows, back, low_cut, high_cut, now = plan
    outs = dict(zip(now, refs[: len(now)]))
    near_ref, cut_ref, home_ref, own_ref, row_ref, flat_ref, potential_ref, sems = refs[len(now) :]
    copies = [
        pltpu.make_async_copy(flat_hbm, flat_ref, sems.at[0]),
        pltpu.make_async_copy(potential_hbm, potential_ref, sems.at[1]),
    ]
    for copy in copies:
        copy.start()
    me = me_ref[0]
    box_dev = fun_dev // 2
    fun_all, box_all = fun_dev * devices, box_dev * devices
    count = near_ref.shape[0]

    start = me * fun_dev - halo * fun_dev
    start = jnp.where(start < 0, start + fun_all, start).astype(jnp.float32)
    at = start + iota((count, 1), 0)
    at = jnp.where(at >= fun_all, at - fun_all, at)
    near = jnp.sum(
        jnp.where(iota((count, fun_all), 1) == at, centers_ref[...].astype(jnp.float32)[None, :], 0.0), axis=1, keepdims=True
    )
    near = near - (me * box_dev).astype(jnp.float32)
    near = jnp.where(near < -(box_all // 2), near + box_all, near)
    near = jnp.where(near >= box_all // 2, near - box_all, near)
    near_row = spread_over(near, iota((1, count), 1))
    near_ref[...] = jnp.broadcast_to(near, near_ref.shape)

    tries = high_cut - low_cut + 1
    trial = iota((rounded_up(tries, 8), 1), 0)
    cuts = []
    for k in range(-REACH, REACH + 2):
        gap = trial + float(low_cut + k * box_dev) - near_row
        twice = jnp.sum(
            jnp.clip(gap, 0.0, support) + jnp.clip(gap + 1.0, 0.0, support), axis=1, keepdims=True
        )
        goal = float(2 * support * fun_dev * (halo + k))
        passed = jnp.where((twice <= goal) & (trial < tries), 1.0, 0.0)
        cut = jnp.sum(passed) + float(low_cut + k * box_dev)
        cuts.append(cut)
        cut_ref[k + REACH] = cut.astype(jnp.int32)

    copies[1].wait()
    potential = potential_ref[...]
    high = potential.astype(jnp.bfloat16)
    low = (potential - high.astype(jnp.float32)).astype(jnp.bfloat16)
    shape = (own_ref.shape[0], box_dev)
    at_high = iota(shape, 0) == iota(shape, 1)
    at_low = iota(shape, 0) - float(shape[0] // 2) == iota(shape, 1)
    own_ref[...] = (times(one_hot(at_high), high) + times(one_hot(at_low), low)).astype(jnp.bfloat16)

    mine = near[halo * fun_dev : (halo + 1) * fun_dev]
    pieces = fun_dev * support
    piece = lax.broadcasted_iota(jnp.int32, (1, pieces), 1)
    of_fun = lax.shift_right_logical(piece, support.bit_length() - 1).astype(jnp.float32)
    step = piece.astype(jnp.float32) - of_fun * support
    mine_row = spread_over(mine, of_fun)
    earlier = iota((fun_dev, pieces), 0) < of_fun
    home, base = jnp.zeros((1, pieces), jnp.float32), 0
    for k in range(-REACH, REACH + 1):
        first, end = cuts[k + REACH], cuts[k + REACH + 1]
        leave = jnp.clip(end - mine, 0.0, support) - jnp.clip(first - mine, 0.0, support)
        leave_at = jnp.sum(jnp.where(earlier, leave, 0.0), axis=0, keepdims=True)
        low_edge = jnp.clip(first - mine_row, 0.0, support)
        goes = (step >= low_edge) & (step < jnp.clip(end - mine_row, 0.0, support))
        row = leave_at + step - low_edge
        home = home + jnp.where(goes, row + float(base), 0.0)
        base += back[k + REACH]
        row_ref[k + REACH : k + REACH + 1] = jnp.where(goes, row, -1.0)
    row_ref[2 * REACH + 1 :] = jnp.full((row_ref.shape[0] - 2 * REACH - 1, pieces), -1.0, jnp.float32)
    home_ref[...] = home
    copies[0].wait()
    packed_rows(rows, box_dev, row_ref, flat_ref, own_ref, outs)


def packed_rows(rows, box_dev, row_ref, flat_ref, own_ref, outs):
    for k, out_ref in outs.items():
        sent = out_ref.shape[0]
        row = row_ref[k + REACH : k + REACH + 1]
        value = times(one_hot(iota((sent, row.shape[1]), 0) == row), flat_ref[...])
        if k < 0:
            shape = (sent, own_ref.shape[0])
            part = iota(shape, 0) - float(rows[k + REACH])
            from_col = jnp.where(part < box_dev, part, part - box_dev + float(shape[1] // 2))
            inside = (part >= 0) & (part < 2 * box_dev)
            value = value + times(one_hot(inside & (iota(shape, 1) == from_col)), own_ref[...])
        out_ref[...] = value.astype(jnp.bfloat16)


def picked(start, low, high, first, rows):
    lane = iota((SLOT, rows), 1)
    picks = []
    for b in range(STEP):
        box = first + float(b)
        row = jnp.where((box >= low) & (box < high), start + box, -1.0)
        picks.append(one_hot(lane == row))
    return jnp.concatenate(picks, axis=0)


def table_kernel(plan, cut_ref, near_ref, flat_ref, column_ref, place_ref, active_ref, local_ref):
    fun_dev, support, halo, boxes = plan
    slots = 2 * REACH + 1
    first = cut_ref[REACH].astype(jnp.float32)
    end = cut_ref[REACH + 1].astype(jnp.float32)
    lane = iota((SLOT, 128), 1)
    along = lax.broadcasted_iota(jnp.int32, (1, boxes * SLOT), 1)
    box = lax.shift_right_logical(along, SLOT.bit_length() - 1).astype(jnp.float32)
    of_fun = along.astype(jnp.float32) - box * SLOT
    levels = [1] * (boxes // STEP)
    for e in range(slots):
        at = (halo - REACH + e) * fun_dev
        others = near_ref[at : at + fun_dev, 0:1]
        edge_low = jnp.clip(first - others, 0.0, support)
        edge_high = jnp.clip(end - others, 0.0, support)
        come = edge_high - edge_low
        come_row = spread_over(come, lane[:1])
        come_at = jnp.sum(
            jnp.where(lane[:fun_dev] < iota((fun_dev, 128), 0), come_row, 0.0), axis=1, keepdims=True
        )
        box_low = edge_low + others - first
        box_high = edge_high + others - first
        packed = come_at - box_low
        spare = jnp.zeros((SLOT - fun_dev, 1), jnp.float32)
        if e == REACH:
            own_start = iota((fun_dev, 1), 0) * support + first - others
            own_start = jnp.concatenate([own_start, spare], axis=0)
        packed, box_low, box_high = (
            jnp.concatenate([column, spare], axis=0) for column in (packed, box_low, box_high)
        )
        if e == REACH:
            for g in range(boxes // STEP):
                pick = picked(own_start, box_low, box_high, float(g * STEP), flat_ref.shape[0])
                local_ref[g * STEP : (g + 1) * STEP] = times(pick, flat_ref[...]).astype(jnp.bfloat16).reshape(
                    STEP, SLOT, flat_ref.shape[1]
                )
        column_ref[e * SLOT : (e + 1) * SLOT, :] = jnp.where(
            lane == 0.0, packed, jnp.where(lane == 1.0, box_low, box_high)
        )
        lies = (box >= spread_over(box_low, of_fun)) & (box < spread_over(box_high, of_fun))
        place = jnp.where(lies, spread_over(packed, of_fun) + box, -1.0)
        for g in range(boxes // STEP):
            place_ref[g, e : e + 1, :] = place[:, g * STEP * SLOT : (g + 1) * STEP * SLOT]
            here = (box >= g * STEP) & (box < (g + 1) * STEP) & lies
            used = jnp.sum(jnp.where(here, 1.0, 0.0)).astype(jnp.int32)
            active_ref[e * (boxes // STEP) + g] = used
            level = jnp.where(used > 0, max(1, abs(e - REACH)), 1)
            levels[g] = jnp.maximum(levels[g], level)
    for g in range(boxes // STEP):
        active_ref[slots * (boxes // STEP) + g] = levels[g]
    spare = place_ref.shape[1] - slots
    place_ref[:, slots:, :] = jnp.full((boxes // STEP, spare, STEP * SLOT), -1.0, jnp.float32)


def function_of(shape, dim, fun_dev):
    row = lax.broadcasted_iota(jnp.int32, shape, dim)
    slot = lax.shift_right_logical(row, SLOT.bit_length() - 1)
    in_slot = row - slot * SLOT
    return jnp.where(in_slot < fun_dev, slot * fun_dev + in_slot, -1)


def moved(value, shift):
    return pltpu.roll(value, shift % value.shape[1], 1)


def skewed(value, sign):
    row = lax.broadcasted_iota(jnp.int32, value.shape, 0)
    bit = 1
    while bit < value.shape[0]:
        value = jnp.where((row & bit) != 0, moved(value, sign * bit), value)
        bit *= 2
    return value


def band_lanes(fun_dev, reading):
    window = (2 * REACH + 1) * fun_dev
    return rounded_up(window + reading + fun_dev + max(0, window - reading), 128)


def level_rows(level):
    return (REACH - level) * SLOT, (REACH + level + 1) * SLOT


def unpack_kernel(plan, cut_ref, me_ref, active_ref, column_ref, own_ref, local_ref, *refs):
    fun_dev, box_dev, reading, volume, rows, back, blocks = plan
    slots = 2 * REACH + 1
    sources = refs[:REACH] + (None,) + refs[REACH : slots - 1]
    window_ref, region_ref = refs[slots - 1 : slots + 1]
    gram_refs = refs[slots + 1 : 2 * slots + 1]
    dense = refs[2 * slots + 1]
    totals = refs[2 * slots + 2 :]
    steps = window_ref.shape[0] // STEP
    width = cut_ref[REACH + 1] - cut_ref[REACH]

    for total in totals:
        total[...] = jnp.zeros_like(total)
    value = None
    for t in range(blocks):
        held = own_ref if t == 0 else sources[REACH + t]
        at = 0 if t == 0 else rows[REACH + t]
        from_row = at // 16 * 16
        held = held[from_row:]
        second = own_ref.shape[0] // 2 if t == 0 else box_dev
        shape = (region_ref.shape[0], held.shape[0])
        row, col = iota(shape, 0), iota(shape, 1)
        box = row - jnp.where(row >= SLOT, float(SLOT), 0.0) + cut_ref[REACH].astype(jnp.float32) - t * box_dev
        wanted = box + jnp.where(row >= SLOT, float(second), 0.0) + float(at - from_row)
        good = (box >= 0) & (box < box_dev) & (row < 2 * SLOT)
        term = times(one_hot(good & (col == wanted)), held)
        value = term if value is None else value + term
    region_ref[...] = value.astype(jnp.bfloat16)

    @pl.loop(0, lax.div(width + STEP - 1, STEP))
    def _(step):
        here_rows = pl.ds(step * STEP, STEP)
        level = active_ref[slots * steps + step]
        window_ref[here_rows, REACH * SLOT : (REACH + 1) * SLOT, :] = local_ref[here_rows]
        for e in range(slots):
            if e == REACH:
                continue
            used = active_ref[e * steps + step] > 0

            @pl.when(used)
            def _():
                start = column_ref[e * SLOT : (e + 1) * SLOT, 0:1]
                low = column_ref[e * SLOT : (e + 1) * SLOT, 1:2]
                high = column_ref[e * SLOT : (e + 1) * SLOT, 2:3]
                pick = picked(start, low, high, (step * STEP).astype(jnp.float32), back[e])
                found = times(pick, sources[e][: back[e]])
                window_ref[here_rows, e * SLOT : (e + 1) * SLOT, :] = found.astype(jnp.bfloat16).reshape(
                    STEP, SLOT, found.shape[-1]
                )

            @pl.when(jnp.logical_not(used) & (level >= abs(e - REACH)))
            def _():
                window_ref[here_rows, e * SLOT : (e + 1) * SLOT, :] = jnp.zeros(
                    (STEP, SLOT, window_ref.shape[-1]), jnp.bfloat16
                )
        for part, total in enumerate(totals):
            @pl.when(level == part + 1)
            def _():
                low, high = level_rows(part + 1)
                value = total[...]
                for b in range(STEP):
                    here = window_ref[step * STEP + b, low:high]
                    value = value + times(here, here, ((1,), (1,)))
                total[...] = value

    wide, lanes = dense.shape
    keep = jnp.where(
        function_of((wide, lanes), 0, fun_dev) == lax.broadcasted_iota(jnp.int32, (wide, lanes), 1), volume, 0.0
    )
    dense[...] = times(totals[-1][...], keep, precision=lax.Precision.HIGHEST)
    for part, total in enumerate(totals[:-1]):
        low, high = level_rows(part + 1)
        dense[low:high] += times(total[...], keep[low:high], precision=lax.Precision.HIGHEST)
    bands = []
    for e in range(slots):
        rows_here = dense[e * SLOT : e * SLOT + fun_dev]
        bands.append(skewed(moved(rows_here, reading - 1 - e * fun_dev), -1)[:, : 2 * reading])
    gram_refs[0][...] = bands[REACH]
    for k in range(1, REACH + 1):
        half = lax.rem(lax.div(me_ref[0], k & -k), 2)
        for part in range(2):
            ahead, behind = (REACH + k, REACH - k) if part == 0 else (REACH - k, REACH + k)

            @pl.when(half == part)
            def _():
                gram_refs[2 * k - 1][...] = bands[ahead]
                gram_refs[2 * k][...] = bands[behind]


def sum_kernel(reading, *refs):
    gram_ref, mixing_ref = refs[-2:]
    value = refs[0][...]
    for ref in refs[1:-2]:
        value = value + ref[...]
    gram_ref[...] = value
    diagonal = jnp.where(lax.broadcasted_iota(jnp.int32, value.shape, 1) == reading - 1, 1.5, 0.0)
    row = diagonal - 0.5 * value
    spare = jnp.zeros((mixing_ref.shape[0] - row.shape[0], row.shape[1]), jnp.float32)
    mixing_ref[...] = jnp.concatenate([row, spare], axis=0).astype(jnp.bfloat16)


def in_level(group, level):
    at = [place for place, e in enumerate(group) if abs(e - REACH) <= level]
    assert not at or at == list(range(at[0], at[-1] + 1))
    return (at[0], at[-1] + 1) if at else (0, 0)


def mix_kernel(plan, cut_ref, me_ref, active_ref, place_ref, window_ref, region_ref, kinetic_ref, *refs):
    fun_dev, reading, group, whole, swaps = plan
    count = len(group)
    bands = dict(zip(swaps, refs[:count]))
    swap_outs = refs[count : 2 * count]
    at_boxes = refs[2 * count : 3 * count]
    mixed = refs[3 * count]
    levels = [v for v in range(1, REACH + 1) if in_level(group, v)[1]]
    mixings = dict(zip(levels, refs[3 * count + 1 :]))
    held = iter(refs[3 * count + 1 + len(levels) :])
    outs = [swap_outs[at] if e == REACH else next(held) for at, e in enumerate(group)]
    slots = 2 * REACH + 1
    steps = window_ref.shape[0] // STEP
    width = cut_ref[REACH + 1] - cut_ref[REACH]
    for out, at_box in zip(outs, at_boxes):
        out[...] = jnp.zeros_like(out)
        at_box[...] = jnp.zeros_like(at_box)
    lanes = band_lanes(fun_dev, reading)
    parts = []
    for e in group:
        k = abs(e - REACH)
        band = bands[k, 0][...].astype(jnp.float32)
        if k:
            half = lax.rem(lax.div(me_ref[0], k & -k), 2).astype(jnp.float32)
            other = half if e > REACH else 1.0 - half
            band = band * (1.0 - other) + bands[k, 1][...].astype(jnp.float32) * other
        band = jnp.concatenate([band, jnp.zeros((SLOT, lanes - 2 * reading), jnp.float32)], axis=1)
        parts.append(moved(skewed(band, 1), e * fun_dev - (reading - 1)).astype(jnp.bfloat16))
    for level, mixing in mixings.items():
        start, end = in_level(group, level)
        shape = (lanes, mixing.shape[1])
        column = function_of(shape, 1, fun_dev)
        column = jnp.where(column >= 0, column + level_rows(level)[0] // SLOT * fun_dev, -1)
        keep = one_hot(column == lax.broadcasted_iota(jnp.int32, shape, 0))
        mixing[...] = times(jnp.concatenate(parts[start:end], axis=0), keep).astype(jnp.bfloat16)

    @pl.loop(0, lax.div(width + STEP - 1, STEP))
    def _(step):
        for level, mixing in mixings.items():
            @pl.when(active_ref[slots * steps + step] == level)
            def _():
                low, high = level_rows(level)
                start, end = in_level(group, level)
                for b in range(STEP):
                    here = window_ref[step * STEP + b, low:high]
                    mixed[b, start * SLOT : end * SLOT] = times(mixing[...], here).astype(jnp.bfloat16)
        shape = (STEP * SLOT, at_boxes[0].shape[1])
        along = lax.broadcasted_iota(jnp.int32, shape, 0)
        box = lax.shift_right_logical(along, SLOT.bit_length() - 1) + step * STEP
        col = lax.broadcasted_iota(jnp.int32, shape, 1)
        boxes_of = one_hot((col == box) | (col == box + SLOT))
        for at, e in enumerate(group):
            @pl.when(active_ref[e * steps + step] > 0)
            def _():
                place = place_ref[step, e : e + 1, :]
                pick = one_hot(iota((outs[at].shape[0], STEP * SLOT), 0) == place)
                part = mixed[:, at * SLOT : (at + 1) * SLOT, :].reshape(STEP * SLOT, mixed.shape[-1])
                outs[at][...] += times(pick, part).astype(jnp.bfloat16)
                at_boxes[at][...] += times(pick, boxes_of).astype(jnp.bfloat16)

    for at, e in enumerate(group):
        if e in whole:
            here = outs[at][...]
            applied = times(here, kinetic_ref[...])
            near_by = times(at_boxes[at][...], region_ref[...])
            outs[at][...] = (applied + near_by * here.astype(jnp.float32)).astype(jnp.bfloat16)
    for k in sorted({abs(e - REACH) for e in group} - {0}):
        behind, ahead = group.index(REACH - k), group.index(REACH + k)
        half = lax.rem(lax.div(me_ref[0], k & -k), 2)
        for part, first, second in ((0, ahead, behind), (1, behind, ahead)):
            @pl.when(half == part)
            def _():
                swap_outs[behind][...] = outs[first][...]
                swap_outs[ahead][...] = outs[second][...]


def home_rows(bases, me_ref, home_ref, sources, at, count):
    shape = (count, home_ref.shape[1])
    here = iota(shape, 1) == iota(shape, 0) + float(at)
    row = jnp.sum(jnp.where(here, home_ref[...], 0.0), axis=1, keepdims=True)
    value = None
    for (ahead, behind, k, part), source in zip(bases, sources):
        base = float(ahead)
        if k:
            half = lax.rem(lax.div(me_ref[0], k & -k), 2)
            base = jnp.where(half == part, ahead, behind).astype(jnp.float32)
        pick = one_hot(iota((count, source.shape[0]), 1) == row - base)
        term = times(pick, source[...])
        value = term if value is None else value + term
    return value


def early_kernel(bases, me_ref, home_ref, *refs):
    sources, out_ref = refs[:-1], refs[-1]
    count = 256
    for at in range(0, out_ref.shape[0], count):
        out_ref[at : at + count] = home_rows(bases, me_ref, home_ref, sources, at, count).astype(jnp.bfloat16)


def home_kernel(bases, me_ref, home_ref, early_ref, *refs):
    sources, out_ref, held, sems = refs[:-3], refs[-3], refs[-2], refs[-1]
    copies = []
    count = held.shape[1]
    for part in range(held.shape[0]):
        at = part * count
        value = home_rows(bases, me_ref, home_ref, sources, at, count) + early_ref[at : at + count].astype(jnp.float32)
        held[part] = value.astype(jnp.bfloat16)
        copy = pltpu.make_async_copy(held.at[part], out_ref.at[pl.ds(at, count)], sems.at[part])
        copy.start()
        copies.append(copy)
    for copy in copies:
        copy.wait()


def on_device(coeffs, centers, kinetic, potential):
    fun_dev, support, points = coeffs.shape
    devices = lax.axis_size(AXES)
    me = lax.axis_index(AXES).astype(jnp.int32).reshape(1)
    box_dev = fun_dev // 2
    volume = 1.0 / (support * points)
    reading = 4 * support
    slots = 2 * REACH + 1
    offsets = list(range(-REACH, REACH + 1))
    last = -REACH
    now = [sign * k for k in range(1, REACH) for sign in (-1, 1)] + [REACH]
    rows, low_cut, high_cut, boxes, blocks = bounds(fun_dev, support)
    assert blocks <= REACH + 1 and support & (support - 1) == 0
    back = tuple(rounded_up(r, 16) for r in rows)
    rows_of = {k: back[k + REACH] for k in offsets}
    flat = coeffs.reshape(fun_dev * support, points)
    halo = REACH + -(-(reading + 8) // fun_dev)
    count = rounded_up((2 * halo + 2) * fun_dev, 128)
    bf16, f32 = jnp.bfloat16, jnp.float32
    smem = pl.BlockSpec(memory_space=pltpu.SMEM)
    vmem = pl.BlockSpec(memory_space=pltpu.VMEM)
    limit = pltpu.CompilerParams(vmem_limit_bytes=26 * 2**20)

    half = rounded_up(box_dev, 16)
    sent_rows = {k: rounded_up(rows[k + REACH] + (2 * box_dev if k < 0 else 0), 16) for k in offsets if k}
    *packed, near, cut, home_row, own_region = pl.pallas_call(
        functools.partial(pack_kernel, (fun_dev, support, devices, halo, rows, back, low_cut, high_cut, now + [last])),
        out_shape=tuple(jax.ShapeDtypeStruct((sent_rows[k], points), bf16) for k in now + [last])
        + (
            jax.ShapeDtypeStruct((count, 128), f32),
            jax.ShapeDtypeStruct((slots + 1,), jnp.int32),
            jax.ShapeDtypeStruct((1, fun_dev * support), f32),
            jax.ShapeDtypeStruct((2 * half, points), bf16),
        ),
        in_specs=[smem, vmem] + [pl.BlockSpec(memory_space=pltpu.HBM)] * 2,
        out_specs=(vmem,) * slots + (smem,) + (vmem,) * 2,
        scratch_shapes=[
            pltpu.VMEM((8, fun_dev * support), f32),
            pltpu.VMEM(flat.shape, bf16),
            pltpu.VMEM(potential.shape, f32),
            pltpu.SemaphoreType.DMA((2,)),
        ],
        compiler_params=pltpu.CompilerParams(vmem_limit_bytes=52 * 2**20),
        name="pack",
    )(me, centers, flat, potential)
    arrived = all_sent(dict(zip(now + [last], packed)), now, last, 1)

    columns, places, active, local = pl.pallas_call(
        functools.partial(table_kernel, (fun_dev, support, halo, boxes)),
        out_shape=(
            jax.ShapeDtypeStruct((slots * SLOT, 128), f32),
            jax.ShapeDtypeStruct((boxes // STEP, 8, STEP * SLOT), f32),
            jax.ShapeDtypeStruct(((slots + 1) * (boxes // STEP),), jnp.int32),
            jax.ShapeDtypeStruct((boxes, SLOT, points), bf16),
        ),
        in_specs=[smem, vmem, vmem],
        out_specs=(vmem, vmem, smem, vmem),
        compiler_params=limit,
        name="tables",
    )(cut, near, flat)

    wide = slots * SLOT
    sources = [arrived[REACH - e] for e in range(slots) if e != REACH]
    read_rows = [rows_of[REACH - e] for e in range(slots)]
    level_sizes = [level_rows(part + 1)[1] - level_rows(part + 1)[0] for part in range(REACH)]
    level_sizes = [level_rows(part + 1)[1] - level_rows(part + 1)[0] for part in range(REACH)]
    exact_rows = [rows[2 * REACH - e] for e in range(slots)]
    band = (fun_dev, 2 * reading)
    exact_rows = [rows[2 * REACH - e] for e in range(slots)]
    pieces, region, *grams = pl.pallas_call(
        functools.partial(unpack_kernel, (fun_dev, box_dev, reading, volume, exact_rows, read_rows, blocks)),
        out_shape=(
            jax.ShapeDtypeStruct((boxes, wide, points), bf16),
            jax.ShapeDtypeStruct((128, points), bf16),
        )
        + tuple(jax.ShapeDtypeStruct(band, f32) for _ in range(slots)),
        in_specs=[smem] * 3 + [vmem] * (3 + len(sources)),
        out_specs=(vmem,) * (2 + slots),
        scratch_shapes=[pltpu.VMEM((wide, band_lanes(fun_dev, reading)), f32)]
        + [pltpu.VMEM((size, size), f32) for size in level_sizes],
        compiler_params=limit,
        name="unpack",
    )(cut, me, active, columns, own_region, local, *sources)

    swaps = [(k, 0) for k in range(1, REACH + 1)] + [(k, 1) for k in range(REACH, 0, -1)]
    summed = [swapped(grams[2 * k - 1 + part], k, part) for k, part in swaps]
    gram_band, mixing_rows = pl.pallas_call(
        functools.partial(sum_kernel, reading),
        out_shape=(jax.ShapeDtypeStruct(band, f32), jax.ShapeDtypeStruct((SLOT, 2 * reading), bf16)),
        in_specs=[vmem] * slots,
        out_specs=(vmem, vmem),
        compiler_params=limit,
        name="sum",
    )(grams[0], *summed)
    mixing_of = {swap: swapped(mixing_rows, *swap) for swap in swaps}

    mixing_of[0, 0] = mixing_rows
    ready, at_boxes = {}, {}
    for group, whole in [([2, -2, REACH, -REACH], [2, -2, REACH, -REACH]), ([0, 1, -1], [1, -1])]:
        group, whole = sorted(REACH - k for k in group), [REACH - k for k in whole]
        most = [max(rows_of[REACH - e], rows_of[e - REACH]) for e in group]
        shapes = [(r, points) for r in most] + [(r, 128) for r in most]
        far = {abs(e - REACH) for e in group}
        group_swaps = [swap for swap in [(0, 0)] + swaps if swap[0] in far]
        sizes = [
            ((in_level(group, v)[1] - in_level(group, v)[0]) * SLOT, level_sizes[v - 1])
            for v in range(1, REACH + 1)
            if in_level(group, v)[1]
        ]
        if ready:
            cut, *held = lax.optimization_barrier((cut, *[ready[k] for k in ready]))
            ready = dict(zip(ready, held))
        mixed = pl.pallas_call(
            functools.partial(mix_kernel, (fun_dev, reading, group, whole, group_swaps)),
            out_shape=tuple(jax.ShapeDtypeStruct(shape, bf16) for shape in shapes),
            in_specs=[smem] * 3 + [vmem] * (4 + len(group)),
            out_specs=(vmem,) * len(shapes),
            scratch_shapes=[pltpu.VMEM((STEP, len(group) * SLOT, points), bf16)]
            + [pltpu.VMEM(size, bf16) for size in sizes]
            + [pltpu.VMEM((r, points), bf16) for r, e in zip(most, group) if e != REACH],
            compiler_params=limit,
            cost_estimate=pl.CostEstimate(
                flops=8 * wide * len(group) * SLOT * boxes * points, bytes_accessed=40 * 2**20, transcendentals=0
            ),
            name="mix",
        )(cut, me, active, places, pieces, region, kinetic, *[mixing_of[swap] for swap in group_swaps])
        for at, e in enumerate(group):
            key = (abs(e - REACH), int(e > REACH))
            ready[key], at_boxes[key] = mixed[at], mixed[len(group) + at]
            if e not in whole:
                near_by = jnp.dot(at_boxes[key], region, preferred_element_type=f32)
                applied = jnp.dot(mixed[at], kinetic, preferred_element_type=f32)
                ready[key] = (applied + near_by * mixed[at].astype(f32)).astype(bf16)
    far = (REACH, 1)
    returned = {swap: swapped(ready[swap], *swap) for swap in swaps if swap != far}
    value, returned[2, 0] = lax.optimization_barrier((ready[far], returned[2, 0]))
    returned[far] = swapped(value, *far)
    returned[0, 0] = ready[0, 0]

    bases = {k: sum(back[: k + REACH]) for k in offsets}
    early, late = [(0, 0), (2, 0), (2, 1), (REACH, 0)], [(1, 0), (1, 1), far]
    early_bases = [(bases[k], bases[-k], k, part) for k, part in early]
    late_bases = [(bases[k], bases[-k], k, part) for k, part in late]
    begun = pl.pallas_call(
        functools.partial(early_kernel, early_bases),
        out_shape=jax.ShapeDtypeStruct(flat.shape, bf16),
        in_specs=[smem] + [vmem] * (1 + len(early)),
        out_specs=vmem,
        compiler_params=limit,
        name="early",
    )(me, home_row, *[returned[swap] for swap in early])
    filtered = pl.pallas_call(
        functools.partial(home_kernel, late_bases),
        out_shape=jax.ShapeDtypeStruct(flat.shape, bf16),
        in_specs=[smem] + [vmem] * (2 + len(late)),
        out_specs=pl.BlockSpec(memory_space=pl.ANY),
        scratch_shapes=[
            pltpu.VMEM((flat.shape[0] // 256, 256, points), bf16),
            pltpu.SemaphoreType.DMA((flat.shape[0] // 256,)),
        ],
        compiler_params=limit,
        name="home",
    )(me, home_row, begun, *[returned[swap] for swap in late])
    return (filtered.reshape(coeffs.shape), gram_band)


def solution(mesh):
    placed = (P(AXES, None, None), P(), P(), P(AXES, None))
    return jax.shard_map(
        on_device,
        mesh=mesh,
        in_specs=placed,
        out_specs=(P(AXES, None, None), P(AXES, None)),
        check_vma=False,
    )
```

```python
import functools
import itertools

import jax
import jax.numpy as jnp
import numpy as np
from jax import lax
from jax.experimental import pallas as pl
from jax.experimental.pallas import tpu as pltpu
from jax.sharding import PartitionSpec as P

AXES = ("func", "box")
REACH = 3
SLOT = 32
STEP = 8


def passed_along(value, steps):
    count = lax.axis_size(AXES)
    pairs = [(source, (source + steps) % count) for source in range(count)]
    return lax.ppermute(value, AXES, pairs)


def half_of(device, k):
    return (device // (k & -k)) % 2


def swapped(value, k, part):
    count = lax.axis_size(AXES)
    assert count % (2 * (k & -k)) == 0
    pairs = [(d, (d + (k if half_of(d, k) == part else -k)) % count) for d in range(count)]
    return lax.ppermute(value, AXES, pairs)


def sent(values, keys, sign):
    return {k: passed_along(values[k], sign * k) for k in keys}


def all_sent(values, now, last, sign):
    there = sent(values, now, sign)
    value, there[now[0]] = lax.optimization_barrier((values[last], there[now[0]]))
    there[last] = passed_along(value, sign * last)
    return there


def rounded_up(value, multiple):
    return -(-int(value) // multiple) * multiple


@functools.lru_cache(maxsize=None)
def bounds(fun_dev, support):
    box_dev = fun_dev // 2
    orders = [
        order
        for order in sorted(set(itertools.permutations((1, 1, 2, 4))))
        if np.abs(np.cumsum(np.array(order) - 2)).max() <= 1
    ]
    box_all, fun_all = 12 * support, 24 * support
    assert fun_all % fun_dev == 0
    devices = fun_all // fun_dev
    rows = np.zeros(2 * REACH + 1, np.int64)
    low, high, boxes, end = 10**6, -(10**6), 0, 0
    for picks in itertools.product(orders, repeat=3):
        density = np.repeat(np.concatenate(picks), support)
        centers = np.repeat(np.arange(box_all), density)
        load = sum(np.roll(density, t) for t in range(support))
        below = np.concatenate([[0], np.cumsum(np.tile(load, 3))])
        over = np.clip(np.arange(box_all)[:, None] + support - box_all, 0, None)
        carried = int((over[:, 0] * density).sum())
        below = below - carried
        twice = below[:-1] + below[1:]
        cut = np.array([
            np.searchsorted(twice, 2 * support * fun_dev * (devices + d), side="right")
            for d in range(-REACH - 1, devices + REACH + 2)
        ]) - box_all
        first = REACH + 1
        width = np.diff(cut)
        place = cut - box_dev * (np.arange(len(cut)) - first)
        low, high = min(low, place.min()), max(high, place.max())
        boxes = max(boxes, width.max())
        end = max(end, (place[:-1] + width).max())
        box = centers[:, None] + np.arange(support)
        owner = np.searchsorted(cut, box, side="right") - 1 - first
        device = np.arange(fun_all)[:, None] // fun_dev
        offset = owner - device
        assert np.abs(offset).max() <= REACH
        count = np.bincount((device * (2 * REACH + 1) + offset + REACH).ravel(), minlength=devices * (2 * REACH + 1))
        rows = np.maximum(rows, count.reshape(devices, -1).max(0))
    return (
        tuple(int(r) for r in rows),
        int(low),
        int(high),
        rounded_up(boxes, STEP),
        -(-int(end) // box_dev),
    )


def iota(shape, dim):
    return lax.broadcasted_iota(jnp.int32, shape, dim).astype(jnp.float32)


def one_hot(mask):
    return jnp.where(mask, 1.0, 0.0).astype(jnp.bfloat16)


def spread_over(column, to):
    return jnp.sum(jnp.where(iota((column.shape[0], to.shape[1]), 0) == to, column, 0.0), axis=0, keepdims=True)


def times(a, b, dims=((1,), (0,)), precision=None):
    return lax.dot_general(
        a, b, (dims, ((), ())), precision=precision, preferred_element_type=jnp.float32
    )


def pack_kernel(plan, me_ref, centers_ref, flat_hbm, potential_hbm, *refs):
    fun_dev, support, devices, halo, rows, back, low_cut, high_cut, now = plan
    outs = dict(zip(now, refs[: len(now)]))
    near_ref, cut_ref, home_ref, own_ref, row_ref, flat_ref, potential_ref, sems = refs[len(now) :]
    copies = [
        pltpu.make_async_copy(flat_hbm, flat_ref, sems.at[0]),
        pltpu.make_async_copy(potential_hbm, potential_ref, sems.at[1]),
    ]
    for copy in copies:
        copy.start()
    me = me_ref[0]
    box_dev = fun_dev // 2
    fun_all, box_all = fun_dev * devices, box_dev * devices
    count = near_ref.shape[0]

    start = me * fun_dev - halo * fun_dev
    start = jnp.where(start < 0, start + fun_all, start).astype(jnp.float32)
    at = start + iota((count, 1), 0)
    at = jnp.where(at >= fun_all, at - fun_all, at)
    near = jnp.sum(
        jnp.where(iota((count, fun_all), 1) == at, centers_ref[...].astype(jnp.float32)[None, :], 0.0), axis=1, keepdims=True
    )
    near = near - (me * box_dev).astype(jnp.float32)
    near = jnp.where(near < -(box_all // 2), near + box_all, near)
    near = jnp.where(near >= box_all // 2, near - box_all, near)
    near_row = spread_over(near, iota((1, count), 1))
    near_ref[...] = jnp.broadcast_to(near, near_ref.shape)

    tries = high_cut - low_cut + 1
    trial = iota((rounded_up(tries, 8), 1), 0)
    cuts = []
    for k in range(-REACH, REACH + 2):
        gap = trial + float(low_cut + k * box_dev) - near_row
        twice = jnp.sum(
            jnp.clip(gap, 0.0, support) + jnp.clip(gap + 1.0, 0.0, support), axis=1, keepdims=True
        )
        goal = float(2 * support * fun_dev * (halo + k))
        passed = jnp.where((twice <= goal) & (trial < tries), 1.0, 0.0)
        cut = jnp.sum(passed) + float(low_cut + k * box_dev)
        cuts.append(cut)
        cut_ref[k + REACH] = cut.astype(jnp.int32)

    copies[1].wait()
    potential = potential_ref[...]
    high = potential.astype(jnp.bfloat16)
    low = (potential - high.astype(jnp.float32)).astype(jnp.bfloat16)
    shape = (own_ref.shape[0], box_dev)
    at_high = iota(shape, 0) == iota(shape, 1)
    at_low = iota(shape, 0) - float(shape[0] // 2) == iota(shape, 1)
    own_ref[...] = (times(one_hot(at_high), high) + times(one_hot(at_low), low)).astype(jnp.bfloat16)

    mine = near[halo * fun_dev : (halo + 1) * fun_dev]
    pieces = fun_dev * support
    piece = lax.broadcasted_iota(jnp.int32, (1, pieces), 1)
    of_fun = lax.shift_right_logical(piece, support.bit_length() - 1).astype(jnp.float32)
    step = piece.astype(jnp.float32) - of_fun * support
    mine_row = spread_over(mine, of_fun)
    earlier = iota((fun_dev, pieces), 0) < of_fun
    home, base = jnp.zeros((1, pieces), jnp.float32), 0
    for k in range(-REACH, REACH + 1):
        first, end = cuts[k + REACH], cuts[k + REACH + 1]
        leave = jnp.clip(end - mine, 0.0, support) - jnp.clip(first - mine, 0.0, support)
        leave_at = jnp.sum(jnp.where(earlier, leave, 0.0), axis=0, keepdims=True)
        low_edge = jnp.clip(first - mine_row, 0.0, support)
        goes = (step >= low_edge) & (step < jnp.clip(end - mine_row, 0.0, support))
        row = leave_at + step - low_edge
        home = home + jnp.where(goes, row + float(base), 0.0)
        base += back[k + REACH]
        row_ref[k + REACH : k + REACH + 1] = jnp.where(goes, row, -1.0)
    row_ref[2 * REACH + 1 :] = jnp.full((row_ref.shape[0] - 2 * REACH - 1, pieces), -1.0, jnp.float32)
    home_ref[...] = home
    copies[0].wait()
    packed_rows(rows, box_dev, row_ref, flat_ref, own_ref, outs)


def packed_rows(rows, box_dev, row_ref, flat_ref, own_ref, outs):
    for k, out_ref in outs.items():
        sent = out_ref.shape[0]
        row = row_ref[k + REACH : k + REACH + 1]
        value = times(one_hot(iota((sent, row.shape[1]), 0) == row), flat_ref[...])
        if k < 0:
            shape = (sent, own_ref.shape[0])
            part = iota(shape, 0) - float(rows[k + REACH])
            from_col = jnp.where(part < box_dev, part, part - box_dev + float(shape[1] // 2))
            inside = (part >= 0) & (part < 2 * box_dev)
            value = value + times(one_hot(inside & (iota(shape, 1) == from_col)), own_ref[...])
        out_ref[...] = value.astype(jnp.bfloat16)


def picked(start, low, high, first, rows):
    lane = iota((SLOT, rows), 1)
    picks = []
    for b in range(STEP):
        box = first + float(b)
        row = jnp.where((box >= low) & (box < high), start + box, -1.0)
        picks.append(one_hot(lane == row))
    return jnp.concatenate(picks, axis=0)


def table_kernel(plan, cut_ref, near_ref, flat_ref, own_ref, column_ref, place_ref, active_ref, local_ref, *passed):
    fun_dev, support, halo, boxes = plan
    slots = 2 * REACH + 1
    first = cut_ref[REACH].astype(jnp.float32)
    end = cut_ref[REACH + 1].astype(jnp.float32)
    lane = iota((SLOT, 128), 1)
    along = lax.broadcasted_iota(jnp.int32, (1, boxes * SLOT), 1)
    box = lax.shift_right_logical(along, SLOT.bit_length() - 1).astype(jnp.float32)
    of_fun = along.astype(jnp.float32) - box * SLOT
    levels = [1] * (boxes // STEP)
    for e in range(slots):
        at = (halo - REACH + e) * fun_dev
        others = near_ref[at : at + fun_dev, 0:1]
        edge_low = jnp.clip(first - others, 0.0, support)
        edge_high = jnp.clip(end - others, 0.0, support)
        come = edge_high - edge_low
        come_row = spread_over(come, lane[:1])
        come_at = jnp.sum(
            jnp.where(lane[:fun_dev] < iota((fun_dev, 128), 0), come_row, 0.0), axis=1, keepdims=True
        )
        box_low = edge_low + others - first
        box_high = edge_high + others - first
        packed = come_at - box_low
        spare = jnp.zeros((SLOT - fun_dev, 1), jnp.float32)
        if e == REACH:
            own_start = iota((fun_dev, 1), 0) * support + first - others
            own_start = jnp.concatenate([own_start, spare], axis=0)
        packed, box_low, box_high = (
            jnp.concatenate([column, spare], axis=0) for column in (packed, box_low, box_high)
        )
        if e == REACH:
            for g in range(boxes // STEP):
                pick = picked(own_start, box_low, box_high, float(g * STEP), flat_ref.shape[0])
                local_ref[g * STEP : (g + 1) * STEP] = times(pick, flat_ref[...]).astype(jnp.bfloat16).reshape(
                    STEP, SLOT, flat_ref.shape[1]
                )
        column_ref[e * SLOT : (e + 1) * SLOT, :] = jnp.where(
            lane == 0.0, packed, jnp.where(lane == 1.0, box_low, box_high)
        )
        lies = (box >= spread_over(box_low, of_fun)) & (box < spread_over(box_high, of_fun))
        place = jnp.where(lies, spread_over(packed, of_fun) + box, -1.0)
        for g in range(boxes // STEP):
            place_ref[g, e : e + 1, :] = place[:, g * STEP * SLOT : (g + 1) * STEP * SLOT]
            here = (box >= g * STEP) & (box < (g + 1) * STEP) & lies
            used = jnp.sum(jnp.where(here, 1.0, 0.0)).astype(jnp.int32)
            active_ref[e * (boxes // STEP) + g] = used
            level = jnp.where(used > 0, max(1, abs(e - REACH)), 1)
            levels[g] = jnp.maximum(levels[g], level)
    for g in range(boxes // STEP):
        active_ref[slots * (boxes // STEP) + g] = levels[g]
    for side in range(slots + 1):
        passed[0][side] = cut_ref[side]
    passed[1][...] = own_ref[...]
    spare = place_ref.shape[1] - slots
    place_ref[:, slots:, :] = jnp.full((boxes // STEP, spare, STEP * SLOT), -1.0, jnp.float32)


def function_of(shape, dim, fun_dev):
    row = lax.broadcasted_iota(jnp.int32, shape, dim)
    slot = lax.shift_right_logical(row, SLOT.bit_length() - 1)
    in_slot = row - slot * SLOT
    return jnp.where(in_slot < fun_dev, slot * fun_dev + in_slot, -1)


def moved(value, shift):
    return pltpu.roll(value, shift % value.shape[1], 1)


def skewed(value, sign):
    row = lax.broadcasted_iota(jnp.int32, value.shape, 0)
    bit = 1
    while bit < value.shape[0]:
        value = jnp.where((row & bit) != 0, moved(value, sign * bit), value)
        bit *= 2
    return value


def band_lanes(fun_dev, reading):
    window = (2 * REACH + 1) * fun_dev
    return rounded_up(window + reading + fun_dev + max(0, window - reading), 128)


def level_rows(level):
    return (REACH - level) * SLOT, (REACH + level + 1) * SLOT


def unpack_kernel(plan, cut_ref, me_ref, active_ref, column_ref, own_ref, local_ref, *refs):
    fun_dev, box_dev, reading, volume, rows, back, blocks = plan
    slots = 2 * REACH + 1
    sources = refs[:REACH] + (None,) + refs[REACH : slots - 1]
    window_ref, region_ref = refs[slots - 1 : slots + 1]
    gram_refs = refs[slots + 1 : 2 * slots + 1]
    dense = refs[2 * slots + 1]
    totals = refs[2 * slots + 2 :]
    steps = window_ref.shape[0] // STEP
    width = cut_ref[REACH + 1] - cut_ref[REACH]

    for total in totals:
        total[...] = jnp.zeros_like(total)
    value = None
    for t in range(blocks):
        held = own_ref if t == 0 else sources[REACH + t]
        at = 0 if t == 0 else rows[REACH + t]
        from_row = at // 16 * 16
        held = held[from_row:]
        second = own_ref.shape[0] // 2 if t == 0 else box_dev
        shape = (region_ref.shape[0], held.shape[0])
        row, col = iota(shape, 0), iota(shape, 1)
        box = row - jnp.where(row >= SLOT, float(SLOT), 0.0) + cut_ref[REACH].astype(jnp.float32) - t * box_dev
        wanted = box + jnp.where(row >= SLOT, float(second), 0.0) + float(at - from_row)
        good = (box >= 0) & (box < box_dev) & (row < 2 * SLOT)
        term = times(one_hot(good & (col == wanted)), held)
        value = term if value is None else value + term
    region_ref[...] = value.astype(jnp.bfloat16)

    @pl.loop(0, lax.div(width + STEP - 1, STEP))
    def _(step):
        here_rows = pl.ds(step * STEP, STEP)
        level = active_ref[slots * steps + step]
        window_ref[here_rows, REACH * SLOT : (REACH + 1) * SLOT, :] = local_ref[here_rows]
        for e in range(slots):
            if e == REACH:
                continue
            used = active_ref[e * steps + step] > 0

            @pl.when(used)
            def _():
                start = column_ref[e * SLOT : (e + 1) * SLOT, 0:1]
                low = column_ref[e * SLOT : (e + 1) * SLOT, 1:2]
                high = column_ref[e * SLOT : (e + 1) * SLOT, 2:3]
                pick = picked(start, low, high, (step * STEP).astype(jnp.float32), back[e])
                found = times(pick, sources[e][: back[e]])
                window_ref[here_rows, e * SLOT : (e + 1) * SLOT, :] = found.astype(jnp.bfloat16).reshape(
                    STEP, SLOT, found.shape[-1]
                )

            @pl.when(jnp.logical_not(used) & (level >= abs(e - REACH)))
            def _():
                window_ref[here_rows, e * SLOT : (e + 1) * SLOT, :] = jnp.zeros(
                    (STEP, SLOT, window_ref.shape[-1]), jnp.bfloat16
                )
        for part, total in enumerate(totals):
            @pl.when(level == part + 1)
            def _():
                low, high = level_rows(part + 1)
                value = total[...]
                for b in range(STEP):
                    here = window_ref[step * STEP + b, low:high]
                    value = value + times(here, here, ((1,), (1,)))
                total[...] = value

    wide, lanes = dense.shape
    keep = jnp.where(
        function_of((wide, lanes), 0, fun_dev) == lax.broadcasted_iota(jnp.int32, (wide, lanes), 1), volume, 0.0
    )
    dense[...] = times(totals[-1][...], keep, precision=lax.Precision.HIGHEST)
    for part, total in enumerate(totals[:-1]):
        low, high = level_rows(part + 1)
        dense[low:high] += times(total[...], keep[low:high], precision=lax.Precision.HIGHEST)
    bands = []
    for e in range(slots):
        rows_here = dense[e * SLOT : e * SLOT + fun_dev]
        bands.append(skewed(moved(rows_here, reading - 1 - e * fun_dev), -1)[:, : 2 * reading])
    gram_refs[0][...] = bands[REACH]
    for k in range(1, REACH + 1):
        half = lax.rem(lax.div(me_ref[0], k & -k), 2)
        for part in range(2):
            ahead, behind = (REACH + k, REACH - k) if part == 0 else (REACH - k, REACH + k)

            @pl.when(half == part)
            def _():
                gram_refs[2 * k - 1][...] = bands[ahead]
                gram_refs[2 * k][...] = bands[behind]


def sum_kernel(reading, *refs):
    gram_ref, mixing_ref = refs[-2:]
    value = refs[0][...]
    for ref in refs[1:-2]:
        value = value + ref[...]
    gram_ref[...] = value
    diagonal = jnp.where(lax.broadcasted_iota(jnp.int32, value.shape, 1) == reading - 1, 1.5, 0.0)
    row = diagonal - 0.5 * value
    spare = jnp.zeros((mixing_ref.shape[0] - row.shape[0], row.shape[1]), jnp.float32)
    mixing_ref[...] = jnp.concatenate([row, spare], axis=0).astype(jnp.bfloat16)


def in_level(group, level):
    at = [place for place, e in enumerate(group) if abs(e - REACH) <= level]
    assert not at or at == list(range(at[0], at[-1] + 1))
    return (at[0], at[-1] + 1) if at else (0, 0)


def mix_kernel(plan, cut_ref, me_ref, active_ref, place_ref, window_ref, region_ref, kinetic_ref, *refs):
    fun_dev, reading, group, whole, swaps = plan
    count = len(group)
    bands = dict(zip(swaps, refs[:count]))
    swap_outs = refs[count : 2 * count]
    at_boxes = refs[2 * count : 3 * count]
    mixed = refs[3 * count]
    levels = [v for v in range(1, REACH + 1) if in_level(group, v)[1]]
    mixings = dict(zip(levels, refs[3 * count + 1 :]))
    held = iter(refs[3 * count + 1 + len(levels) :])
    outs = [swap_outs[at] if e == REACH else next(held) for at, e in enumerate(group)]
    slots = 2 * REACH + 1
    steps = window_ref.shape[0] // STEP
    width = cut_ref[REACH + 1] - cut_ref[REACH]
    for out, at_box in zip(outs, at_boxes):
        out[...] = jnp.zeros_like(out)
        at_box[...] = jnp.zeros_like(at_box)
    lanes = band_lanes(fun_dev, reading)
    parts = []
    for e in group:
        k = abs(e - REACH)
        band = bands[k, 0][...].astype(jnp.float32)
        if k:
            half = lax.rem(lax.div(me_ref[0], k & -k), 2).astype(jnp.float32)
            other = half if e > REACH else 1.0 - half
            band = band * (1.0 - other) + bands[k, 1][...].astype(jnp.float32) * other
        band = jnp.concatenate([band, jnp.zeros((SLOT, lanes - 2 * reading), jnp.float32)], axis=1)
        parts.append(moved(skewed(band, 1), e * fun_dev - (reading - 1)).astype(jnp.bfloat16))
    for level, mixing in mixings.items():
        start, end = in_level(group, level)
        shape = (lanes, mixing.shape[1])
        column = function_of(shape, 1, fun_dev)
        column = jnp.where(column >= 0, column + level_rows(level)[0] // SLOT * fun_dev, -1)
        keep = one_hot(column == lax.broadcasted_iota(jnp.int32, shape, 0))
        mixing[...] = times(jnp.concatenate(parts[start:end], axis=0), keep).astype(jnp.bfloat16)

    @pl.loop(0, lax.div(width + STEP - 1, STEP))
    def _(step):
        for level, mixing in mixings.items():
            @pl.when(active_ref[slots * steps + step] == level)
            def _():
                low, high = level_rows(level)
                start, end = in_level(group, level)
                for b in range(STEP):
                    here = window_ref[step * STEP + b, low:high]
                    mixed[b, start * SLOT : end * SLOT] = times(mixing[...], here).astype(jnp.bfloat16)
        shape = (STEP * SLOT, at_boxes[0].shape[1])
        along = lax.broadcasted_iota(jnp.int32, shape, 0)
        box = lax.shift_right_logical(along, SLOT.bit_length() - 1) + step * STEP
        col = lax.broadcasted_iota(jnp.int32, shape, 1)
        boxes_of = one_hot((col == box) | (col == box + SLOT))
        for at, e in enumerate(group):
            @pl.when(active_ref[e * steps + step] > 0)
            def _():
                place = place_ref[step, e : e + 1, :]
                pick = one_hot(iota((outs[at].shape[0], STEP * SLOT), 0) == place)
                part = mixed[:, at * SLOT : (at + 1) * SLOT, :].reshape(STEP * SLOT, mixed.shape[-1])
                outs[at][...] += times(pick, part).astype(jnp.bfloat16)
                at_boxes[at][...] += times(pick, boxes_of).astype(jnp.bfloat16)

    for at, e in enumerate(group):
        if e in whole:
            here = outs[at][...]
            applied = times(here, kinetic_ref[...])
            near_by = times(at_boxes[at][...], region_ref[...])
            outs[at][...] = (applied + near_by * here.astype(jnp.float32)).astype(jnp.bfloat16)
    for k in sorted({abs(e - REACH) for e in group} - {0}):
        behind, ahead = group.index(REACH - k), group.index(REACH + k)
        half = lax.rem(lax.div(me_ref[0], k & -k), 2)
        for part, first, second in ((0, ahead, behind), (1, behind, ahead)):
            @pl.when(half == part)
            def _():
                swap_outs[behind][...] = outs[first][...]
                swap_outs[ahead][...] = outs[second][...]


def home_rows(bases, me_ref, home_ref, sources, at, count):
    shape = (count, home_ref.shape[1])
    here = iota(shape, 1) == iota(shape, 0) + float(at)
    row = jnp.sum(jnp.where(here, home_ref[...], 0.0), axis=1, keepdims=True)
    value = None
    for (ahead, behind, k, part), source in zip(bases, sources):
        base = float(ahead)
        if k:
            half = lax.rem(lax.div(me_ref[0], k & -k), 2)
            base = jnp.where(half == part, ahead, behind).astype(jnp.float32)
        pick = one_hot(iota((count, source.shape[0]), 1) == row - base)
        term = times(pick, source[...])
        value = term if value is None else value + term
    return value


def early_kernel(bases, me_ref, home_ref, *refs):
    sources, out_ref = refs[:-1], refs[-1]
    count = 256
    for at in range(0, out_ref.shape[0], count):
        out_ref[at : at + count] = home_rows(bases, me_ref, home_ref, sources, at, count).astype(jnp.bfloat16)


def home_kernel(bases, me_ref, home_ref, early_ref, *refs):
    sources, out_ref, held, sems = refs[:-3], refs[-3], refs[-2], refs[-1]
    copies = []
    count = held.shape[1]
    for part in range(held.shape[0]):
        at = part * count
        value = home_rows(bases, me_ref, home_ref, sources, at, count) + early_ref[at : at + count].astype(jnp.float32)
        held[part] = value.astype(jnp.bfloat16)
        copy = pltpu.make_async_copy(held.at[part], out_ref.at[pl.ds(at, count)], sems.at[part])
        copy.start()
        copies.append(copy)
    for copy in copies:
        copy.wait()


def on_device(coeffs, centers, kinetic, potential):
    fun_dev, support, points = coeffs.shape
    devices = lax.axis_size(AXES)
    me = lax.axis_index(AXES).astype(jnp.int32).reshape(1)
    box_dev = fun_dev // 2
    volume = 1.0 / (support * points)
    reading = 4 * support
    slots = 2 * REACH + 1
    offsets = list(range(-REACH, REACH + 1))
    last = -REACH
    now = [sign * k for k in range(1, REACH) for sign in (-1, 1)] + [REACH]
    rows, low_cut, high_cut, boxes, blocks = bounds(fun_dev, support)
    assert blocks <= REACH + 1 and support & (support - 1) == 0
    back = tuple(rounded_up(r, 16) for r in rows)
    rows_of = {k: back[k + REACH] for k in offsets}
    flat = coeffs.reshape(fun_dev * support, points)
    halo = REACH + -(-(reading + 8) // fun_dev)
    count = rounded_up((2 * halo + 2) * fun_dev, 128)
    bf16, f32 = jnp.bfloat16, jnp.float32
    smem = pl.BlockSpec(memory_space=pltpu.SMEM)
    vmem = pl.BlockSpec(memory_space=pltpu.VMEM)
    limit = pltpu.CompilerParams(vmem_limit_bytes=26 * 2**20)

    half = rounded_up(box_dev, 16)
    sent_rows = {k: rounded_up(rows[k + REACH] + (2 * box_dev if k < 0 else 0), 16) for k in offsets if k}
    *packed, near, cut, home_row, own_region = pl.pallas_call(
        functools.partial(pack_kernel, (fun_dev, support, devices, halo, rows, back, low_cut, high_cut, now + [last])),
        out_shape=tuple(jax.ShapeDtypeStruct((sent_rows[k], points), bf16) for k in now + [last])
        + (
            jax.ShapeDtypeStruct((count, 128), f32),
            jax.ShapeDtypeStruct((slots + 1,), jnp.int32),
            jax.ShapeDtypeStruct((1, fun_dev * support), f32),
            jax.ShapeDtypeStruct((2 * half, points), bf16),
        ),
        in_specs=[smem, vmem] + [pl.BlockSpec(memory_space=pltpu.HBM)] * 2,
        out_specs=(vmem,) * slots + (smem,) + (vmem,) * 2,
        scratch_shapes=[
            pltpu.VMEM((8, fun_dev * support), f32),
            pltpu.VMEM(flat.shape, bf16),
            pltpu.VMEM(potential.shape, f32),
            pltpu.SemaphoreType.DMA((2,)),
        ],
        compiler_params=pltpu.CompilerParams(vmem_limit_bytes=57 * 2**20),
        name="pack",
    )(me, centers, flat, potential)
    arrived = all_sent(dict(zip(now + [last], packed)), now, last, 1)

    columns, places, active, local, cut, own_region = pl.pallas_call(
        functools.partial(table_kernel, (fun_dev, support, halo, boxes)),
        out_shape=(
            jax.ShapeDtypeStruct((slots * SLOT, 128), f32),
            jax.ShapeDtypeStruct((boxes // STEP, 8, STEP * SLOT), f32),
            jax.ShapeDtypeStruct(((slots + 1) * (boxes // STEP),), jnp.int32),
            jax.ShapeDtypeStruct((boxes, SLOT, points), bf16),
            jax.ShapeDtypeStruct(cut.shape, jnp.int32),
            jax.ShapeDtypeStruct(own_region.shape, bf16),
        ),
        in_specs=[smem, vmem, vmem, vmem],
        out_specs=(vmem, vmem, smem, vmem, smem, vmem),
        compiler_params=limit,
        name="tables",
    )(cut, near, flat, own_region)

    wide = slots * SLOT
    sources = [arrived[REACH - e] for e in range(slots) if e != REACH]
    read_rows = [rows_of[REACH - e] for e in range(slots)]
    level_sizes = [level_rows(part + 1)[1] - level_rows(part + 1)[0] for part in range(REACH)]
    level_sizes = [level_rows(part + 1)[1] - level_rows(part + 1)[0] for part in range(REACH)]
    exact_rows = [rows[2 * REACH - e] for e in range(slots)]
    band = (fun_dev, 2 * reading)
    exact_rows = [rows[2 * REACH - e] for e in range(slots)]
    pieces, region, *grams = pl.pallas_call(
        functools.partial(unpack_kernel, (fun_dev, box_dev, reading, volume, exact_rows, read_rows, blocks)),
        out_shape=(
            jax.ShapeDtypeStruct((boxes, wide, points), bf16),
            jax.ShapeDtypeStruct((128, points), bf16),
        )
        + tuple(jax.ShapeDtypeStruct(band, f32) for _ in range(slots)),
        in_specs=[smem] * 3 + [vmem] * (3 + len(sources)),
        out_specs=(vmem,) * (2 + slots),
        scratch_shapes=[pltpu.VMEM((wide, band_lanes(fun_dev, reading)), f32)]
        + [pltpu.VMEM((size, size), f32) for size in level_sizes],
        compiler_params=limit,
        name="unpack",
    )(cut, me, active, columns, own_region, local, *sources)

    swaps = [(k, 0) for k in range(1, REACH + 1)] + [(k, 1) for k in range(REACH, 0, -1)]
    summed = [swapped(grams[2 * k - 1 + part], k, part) for k, part in swaps]
    gram_band, mixing_rows = pl.pallas_call(
        functools.partial(sum_kernel, reading),
        out_shape=(jax.ShapeDtypeStruct(band, f32), jax.ShapeDtypeStruct((SLOT, 2 * reading), bf16)),
        in_specs=[vmem] * slots,
        out_specs=(vmem, vmem),
        compiler_params=limit,
        name="sum",
    )(grams[0], *summed)
    mixing_of = {swap: swapped(mixing_rows, *swap) for swap in swaps}

    mixing_of[0, 0] = mixing_rows
    ready, at_boxes = {}, {}
    for group, whole in [([2, -2, REACH, -REACH], [2, -2, REACH, -REACH]), ([0, 1, -1], [1, -1])]:
        group, whole = sorted(REACH - k for k in group), [REACH - k for k in whole]
        most = [max(rows_of[REACH - e], rows_of[e - REACH]) for e in group]
        shapes = [(r, points) for r in most] + [(r, 128) for r in most]
        far = {abs(e - REACH) for e in group}
        group_swaps = [swap for swap in [(0, 0)] + swaps if swap[0] in far]
        sizes = [
            ((in_level(group, v)[1] - in_level(group, v)[0]) * SLOT, level_sizes[v - 1])
            for v in range(1, REACH + 1)
            if in_level(group, v)[1]
        ]
        if ready:
            cut, *held = lax.optimization_barrier((cut, *[ready[k] for k in ready]))
            ready = dict(zip(ready, held))
        mixed = pl.pallas_call(
            functools.partial(mix_kernel, (fun_dev, reading, group, whole, group_swaps)),
            out_shape=tuple(jax.ShapeDtypeStruct(shape, bf16) for shape in shapes),
            in_specs=[smem] * 3 + [vmem] * (4 + len(group)),
            out_specs=(vmem,) * len(shapes),
            scratch_shapes=[pltpu.VMEM((STEP, len(group) * SLOT, points), bf16)]
            + [pltpu.VMEM(size, bf16) for size in sizes]
            + [pltpu.VMEM((r, points), bf16) for r, e in zip(most, group) if e != REACH],
            compiler_params=limit,
            cost_estimate=pl.CostEstimate(
                flops=8 * wide * len(group) * SLOT * boxes * points, bytes_accessed=40 * 2**20, transcendentals=0
            ),
            name="mix",
        )(cut, me, active, places, pieces, region, kinetic, *[mixing_of[swap] for swap in group_swaps])
        for at, e in enumerate(group):
            key = (abs(e - REACH), int(e > REACH))
            ready[key], at_boxes[key] = mixed[at], mixed[len(group) + at]
            if e not in whole:
                near_by = jnp.dot(at_boxes[key], region, preferred_element_type=f32)
                applied = jnp.dot(mixed[at], kinetic, preferred_element_type=f32)
                ready[key] = (applied + near_by * mixed[at].astype(f32)).astype(bf16)
    far = (REACH, 1)
    returned = {swap: swapped(ready[swap], *swap) for swap in swaps if swap != far}
    value, returned[2, 0] = lax.optimization_barrier((ready[far], returned[2, 0]))
    returned[far] = swapped(value, *far)
    returned[0, 0] = ready[0, 0]

    bases = {k: sum(back[: k + REACH]) for k in offsets}
    early, late = [(0, 0), (2, 0), (2, 1), (REACH, 0)], [(1, 0), (1, 1), far]
    early_bases = [(bases[k], bases[-k], k, part) for k, part in early]
    late_bases = [(bases[k], bases[-k], k, part) for k, part in late]
    begun = pl.pallas_call(
        functools.partial(early_kernel, early_bases),
        out_shape=jax.ShapeDtypeStruct(flat.shape, bf16),
        in_specs=[smem] + [vmem] * (1 + len(early)),
        out_specs=vmem,
        compiler_params=limit,
        name="early",
    )(me, home_row, *[returned[swap] for swap in early])
    filtered = pl.pallas_call(
        functools.partial(home_kernel, late_bases),
        out_shape=jax.ShapeDtypeStruct(flat.shape, bf16),
        in_specs=[smem] + [vmem] * (2 + len(late)),
        out_specs=pl.BlockSpec(memory_space=pl.ANY),
        scratch_shapes=[
            pltpu.VMEM((flat.shape[0] // 256, 256, points), bf16),
            pltpu.SemaphoreType.DMA((flat.shape[0] // 256,)),
        ],
        compiler_params=limit,
        name="home",
    )(me, home_row, begun, *[returned[swap] for swap in late])
    return (filtered.reshape(coeffs.shape), gram_band)


def solution(mesh):
    placed = (P(AXES, None, None), P(), P(), P(AXES, None))
    return jax.shard_map(
        on_device,
        mesh=mesh,
        in_specs=placed,
        out_specs=(P(AXES, None, None), P(AXES, None)),
        check_vma=False,
    )
```

```python
import functools
import itertools

import jax
import jax.numpy as jnp
import numpy as np
from jax import lax
from jax.experimental import pallas as pl
from jax.experimental.pallas import tpu as pltpu
from jax.sharding import PartitionSpec as P

AXES = ("func", "box")
REACH = 3
SLOT = 32
STEP = 12


def passed_along(value, steps):
    count = lax.axis_size(AXES)
    pairs = [(source, (source + steps) % count) for source in range(count)]
    return lax.ppermute(value, AXES, pairs)


def half_of(device, k):
    return (device // (k & -k)) % 2


def swapped(value, k, part):
    count = lax.axis_size(AXES)
    assert count % (2 * (k & -k)) == 0
    pairs = [(d, (d + (k if half_of(d, k) == part else -k)) % count) for d in range(count)]
    return lax.ppermute(value, AXES, pairs)


def sent(values, keys, sign):
    return {k: passed_along(values[k], sign * k) for k in keys}


def all_sent(values, now, last, sign):
    there = sent(values, now, sign)
    value, there[now[0]] = lax.optimization_barrier((values[last], there[now[0]]))
    there[last] = passed_along(value, sign * last)
    return there


def rounded_up(value, multiple):
    return -(-int(value) // multiple) * multiple


@functools.lru_cache(maxsize=None)
def bounds(fun_dev, support):
    box_dev = fun_dev // 2
    orders = [
        order
        for order in sorted(set(itertools.permutations((1, 1, 2, 4))))
        if np.abs(np.cumsum(np.array(order) - 2)).max() <= 1
    ]
    box_all, fun_all = 12 * support, 24 * support
    assert fun_all % fun_dev == 0
    devices = fun_all // fun_dev
    rows = np.zeros(2 * REACH + 1, np.int64)
    low, high, boxes, end = 10**6, -(10**6), 0, 0
    for picks in itertools.product(orders, repeat=3):
        density = np.repeat(np.concatenate(picks), support)
        centers = np.repeat(np.arange(box_all), density)
        load = sum(np.roll(density, t) for t in range(support))
        below = np.concatenate([[0], np.cumsum(np.tile(load, 3))])
        over = np.clip(np.arange(box_all)[:, None] + support - box_all, 0, None)
        carried = int((over[:, 0] * density).sum())
        below = below - carried
        twice = below[:-1] + below[1:]
        cut = np.array([
            np.searchsorted(twice, 2 * support * fun_dev * (devices + d), side="right")
            for d in range(-REACH - 1, devices + REACH + 2)
        ]) - box_all
        first = REACH + 1
        width = np.diff(cut)
        place = cut - box_dev * (np.arange(len(cut)) - first)
        low, high = min(low, place.min()), max(high, place.max())
        boxes = max(boxes, width.max())
        end = max(end, (place[:-1] + width).max())
        box = centers[:, None] + np.arange(support)
        owner = np.searchsorted(cut, box, side="right") - 1 - first
        device = np.arange(fun_all)[:, None] // fun_dev
        offset = owner - device
        assert np.abs(offset).max() <= REACH
        count = np.bincount((device * (2 * REACH + 1) + offset + REACH).ravel(), minlength=devices * (2 * REACH + 1))
        rows = np.maximum(rows, count.reshape(devices, -1).max(0))
    return (
        tuple(int(r) for r in rows),
        int(low),
        int(high),
        rounded_up(boxes, STEP),
        -(-int(end) // box_dev),
    )


def iota(shape, dim):
    return lax.broadcasted_iota(jnp.int32, shape, dim).astype(jnp.float32)


def one_hot(mask):
    return jnp.where(mask, 1.0, 0.0).astype(jnp.bfloat16)


def spread_over(column, to):
    return jnp.sum(jnp.where(iota((column.shape[0], to.shape[1]), 0) == to, column, 0.0), axis=0, keepdims=True)


def times(a, b, dims=((1,), (0,)), precision=None):
    return lax.dot_general(
        a, b, (dims, ((), ())), precision=precision, preferred_element_type=jnp.float32
    )


def pack_kernel(plan, me_ref, centers_ref, flat_hbm, potential_hbm, *refs):
    fun_dev, support, devices, halo, rows, back, low_cut, high_cut, now = plan
    outs = dict(zip(now, refs[: len(now)]))
    near_ref, cut_ref, home_ref, own_ref, row_ref, flat_ref, potential_ref, sems = refs[len(now) :]
    copies = [
        pltpu.make_async_copy(flat_hbm, flat_ref, sems.at[0]),
        pltpu.make_async_copy(potential_hbm, potential_ref, sems.at[1]),
    ]
    for copy in copies:
        copy.start()
    me = me_ref[0]
    box_dev = fun_dev // 2
    fun_all, box_all = fun_dev * devices, box_dev * devices
    count = near_ref.shape[0]

    start = me * fun_dev - halo * fun_dev
    start = jnp.where(start < 0, start + fun_all, start).astype(jnp.float32)
    at = start + iota((count, 1), 0)
    at = jnp.where(at >= fun_all, at - fun_all, at)
    near = jnp.sum(
        jnp.where(iota((count, fun_all), 1) == at, centers_ref[...].astype(jnp.float32)[None, :], 0.0), axis=1, keepdims=True
    )
    near = near - (me * box_dev).astype(jnp.float32)
    near = jnp.where(near < -(box_all // 2), near + box_all, near)
    near = jnp.where(near >= box_all // 2, near - box_all, near)
    near_row = spread_over(near, iota((1, count), 1))
    near_ref[...] = jnp.broadcast_to(near, near_ref.shape)

    tries = high_cut - low_cut + 1
    trial = iota((rounded_up(tries, 8), 1), 0)
    cuts = []
    for k in range(-REACH, REACH + 2):
        gap = trial + float(low_cut + k * box_dev) - near_row
        twice = jnp.sum(
            jnp.clip(gap, 0.0, support) + jnp.clip(gap + 1.0, 0.0, support), axis=1, keepdims=True
        )
        goal = float(2 * support * fun_dev * (halo + k))
        passed = jnp.where((twice <= goal) & (trial < tries), 1.0, 0.0)
        cut = jnp.sum(passed) + float(low_cut + k * box_dev)
        cuts.append(cut)
        cut_ref[k + REACH] = cut.astype(jnp.int32)

    copies[1].wait()
    potential = potential_ref[...]
    high = potential.astype(jnp.bfloat16)
    low = (potential - high.astype(jnp.float32)).astype(jnp.bfloat16)
    shape = (own_ref.shape[0], box_dev)
    at_high = iota(shape, 0) == iota(shape, 1)
    at_low = iota(shape, 0) - float(shape[0] // 2) == iota(shape, 1)
    own_ref[...] = (times(one_hot(at_high), high) + times(one_hot(at_low), low)).astype(jnp.bfloat16)

    mine = near[halo * fun_dev : (halo + 1) * fun_dev]
    pieces = fun_dev * support
    piece = lax.broadcasted_iota(jnp.int32, (1, pieces), 1)
    of_fun = lax.shift_right_logical(piece, support.bit_length() - 1).astype(jnp.float32)
    step = piece.astype(jnp.float32) - of_fun * support
    mine_row = spread_over(mine, of_fun)
    earlier = iota((fun_dev, pieces), 0) < of_fun
    home, base = jnp.zeros((1, pieces), jnp.float32), 0
    for k in range(-REACH, REACH + 1):
        first, end = cuts[k + REACH], cuts[k + REACH + 1]
        leave = jnp.clip(end - mine, 0.0, support) - jnp.clip(first - mine, 0.0, support)
        leave_at = jnp.sum(jnp.where(earlier, leave, 0.0), axis=0, keepdims=True)
        low_edge = jnp.clip(first - mine_row, 0.0, support)
        goes = (step >= low_edge) & (step < jnp.clip(end - mine_row, 0.0, support))
        row = leave_at + step - low_edge
        home = home + jnp.where(goes, row + float(base), 0.0)
        base += back[k + REACH]
        row_ref[k + REACH : k + REACH + 1] = jnp.where(goes, row, -1.0)
    row_ref[2 * REACH + 1 :] = jnp.full((row_ref.shape[0] - 2 * REACH - 1, pieces), -1.0, jnp.float32)
    home_ref[...] = home
    copies[0].wait()
    packed_rows(rows, box_dev, row_ref, flat_ref, own_ref, outs)


def packed_rows(rows, box_dev, row_ref, flat_ref, own_ref, outs):
    for k, out_ref in outs.items():
        sent = out_ref.shape[0]
        row = row_ref[k + REACH : k + REACH + 1]
        value = times(one_hot(iota((sent, row.shape[1]), 0) == row), flat_ref[...])
        if k < 0:
            shape = (sent, own_ref.shape[0])
            part = iota(shape, 0) - float(rows[k + REACH])
            from_col = jnp.where(part < box_dev, part, part - box_dev + float(shape[1] // 2))
            inside = (part >= 0) & (part < 2 * box_dev)
            value = value + times(one_hot(inside & (iota(shape, 1) == from_col)), own_ref[...])
        out_ref[...] = value.astype(jnp.bfloat16)


def picked(start, low, high, first, rows):
    lane = iota((SLOT, rows), 1)
    picks = []
    for b in range(STEP):
        box = first + float(b)
        row = jnp.where((box >= low) & (box < high), start + box, -1.0)
        picks.append(one_hot(lane == row))
    return jnp.concatenate(picks, axis=0)


def table_kernel(plan, cut_ref, near_ref, flat_ref, column_ref, place_ref, active_ref, local_ref):
    fun_dev, support, halo, boxes = plan
    slots = 2 * REACH + 1
    first = cut_ref[REACH].astype(jnp.float32)
    end = cut_ref[REACH + 1].astype(jnp.float32)
    lane = iota((SLOT, 128), 1)
    along = lax.broadcasted_iota(jnp.int32, (1, boxes * SLOT), 1)
    box = lax.shift_right_logical(along, SLOT.bit_length() - 1).astype(jnp.float32)
    of_fun = along.astype(jnp.float32) - box * SLOT
    levels = [1] * (boxes // STEP)
    for e in range(slots):
        at = (halo - REACH + e) * fun_dev
        others = near_ref[at : at + fun_dev, 0:1]
        edge_low = jnp.clip(first - others, 0.0, support)
        edge_high = jnp.clip(end - others, 0.0, support)
        come = edge_high - edge_low
        come_row = spread_over(come, lane[:1])
        come_at = jnp.sum(
            jnp.where(lane[:fun_dev] < iota((fun_dev, 128), 0), come_row, 0.0), axis=1, keepdims=True
        )
        box_low = edge_low + others - first
        box_high = edge_high + others - first
        packed = come_at - box_low
        spare = jnp.zeros((SLOT - fun_dev, 1), jnp.float32)
        if e == REACH:
            own_start = iota((fun_dev, 1), 0) * support + first - others
            own_start = jnp.concatenate([own_start, spare], axis=0)
        packed, box_low, box_high = (
            jnp.concatenate([column, spare], axis=0) for column in (packed, box_low, box_high)
        )
        if e == REACH:
            for g in range(boxes // STEP):
                pick = picked(own_start, box_low, box_high, float(g * STEP), flat_ref.shape[0])
                local_ref[g * STEP : (g + 1) * STEP] = times(pick, flat_ref[...]).astype(jnp.bfloat16).reshape(
                    STEP, SLOT, flat_ref.shape[1]
                )
        column_ref[e * SLOT : (e + 1) * SLOT, :] = jnp.where(
            lane == 0.0, packed, jnp.where(lane == 1.0, box_low, box_high)
        )
        lies = (box >= spread_over(box_low, of_fun)) & (box < spread_over(box_high, of_fun))
        place = jnp.where(lies, spread_over(packed, of_fun) + box, -1.0)
        for g in range(boxes // STEP):
            place_ref[g, e : e + 1, :] = place[:, g * STEP * SLOT : (g + 1) * STEP * SLOT]
            here = (box >= g * STEP) & (box < (g + 1) * STEP) & lies
            used = jnp.sum(jnp.where(here, 1.0, 0.0)).astype(jnp.int32)
            active_ref[e * (boxes // STEP) + g] = used
            level = jnp.where(used > 0, max(1, abs(e - REACH)), 1)
            levels[g] = jnp.maximum(levels[g], level)
    for g in range(boxes // STEP):
        active_ref[slots * (boxes // STEP) + g] = levels[g]
    spare = place_ref.shape[1] - slots
    place_ref[:, slots:, :] = jnp.full((boxes // STEP, spare, STEP * SLOT), -1.0, jnp.float32)


def function_of(shape, dim, fun_dev):
    row = lax.broadcasted_iota(jnp.int32, shape, dim)
    slot = lax.shift_right_logical(row, SLOT.bit_length() - 1)
    in_slot = row - slot * SLOT
    return jnp.where(in_slot < fun_dev, slot * fun_dev + in_slot, -1)


def moved(value, shift):
    return pltpu.roll(value, shift % value.shape[1], 1)


def skewed(value, sign):
    row = lax.broadcasted_iota(jnp.int32, value.shape, 0)
    bit = 1
    while bit < value.shape[0]:
        value = jnp.where((row & bit) != 0, moved(value, sign * bit), value)
        bit *= 2
    return value


def band_lanes(fun_dev, reading):
    window = (2 * REACH + 1) * fun_dev
    return rounded_up(window + reading + fun_dev + max(0, window - reading), 128)


def level_rows(level):
    return (REACH - level) * SLOT, (REACH + level + 1) * SLOT


def unpack_kernel(plan, cut_ref, me_ref, active_ref, column_ref, own_ref, local_ref, *refs):
    fun_dev, box_dev, reading, volume, rows, back, blocks = plan
    slots = 2 * REACH + 1
    sources = refs[:REACH] + (None,) + refs[REACH : slots - 1]
    window_ref, region_ref = refs[slots - 1 : slots + 1]
    gram_refs = refs[slots + 1 : 2 * slots + 1]
    dense = refs[2 * slots + 1]
    totals = refs[2 * slots + 2 :]
    steps = window_ref.shape[0] // STEP
    width = cut_ref[REACH + 1] - cut_ref[REACH]

    for total in totals:
        total[...] = jnp.zeros_like(total)
    value = None
    for t in range(blocks):
        held = own_ref if t == 0 else sources[REACH + t]
        at = 0 if t == 0 else rows[REACH + t]
        from_row = at // 16 * 16
        held = held[from_row:]
        second = own_ref.shape[0] // 2 if t == 0 else box_dev
        shape = (region_ref.shape[0], held.shape[0])
        row, col = iota(shape, 0), iota(shape, 1)
        box = row - jnp.where(row >= SLOT, float(SLOT), 0.0) + cut_ref[REACH].astype(jnp.float32) - t * box_dev
        wanted = box + jnp.where(row >= SLOT, float(second), 0.0) + float(at - from_row)
        good = (box >= 0) & (box < box_dev) & (row < 2 * SLOT)
        term = times(one_hot(good & (col == wanted)), held)
        value = term if value is None else value + term
    region_ref[...] = value.astype(jnp.bfloat16)

    @pl.loop(0, lax.div(width + STEP - 1, STEP))
    def _(step):
        here_rows = pl.ds(step * STEP, STEP)
        level = active_ref[slots * steps + step]
        window_ref[here_rows, REACH * SLOT : (REACH + 1) * SLOT, :] = local_ref[here_rows]
        for e in range(slots):
            if e == REACH:
                continue
            used = active_ref[e * steps + step] > 0

            @pl.when(used)
            def _():
                start = column_ref[e * SLOT : (e + 1) * SLOT, 0:1]
                low = column_ref[e * SLOT : (e + 1) * SLOT, 1:2]
                high = column_ref[e * SLOT : (e + 1) * SLOT, 2:3]
                pick = picked(start, low, high, (step * STEP).astype(jnp.float32), back[e])
                found = times(pick, sources[e][: back[e]])
                window_ref[here_rows, e * SLOT : (e + 1) * SLOT, :] = found.astype(jnp.bfloat16).reshape(
                    STEP, SLOT, found.shape[-1]
                )

            @pl.when(jnp.logical_not(used) & (level >= abs(e - REACH)))
            def _():
                window_ref[here_rows, e * SLOT : (e + 1) * SLOT, :] = jnp.zeros(
                    (STEP, SLOT, window_ref.shape[-1]), jnp.bfloat16
                )
        for part, total in enumerate(totals):
            @pl.when(level == part + 1)
            def _():
                low, high = level_rows(part + 1)
                value = total[...]
                for b in range(STEP):
                    here = window_ref[step * STEP + b, low:high]
                    value = value + times(here, here, ((1,), (1,)))
                total[...] = value

    wide, lanes = dense.shape
    keep = jnp.where(
        function_of((wide, lanes), 0, fun_dev) == lax.broadcasted_iota(jnp.int32, (wide, lanes), 1), volume, 0.0
    )
    dense[...] = times(totals[-1][...], keep, precision=lax.Precision.HIGHEST)
    for part, total in enumerate(totals[:-1]):
        low, high = level_rows(part + 1)
        dense[low:high] += times(total[...], keep[low:high], precision=lax.Precision.HIGHEST)
    bands = []
    for e in range(slots):
        rows_here = dense[e * SLOT : e * SLOT + fun_dev]
        bands.append(skewed(moved(rows_here, reading - 1 - e * fun_dev), -1)[:, : 2 * reading])
    gram_refs[0][...] = bands[REACH]
    for k in range(1, REACH + 1):
        half = lax.rem(lax.div(me_ref[0], k & -k), 2)
        for part in range(2):
            ahead, behind = (REACH + k, REACH - k) if part == 0 else (REACH - k, REACH + k)

            @pl.when(half == part)
            def _():
                gram_refs[2 * k - 1][...] = bands[ahead]
                gram_refs[2 * k][...] = bands[behind]


def sum_kernel(reading, *refs):
    gram_ref, mixing_ref = refs[-2:]
    value = refs[0][...]
    for ref in refs[1:-2]:
        value = value + ref[...]
    gram_ref[...] = value
    diagonal = jnp.where(lax.broadcasted_iota(jnp.int32, value.shape, 1) == reading - 1, 1.5, 0.0)
    row = diagonal - 0.5 * value
    spare = jnp.zeros((mixing_ref.shape[0] - row.shape[0], row.shape[1]), jnp.float32)
    mixing_ref[...] = jnp.concatenate([row, spare], axis=0).astype(jnp.bfloat16)


def in_level(group, level):
    at = [place for place, e in enumerate(group) if abs(e - REACH) <= level]
    assert not at or at == list(range(at[0], at[-1] + 1))
    return (at[0], at[-1] + 1) if at else (0, 0)


def mix_kernel(plan, cut_ref, me_ref, active_ref, place_ref, window_ref, region_ref, kinetic_ref, *refs):
    fun_dev, reading, group, whole, swaps = plan
    count = len(group)
    bands = dict(zip(swaps, refs[:count]))
    swap_outs = refs[count : 2 * count]
    at_boxes = refs[2 * count : 3 * count]
    mixed = refs[3 * count]
    levels = [v for v in range(1, REACH + 1) if in_level(group, v)[1]]
    mixings = dict(zip(levels, refs[3 * count + 1 :]))
    held = iter(refs[3 * count + 1 + len(levels) :])
    outs = [swap_outs[at] if e == REACH else next(held) for at, e in enumerate(group)]
    slots = 2 * REACH + 1
    steps = window_ref.shape[0] // STEP
    width = cut_ref[REACH + 1] - cut_ref[REACH]
    for out, at_box in zip(outs, at_boxes):
        out[...] = jnp.zeros_like(out)
        at_box[...] = jnp.zeros_like(at_box)
    lanes = band_lanes(fun_dev, reading)
    parts = []
    for e in group:
        k = abs(e - REACH)
        band = bands[k, 0][...].astype(jnp.float32)
        if k:
            half = lax.rem(lax.div(me_ref[0], k & -k), 2).astype(jnp.float32)
            other = half if e > REACH else 1.0 - half
            band = band * (1.0 - other) + bands[k, 1][...].astype(jnp.float32) * other
        band = jnp.concatenate([band, jnp.zeros((SLOT, lanes - 2 * reading), jnp.float32)], axis=1)
        parts.append(moved(skewed(band, 1), e * fun_dev - (reading - 1)).astype(jnp.bfloat16))
    for level, mixing in mixings.items():
        start, end = in_level(group, level)
        shape = (lanes, mixing.shape[1])
        column = function_of(shape, 1, fun_dev)
        column = jnp.where(column >= 0, column + level_rows(level)[0] // SLOT * fun_dev, -1)
        keep = one_hot(column == lax.broadcasted_iota(jnp.int32, shape, 0))
        mixing[...] = times(jnp.concatenate(parts[start:end], axis=0), keep).astype(jnp.bfloat16)

    @pl.loop(0, lax.div(width + STEP - 1, STEP))
    def _(step):
        for level, mixing in mixings.items():
            @pl.when(active_ref[slots * steps + step] == level)
            def _():
                low, high = level_rows(level)
                start, end = in_level(group, level)
                for b in range(STEP):
                    here = window_ref[step * STEP + b, low:high]
                    mixed[b, start * SLOT : end * SLOT] = times(mixing[...], here).astype(jnp.bfloat16)
        shape = (STEP * SLOT, at_boxes[0].shape[1])
        along = lax.broadcasted_iota(jnp.int32, shape, 0)
        box = lax.shift_right_logical(along, SLOT.bit_length() - 1) + step * STEP
        col = lax.broadcasted_iota(jnp.int32, shape, 1)
        boxes_of = one_hot((col == box) | (col == box + SLOT))
        for at, e in enumerate(group):
            @pl.when(active_ref[e * steps + step] > 0)
            def _():
                place = place_ref[step, e : e + 1, :]
                pick = one_hot(iota((outs[at].shape[0], STEP * SLOT), 0) == place)
                part = mixed[:, at * SLOT : (at + 1) * SLOT, :].reshape(STEP * SLOT, mixed.shape[-1])
                outs[at][...] += times(pick, part).astype(jnp.bfloat16)
                at_boxes[at][...] += times(pick, boxes_of).astype(jnp.bfloat16)

    for at, e in enumerate(group):
        if e in whole:
            here = outs[at][...]
            applied = times(here, kinetic_ref[...])
            near_by = times(at_boxes[at][...], region_ref[...])
            outs[at][...] = (applied + near_by * here.astype(jnp.float32)).astype(jnp.bfloat16)
    for k in sorted({abs(e - REACH) for e in group} - {0}):
        behind, ahead = group.index(REACH - k), group.index(REACH + k)
        half = lax.rem(lax.div(me_ref[0], k & -k), 2)
        for part, first, second in ((0, ahead, behind), (1, behind, ahead)):
            @pl.when(half == part)
            def _():
                swap_outs[behind][...] = outs[first][...]
                swap_outs[ahead][...] = outs[second][...]


def home_rows(bases, me_ref, home_ref, sources, at, count):
    shape = (count, home_ref.shape[1])
    here = iota(shape, 1) == iota(shape, 0) + float(at)
    row = jnp.sum(jnp.where(here, home_ref[...], 0.0), axis=1, keepdims=True)
    value = None
    for (ahead, behind, k, part), source in zip(bases, sources):
        base = float(ahead)
        if k:
            half = lax.rem(lax.div(me_ref[0], k & -k), 2)
            base = jnp.where(half == part, ahead, behind).astype(jnp.float32)
        pick = one_hot(iota((count, source.shape[0]), 1) == row - base)
        term = times(pick, source[...])
        value = term if value is None else value + term
    return value


def early_kernel(bases, me_ref, home_ref, *refs):
    sources, out_ref = refs[:-1], refs[-1]
    count = 256
    for at in range(0, out_ref.shape[0], count):
        out_ref[at : at + count] = home_rows(bases, me_ref, home_ref, sources, at, count).astype(jnp.bfloat16)


def home_kernel(bases, me_ref, home_ref, early_ref, *refs):
    sources, out_ref, held, sems = refs[:-3], refs[-3], refs[-2], refs[-1]
    copies = []
    count = held.shape[1]
    for part in range(held.shape[0]):
        at = part * count
        value = home_rows(bases, me_ref, home_ref, sources, at, count) + early_ref[at : at + count].astype(jnp.float32)
        held[part] = value.astype(jnp.bfloat16)
        copy = pltpu.make_async_copy(held.at[part], out_ref.at[pl.ds(at, count)], sems.at[part])
        copy.start()
        copies.append(copy)
    for copy in copies:
        copy.wait()


def on_device(coeffs, centers, kinetic, potential):
    fun_dev, support, points = coeffs.shape
    devices = lax.axis_size(AXES)
    me = lax.axis_index(AXES).astype(jnp.int32).reshape(1)
    box_dev = fun_dev // 2
    volume = 1.0 / (support * points)
    reading = 4 * support
    slots = 2 * REACH + 1
    offsets = list(range(-REACH, REACH + 1))
    last = -REACH
    now = [sign * k for k in range(1, REACH) for sign in (-1, 1)] + [REACH]
    rows, low_cut, high_cut, boxes, blocks = bounds(fun_dev, support)
    assert blocks <= REACH + 1 and support & (support - 1) == 0
    back = tuple(rounded_up(r, 16) for r in rows)
    rows_of = {k: back[k + REACH] for k in offsets}
    flat = coeffs.reshape(fun_dev * support, points)
    halo = REACH + -(-(reading + 8) // fun_dev)
    count = rounded_up((2 * halo + 2) * fun_dev, 128)
    bf16, f32 = jnp.bfloat16, jnp.float32
    smem = pl.BlockSpec(memory_space=pltpu.SMEM)
    vmem = pl.BlockSpec(memory_space=pltpu.VMEM)
    limit = pltpu.CompilerParams(vmem_limit_bytes=26 * 2**20)

    half = rounded_up(box_dev, 16)
    sent_rows = {k: rounded_up(rows[k + REACH] + (2 * box_dev if k < 0 else 0), 16) for k in offsets if k}
    *packed, near, cut, home_row, own_region = pl.pallas_call(
        functools.partial(pack_kernel, (fun_dev, support, devices, halo, rows, back, low_cut, high_cut, now + [last])),
        out_shape=tuple(jax.ShapeDtypeStruct((sent_rows[k], points), bf16) for k in now + [last])
        + (
            jax.ShapeDtypeStruct((count, 128), f32),
            jax.ShapeDtypeStruct((slots + 1,), jnp.int32),
            jax.ShapeDtypeStruct((1, fun_dev * support), f32),
            jax.ShapeDtypeStruct((2 * half, points), bf16),
        ),
        in_specs=[smem, vmem] + [pl.BlockSpec(memory_space=pltpu.HBM)] * 2,
        out_specs=(vmem,) * slots + (smem,) + (vmem,) * 2,
        scratch_shapes=[
            pltpu.VMEM((8, fun_dev * support), f32),
            pltpu.VMEM(flat.shape, bf16),
            pltpu.VMEM(potential.shape, f32),
            pltpu.SemaphoreType.DMA((2,)),
        ],
        compiler_params=pltpu.CompilerParams(vmem_limit_bytes=52 * 2**20),
        name="pack",
    )(me, centers, flat, potential)
    arrived = all_sent(dict(zip(now + [last], packed)), now, last, 1)

    columns, places, active, local = pl.pallas_call(
        functools.partial(table_kernel, (fun_dev, support, halo, boxes)),
        out_shape=(
            jax.ShapeDtypeStruct((slots * SLOT, 128), f32),
            jax.ShapeDtypeStruct((boxes // STEP, 8, STEP * SLOT), f32),
            jax.ShapeDtypeStruct(((slots + 1) * (boxes // STEP),), jnp.int32),
            jax.ShapeDtypeStruct((boxes, SLOT, points), bf16),
        ),
        in_specs=[smem, vmem, vmem],
        out_specs=(vmem, vmem, smem, vmem),
        compiler_params=limit,
        name="tables",
    )(cut, near, flat)

    wide = slots * SLOT
    sources = [arrived[REACH - e] for e in range(slots) if e != REACH]
    read_rows = [rows_of[REACH - e] for e in range(slots)]
    level_sizes = [level_rows(part + 1)[1] - level_rows(part + 1)[0] for part in range(REACH)]
    level_sizes = [level_rows(part + 1)[1] - level_rows(part + 1)[0] for part in range(REACH)]
    exact_rows = [rows[2 * REACH - e] for e in range(slots)]
    band = (fun_dev, 2 * reading)
    exact_rows = [rows[2 * REACH - e] for e in range(slots)]
    pieces, region, *grams = pl.pallas_call(
        functools.partial(unpack_kernel, (fun_dev, box_dev, reading, volume, exact_rows, read_rows, blocks)),
        out_shape=(
            jax.ShapeDtypeStruct((boxes, wide, points), bf16),
            jax.ShapeDtypeStruct((128, points), bf16),
        )
        + tuple(jax.ShapeDtypeStruct(band, f32) for _ in range(slots)),
        in_specs=[smem] * 3 + [vmem] * (3 + len(sources)),
        out_specs=(vmem,) * (2 + slots),
        scratch_shapes=[pltpu.VMEM((wide, band_lanes(fun_dev, reading)), f32)]
        + [pltpu.VMEM((size, size), f32) for size in level_sizes],
        compiler_params=limit,
        name="unpack",
    )(cut, me, active, columns, own_region, local, *sources)

    swaps = [(k, 0) for k in range(1, REACH + 1)] + [(k, 1) for k in range(REACH, 0, -1)]
    summed = [swapped(grams[2 * k - 1 + part], k, part) for k, part in swaps]
    gram_band, mixing_rows = pl.pallas_call(
        functools.partial(sum_kernel, reading),
        out_shape=(jax.ShapeDtypeStruct(band, f32), jax.ShapeDtypeStruct((SLOT, 2 * reading), bf16)),
        in_specs=[vmem] * slots,
        out_specs=(vmem, vmem),
        compiler_params=limit,
        name="sum",
    )(grams[0], *summed)
    mixing_of = {swap: swapped(mixing_rows, *swap) for swap in swaps}

    mixing_of[0, 0] = mixing_rows
    ready, at_boxes = {}, {}
    for group, whole in [([2, -2, REACH, -REACH], [2, -2, REACH, -REACH]), ([0, 1, -1], [1, -1])]:
        group, whole = sorted(REACH - k for k in group), [REACH - k for k in whole]
        most = [max(rows_of[REACH - e], rows_of[e - REACH]) for e in group]
        shapes = [(r, points) for r in most] + [(r, 128) for r in most]
        far = {abs(e - REACH) for e in group}
        group_swaps = [swap for swap in [(0, 0)] + swaps if swap[0] in far]
        sizes = [
            ((in_level(group, v)[1] - in_level(group, v)[0]) * SLOT, level_sizes[v - 1])
            for v in range(1, REACH + 1)
            if in_level(group, v)[1]
        ]
        if ready:
            cut, *held = lax.optimization_barrier((cut, *[ready[k] for k in ready]))
            ready = dict(zip(ready, held))
        mixed = pl.pallas_call(
            functools.partial(mix_kernel, (fun_dev, reading, group, whole, group_swaps)),
            out_shape=tuple(jax.ShapeDtypeStruct(shape, bf16) for shape in shapes),
            in_specs=[smem] * 3 + [vmem] * (4 + len(group)),
            out_specs=(vmem,) * len(shapes),
            scratch_shapes=[pltpu.VMEM((STEP, len(group) * SLOT, points), bf16)]
            + [pltpu.VMEM(size, bf16) for size in sizes]
            + [pltpu.VMEM((r, points), bf16) for r, e in zip(most, group) if e != REACH],
            compiler_params=limit,
            cost_estimate=pl.CostEstimate(
                flops=8 * wide * len(group) * SLOT * boxes * points, bytes_accessed=40 * 2**20, transcendentals=0
            ),
            name="mix",
        )(cut, me, active, places, pieces, region, kinetic, *[mixing_of[swap] for swap in group_swaps])
        for at, e in enumerate(group):
            key = (abs(e - REACH), int(e > REACH))
            ready[key], at_boxes[key] = mixed[at], mixed[len(group) + at]
            if e not in whole:
                near_by = jnp.dot(at_boxes[key], region, preferred_element_type=f32)
                applied = jnp.dot(mixed[at], kinetic, preferred_element_type=f32)
                ready[key] = (applied + near_by * mixed[at].astype(f32)).astype(bf16)
    far = (REACH, 1)
    returned = {swap: swapped(ready[swap], *swap) for swap in swaps if swap != far}
    value, returned[2, 0] = lax.optimization_barrier((ready[far], returned[2, 0]))
    returned[far] = swapped(value, *far)
    returned[0, 0] = ready[0, 0]

    bases = {k: sum(back[: k + REACH]) for k in offsets}
    early, late = [(0, 0), (2, 0), (2, 1), (REACH, 0)], [(1, 0), (1, 1), far]
    early_bases = [(bases[k], bases[-k], k, part) for k, part in early]
    late_bases = [(bases[k], bases[-k], k, part) for k, part in late]
    begun = pl.pallas_call(
        functools.partial(early_kernel, early_bases),
        out_shape=jax.ShapeDtypeStruct(flat.shape, bf16),
        in_specs=[smem] + [vmem] * (1 + len(early)),
        out_specs=vmem,
        compiler_params=limit,
        name="early",
    )(me, home_row, *[returned[swap] for swap in early])
    filtered = pl.pallas_call(
        functools.partial(home_kernel, late_bases),
        out_shape=jax.ShapeDtypeStruct(flat.shape, bf16),
        in_specs=[smem] + [vmem] * (2 + len(late)),
        out_specs=pl.BlockSpec(memory_space=pl.ANY),
        scratch_shapes=[
            pltpu.VMEM((flat.shape[0] // 256, 256, points), bf16),
            pltpu.SemaphoreType.DMA((flat.shape[0] // 256,)),
        ],
        compiler_params=limit,
        name="home",
    )(me, home_row, begun, *[returned[swap] for swap in late])
    return (filtered.reshape(coeffs.shape), gram_band)


def solution(mesh):
    placed = (P(AXES, None, None), P(), P(), P(AXES, None))
    return jax.shard_map(
        on_device,
        mesh=mesh,
        in_specs=placed,
        out_specs=(P(AXES, None, None), P(AXES, None)),
        check_vma=False,
    )
```
